32 devices in a mesh: fsdp: 4 (over z), ctx: 2 (over core), tp: 4 (over y, x).
Axes of the slice: x: 2, y: 2, z: 4, core: 2. Of those that a mesh axis runs over, the one named last changes fastest.
Arguments:
- latents: bfloat16 [32, 4, 32, 32], P(('fsdp', 'ctx')), may hold values from -5 to 5
- noise_sample: bfloat16 [32, 4, 32, 32], P(('fsdp', 'ctx')), may hold values from -5 to 5
- timesteps: int32 [32], P(('fsdp', 'ctx')), may hold values from 0 to 999
- class_labels: int32 [32], P(('fsdp', 'ctx')), may hold values from 0 to 999
- w_block: float32 [1024, 13, 1024], P(('fsdp', 'ctx'), None, 'tp'), may hold values from -0.1875 to 0.1875
- w_output: float32 [5, 1024, 1024], P(None, 'tp', ('fsdp', 'ctx')), may hold values from -0.375 to 0.375
- w_top: float32 [1024, 3072], P(('fsdp', 'ctx'), 'tp'), may hold values from -0.1875 to 0.1875
- w_head: float32 [1024, 16], P(('fsdp', 'ctx')), may hold values from -0.1875 to 0.1875
- w_embed: float32 [1272, 1024], P('tp', ('fsdp', 'ctx')), may hold values from -1 to 1
- biases: float32 [19, 1024], replicated, may hold values from -0.6 to 0.6
- m_block: float32 [1024, 13, 1024], P(('fsdp', 'ctx'), None, 'tp'), may hold values from -0.000113846974 to 0.000113846974
- m_output: float32 [5, 1024, 1024], P(None, 'tp', ('fsdp', 'ctx')), may hold values from -0.000113846974 to 0.000113846974
- m_top: float32 [1024, 3072], P(('fsdp', 'ctx'), 'tp'), may hold values from -0.000113846974 to 0.000113846974
- m_head: float32 [1024, 16], P(('fsdp', 'ctx')), may hold values from -0.004296875 to 0.004296875
- m_embed: float32 [1272, 1024], P('tp', ('fsdp', 'ctx')), may hold values from -0.000113846974 to 0.000113846974
- m_biases: float32 [19, 1024], replicated, may hold values from -0.0004553879 to 0.0004553879
- v_block: float32 [1024, 13, 1024], P(('fsdp', 'ctx'), None, 'tp'), may hold values from 2.1423361e-11 to 1.7138689e-10
- v_output: float32 [5, 1024, 1024], P(None, 'tp', ('fsdp', 'ctx')), may hold values from 2.1423361e-11 to 1.7138689e-10
- v_top: float32 [1024, 3072], P(('fsdp', 'ctx'), 'tp'), may hold values from 2.1423361e-11 to 1.7138689e-10
- v_head: float32 [1024, 16], P(('fsdp', 'ctx')), may hold values from 3.051758e-08 to 2.4414064e-07
- v_embed: float32 [1272, 1024], P('tp', ('fsdp', 'ctx')), may hold values from 2.1423361e-11 to 1.7138689e-10
- v_biases: float32 [19, 1024], replicated, may hold values from 3.4277378e-10 to 2.7421903e-09
Outputs:
- loss: float32 [], replicated
- grad_norm: float32 [], replicated
- new_block: float32 [1024, 13, 1024], P(('fsdp', 'ctx'), None, 'tp')
- new_output: float32 [5, 1024, 1024], P(None, 'tp', ('fsdp', 'ctx'))
- new_top: float32 [1024, 3072], P(('fsdp', 'ctx'), 'tp')
- new_head: float32 [1024, 16], P(('fsdp', 'ctx'))
- new_embed: float32 [1272, 1024], P('tp', ('fsdp', 'ctx'))
- new_biases: float32 [19, 1024], replicated
- first_block: float32 [1024, 13, 1024], P(('fsdp', 'ctx'), None, 'tp')
- first_output: float32 [5, 1024, 1024], P(None, 'tp', ('fsdp', 'ctx'))
- first_top: float32 [1024, 3072], P(('fsdp', 'ctx'), 'tp')
- first_head: float32 [1024, 16], P(('fsdp', 'ctx'))
- first_embed: float32 [1272, 1024], P('tp', ('fsdp', 'ctx'))
- first_biases: float32 [19, 1024], replicated
- second_block: float32 [1024, 13, 1024], P(('fsdp', 'ctx'), None, 'tp')
- second_output: float32 [5, 1024, 1024], P(None, 'tp', ('fsdp', 'ctx'))
- second_top: float32 [1024, 3072], P(('fsdp', 'ctx'), 'tp')
- second_head: float32 [1024, 16], P(('fsdp', 'ctx'))
- second_embed: float32 [1272, 1024], P('tp', ('fsdp', 'ctx'))
- second_biases: float32 [19, 1024], replicated
- clipped_bias_grad: float32 [19, 1024], replicated
The draws below stay inside these ranges and needn't reach their ends.
All inputs are finite; a program needn't handle non-finite values.
Results may differ from the reference program's by a relative error of at most 0.012.
Values may be sent and summed in bfloat16 or wider, within the bound.
No kernel may reach another device: no remote copies, remote signals or barrier semaphores. Data moves between devices by JAX's collectives and lax.ppermute only.
A program may use at most 192 MiB of HBM per device.

```python
import math
import jax
import jax.numpy as jnp
from jax import lax

D = 1024
HEADS = 16
HEAD_DIM = 64
FF = 4096
CLASSES = 1000
FREQ = 256
CH_IN = 4
LAT = 32
TIMESTEPS = 1000
ADAM_STEP = 10
BIAS_ROWS = 19
IMAGES = 32
GRID = 16
TOK_IMG = 256
CH = 16
EMB_ROWS = 1272
PARAMS = 23339008


def draw_w_output(key, part):
    key = jax.random.fold_in(key, 11)
    base = jnp.clip(jax.random.normal(key, (5, D, D), jnp.float32), -4.0, 4.0)
    block_scale = jnp.where(jnp.arange(5) == 0, 3.0 * D ** (-0.5), FF ** (-0.5)).astype(jnp.float32)
    return base * block_scale[:, None, None]


def draw_w_embed(key, part):
    key = jax.random.fold_in(key, 23)
    base = jnp.clip(jax.random.normal(key, (EMB_ROWS, D), jnp.float32), -4.0, 4.0)
    row_ids = jnp.arange(EMB_ROWS)
    row_scale = jnp.where(row_ids < FREQ, 2.0 * FREQ ** (-0.5), jnp.where(row_ids < FREQ + CLASSES, 0.25, CH ** (-0.5)))
    return base * row_scale.astype(jnp.float32)[:, None]


def set_ends(values, key, low, top_value):
    extent = values.shape
    spot = [jax.random.randint(jax.random.fold_in(key, axis), (), 0, extent[axis]) for axis in range(len(extent))]
    values = values.at[tuple(spot)].set(low)
    longest = extent.index(max(extent))
    spot[longest] = (spot[longest] + 1) % extent[longest]
    return values.at[tuple(spot)].set(top_value)


def shard_levels(key, shape, shards, low, largest):
    def one(position, blocks):
        draws = jax.random.uniform(jax.random.fold_in(jax.random.fold_in(key, 6), position), (blocks,), jnp.float32, low / len(shards), largest / len(shards))
        return jnp.repeat(jnp.exp(draws), shape[position] // blocks).reshape((-1,) + (1,) * (len(shape) - position - 1))

    factor_of = one(*shards[0])
    for cut in shards[1:]:
        factor_of = factor_of * one(*cut)
    return factor_of


def bell_draw(own_key, dims, scale, reach, pieces=(), kind=jnp.bfloat16):
    drawn = scale * jax.random.normal(own_key, dims, jnp.float32)
    if pieces:
        drawn = drawn * shard_levels(own_key, dims, pieces, -0.22, 0.18)
    return jnp.clip(drawn, -reach, reach).astype(kind)


def setup_inputs(seed: int = 0) -> dict:
    arg_keys = jax.random.split(jax.random.key(seed), 23)
    return {
        "latents": bell_draw(arg_keys[0], (IMAGES, CH_IN, LAT, LAT), 1.0, 5.0, ((0, 8),)),
        "noise_sample": bell_draw(arg_keys[1], (IMAGES, CH_IN, LAT, LAT), 1.0, 5.0, ((0, 8),)),
        "timesteps": set_ends(jax.random.randint(arg_keys[2], (IMAGES,), 0, TIMESTEPS), jax.random.fold_in(arg_keys[2], 1), 0, TIMESTEPS - 1).astype(jnp.int32),
        "class_labels": set_ends(jax.random.randint(arg_keys[3], (IMAGES,), 0, CLASSES), jax.random.fold_in(arg_keys[3], 1), 0, CLASSES - 1).astype(jnp.int32),
        "w_block": bell_draw(arg_keys[4], (D, 13, D), D ** -0.5, 0.1875, ((0, 8), (2, 4)), jnp.float32),
        "w_output": draw_w_output(jax.random.fold_in(arg_keys[22], 71), 0),
        "w_top": bell_draw(arg_keys[6], (D, 3 * D), D ** -0.5, 0.1875, ((0, 8), (1, 4)), jnp.float32),
        "w_head": bell_draw(arg_keys[7], (D, CH), D ** -0.5, 0.1875, ((0, 8),), jnp.float32),
        "w_embed": draw_w_embed(jax.random.fold_in(arg_keys[22], 71), 0),
        "biases": bell_draw(arg_keys[9], (BIAS_ROWS, D), 0.15, 0.6, (), jnp.float32),
        "m_block": bell_draw(arg_keys[10], (D, 13, D), (0.11 * PARAMS ** -0.5), 0.000113846974, ((0, 8), (2, 4)), jnp.float32),
        "m_output": bell_draw(arg_keys[11], (5, D, D), (0.11 * PARAMS ** -0.5), 0.000113846974, ((1, 4), (2, 8)), jnp.float32),
        "m_top": bell_draw(arg_keys[12], (D, 3 * D), (0.11 * PARAMS ** -0.5), 0.000113846974, ((0, 8), (1, 4)), jnp.float32),
        "m_head": bell_draw(arg_keys[13], (D, CH), (0.11 * (D * CH) ** -0.5), 0.004296875, ((0, 8),), jnp.float32),
        "m_embed": bell_draw(arg_keys[14], (EMB_ROWS, D), (0.11 * PARAMS ** -0.5), 0.000113846974, ((0, 4), (1, 8)), jnp.float32),
        "m_biases": bell_draw(arg_keys[15], (BIAS_ROWS, D), (0.44 * PARAMS ** -0.5), 0.0004553879, (), jnp.float32),
        "v_block": jnp.clip(jnp.exp(math.log(1.71386890790437e-10) - 2.0794415 * jax.random.uniform(arg_keys[16], (D, 13, D), jnp.float32) ** shard_levels(arg_keys[16], (D, 13, D), ((0, 8), (2, 4)), -0.2, 0.2)), 2.1423361348804626e-11, 1.71386890790437e-10),
        "v_output": jnp.clip(jnp.exp(math.log(1.71386890790437e-10) - 2.0794415 * jax.random.uniform(arg_keys[17], (5, D, D), jnp.float32) ** shard_levels(arg_keys[17], (5, D, D), ((1, 4), (2, 8)), -0.2, 0.2)), 2.1423361348804626e-11, 1.71386890790437e-10),
        "v_top": jnp.clip(jnp.exp(math.log(1.71386890790437e-10) - 2.0794415 * jax.random.uniform(arg_keys[18], (D, 3 * D), jnp.float32) ** shard_levels(arg_keys[18], (D, 3 * D), ((0, 8), (1, 4)), -0.2, 0.2)), 2.1423361348804626e-11, 1.71386890790437e-10),
        "v_head": jnp.clip(jnp.exp(math.log(2.4414063659605745e-07) - 2.0794415 * jax.random.uniform(arg_keys[19], (D, CH), jnp.float32) ** shard_levels(arg_keys[19], (D, CH), ((0, 8),), -0.2, 0.2)), 3.051757957450718e-08, 2.4414063659605745e-07),
        "v_embed": jnp.clip(jnp.exp(math.log(1.71386890790437e-10) - 2.0794415 * jax.random.uniform(arg_keys[20], (EMB_ROWS, D), jnp.float32) ** shard_levels(arg_keys[20], (EMB_ROWS, D), ((0, 4), (1, 8)), -0.2, 0.2)), 2.1423361348804626e-11, 1.71386890790437e-10),
        "v_biases": jnp.clip(jnp.exp(jax.random.uniform(arg_keys[21], (BIAS_ROWS, D), jnp.float32, math.log(3.42773781580874e-10), math.log(2.742190252646992e-09))), 3.42773781580874e-10, 2.742190252646992e-09),
    }


@jax.custom_vjp
def low(v):
    return lax.optimization_barrier(v.astype(jnp.bfloat16)).astype(jnp.float32)

@jax.custom_vjp
def low_back(v):
    return v

def low_keep(v):
    return (low(v), None)

def low_pass(kept, grad):
    return (grad,)

def back_keep(v):
    return (v, None)

def back_low(kept, grad):
    return (low(grad),)
low.defvjp(low_keep, low_pass)
low_back.defvjp(back_keep, back_low)
PRECISE = lax.Precision.HIGHEST

def both_ways(values):
    return low(low_back(values))

def dense(left, right):
    return jnp.einsum('...d,de->...e', left, right, precision=PRECISE)

def layer_norm(values):
    center = values - lax.optimization_barrier(jnp.mean(values, axis=-1, keepdims=True))
    spread = lax.optimization_barrier(jnp.mean(center * center, axis=-1, keepdims=True))
    return center * lax.rsqrt(spread + 1e-06)

def modulate(values, shift, scale):
    return layer_norm(values) * (1.0 + scale[:, None, :]) + shift[:, None, :]

def gelu_tanh(values):
    return jax.nn.gelu(values, approximate=True)

def time_freq(step_ids, width):
    half_width = width // 2
    rates = jnp.exp(-math.log(10000.0) * jnp.arange(half_width, dtype=jnp.float32) / half_width)
    angles = step_ids.astype(jnp.float32)[:, None] * rates[None, :]
    return jnp.concatenate([jnp.cos(angles), jnp.sin(angles)], axis=-1)

def position_table(token_ids, grid_side, width):
    quarter = width // 4
    rates = jnp.exp(-math.log(10000.0) * jnp.arange(quarter, dtype=jnp.float32) / quarter)
    row_angle = (token_ids // grid_side).astype(jnp.float32)[:, None] * rates[None, :]
    col_angle = (token_ids % grid_side).astype(jnp.float32)[:, None] * rates[None, :]
    return jnp.concatenate([jnp.sin(row_angle), jnp.cos(row_angle), jnp.sin(col_angle), jnp.cos(col_angle)], axis=-1)

def plan(step_ids):
    fraction = (step_ids.astype(jnp.float32) / TIMESTEPS + 0.008) / 1.008
    kept_share = jnp.cos(fraction * (math.pi / 2.0)) ** 2
    return (jnp.sqrt(kept_share), jnp.sqrt(1.0 - kept_share))

def patchify(field):
    img_count, chan_count, row_count, col_count = field.shape
    shaped = field.reshape(img_count, chan_count, row_count // 2, 2, col_count // 2, 2)
    shaped = shaped.transpose(0, 2, 4, 1, 3, 5)
    return shaped.reshape(img_count, row_count // 2 * (col_count // 2), chan_count * 4)

def adam_update(weight, gradient, first_mom, second_mom, clip_factor):
    clipped = gradient * clip_factor
    first_new = 0.9 * first_mom + 0.1 * clipped
    second_new = 0.999 * second_mom + 0.001 * clipped * clipped
    corr_first = 1.0 - 0.9 ** ADAM_STEP
    corr_second = 1.0 - 0.999 ** ADAM_STEP
    direction = first_new / corr_first / (jnp.sqrt(second_new / corr_second) + 1e-08)
    return (weight - 0.04 * (direction + 0.01 * weight), first_new, second_new)

def forward_group(params, group):
    w_block, w_output, w_top, w_head, w_embed, biases = params
    latent_part, noise_part, time_part, label_part = group
    width = w_block.shape[0]
    img_count = latent_part.shape[0]
    keep_rate, drop_rate = plan(time_part)
    noisy = keep_rate[:, None, None, None] * latent_part + drop_rate[:, None, None, None] * noise_part
    patches = low(patchify(noisy))
    target = patchify(noise_part)
    freq_low = low(time_freq(time_part, FREQ))
    w_t1 = w_embed[:FREQ]
    table = w_embed[FREQ:FREQ + CLASSES]
    w_patch = w_embed[FREQ + CLASSES:]
    t_hidden = low(jax.nn.silu(dense(freq_low, w_t1) + biases[1]))
    cond = dense(t_hidden, w_top[:, :width]) + biases[2] + table[label_part]
    cond_low = low(jax.nn.silu(cond))
    modulation = (dense(cond_low, w_block[:, 7:13].reshape(width, 6 * width)) + biases[3:9].reshape(6 * width)).reshape(img_count, 6, width)
    final_mod = dense(cond_low, w_top[:, width:3 * width]) + biases[17:19].reshape(2 * width)
    token_ids = jnp.arange(TOK_IMG, dtype=jnp.int32)
    resid_in = low_back(dense(patches, w_patch) + biases[0] + position_table(token_ids, GRID, width)[None])
    attn_in = low(modulate(resid_in, modulation[:, 0], modulation[:, 1]))
    head_shape = (img_count, TOK_IMG, HEADS, HEAD_DIM)
    queries = both_ways(dense(attn_in, w_block[:, 0]) + biases[9]).reshape(head_shape)
    keys_all = both_ways(dense(attn_in, w_block[:, 1])).reshape(head_shape)
    values_all = both_ways(dense(attn_in, w_block[:, 2]) + biases[10]).reshape(head_shape)
    scores = low_back(jnp.einsum('bqhd,bkhd->bhqk', queries, keys_all, precision=PRECISE) * 0.125)
    probs = low(jax.nn.softmax(scores, axis=-1))
    attended = both_ways(jnp.einsum('bhqk,bkhd->bqhd', probs, values_all, precision=PRECISE).reshape(img_count, TOK_IMG, width))
    attn_out = low_back(dense(attended, w_output[0]) + biases[11])
    resid_mid = resid_in + modulation[:, 2][:, None, :] * attn_out
    mlp_in = low(modulate(resid_mid, modulation[:, 3], modulation[:, 4]))
    up_pre = low_back(dense(mlp_in, w_block[:, 3:7].reshape(width, 4 * width)) + biases[12:16].reshape(4 * width))
    up_act = low(gelu_tanh(up_pre))
    mlp_out = low_back(dense(up_act, w_output[1:5].reshape(4 * width, width)) + biases[16])
    resid_out = resid_mid + modulation[:, 5][:, None, :] * mlp_out
    head_in = low(modulate(resid_out, final_mod[:, :width], final_mod[:, width:]))
    predicted = low_back(dense(head_in, w_head))
    error = predicted - target
    return jnp.sum(error * error)

def reference(latents, noise_sample, timesteps, class_labels, w_block, w_output, w_top, w_head, w_embed, biases, m_block, m_output, m_top, m_head, m_embed, m_biases, v_block, v_output, v_top, v_head, v_embed, v_biases):
    group_size = 16
    group_count = IMAGES // group_size
    data = (latents.astype(jnp.float32).reshape(group_count, group_size, CH_IN, LAT, LAT), noise_sample.astype(jnp.float32).reshape(group_count, group_size, CH_IN, LAT, LAT), timesteps.reshape(group_count, group_size), class_labels.reshape(group_count, group_size))
    weights = (w_block, w_output, w_top, w_head, w_embed, biases)

    def total_loss(params):
        rounded = (low(params[0]), low(params[1]), low(params[2]), low(params[3]), low(params[4]), params[5])

        def one_group(carry, group):
            return (carry + jax.checkpoint(forward_group)(rounded, group), None)
        total, scan_rest = lax.scan(one_group, jnp.zeros((), jnp.float32), data)
        return total / IMAGES
    loss, pullback = jax.vjp(total_loss, weights)
    grads = pullback(jnp.ones((), jnp.float32))[0]
    squares = sum((jnp.sum(array_item * array_item) for array_item in grads))
    grad_norm = jnp.sqrt(squares)
    clip_factor = jnp.minimum(1.0, 1.0 / (grad_norm + 1e-06))
    firsts = (m_block, m_output, m_top, m_head, m_embed, m_biases)
    seconds = (v_block, v_output, v_top, v_head, v_embed, v_biases)
    results = [adam_update(weights[index_at], grads[index_at], firsts[index_at], seconds[index_at], clip_factor) for index_at in range(6)]
    return (loss, grad_norm, results[0][0], results[1][0], results[2][0], results[3][0], results[4][0], results[5][0], results[0][1], results[1][1], results[2][1], results[3][1], results[4][1], results[5][1], results[0][2], results[1][2], results[2][2], results[3][2], results[4][2], results[5][2], grads[5] * clip_factor)
```

```python
import functools
import math

import jax
import jax.numpy as jnp
from jax import lax
from jax.experimental import pallas as pl
from jax.experimental.pallas import tpu as pltpu
from jax.sharding import PartitionSpec as P

HEAD_DIM = 64
CLASSES = 1000
FREQ = 256
TIMESTEPS = 1000
ADAM_STEP = 10
PATCH_ROWS = 16

PRECISE = lax.Precision.HIGHEST
BF = jnp.bfloat16
F32 = jnp.float32


def exact_dot(left, right):
    return jnp.dot(left, right, precision=PRECISE)


def mm(left, right):
    return jnp.dot(left, right, preferred_element_type=F32)


def mm_nt(left, right):
    return lax.dot_general(left, right, (((1,), (1,)), ((), ())), preferred_element_type=F32)


def mm_tn(left, right):
    return lax.dot_general(left, right, (((0,), (0,)), ((), ())), preferred_element_type=F32)


def layer_norm(values):
    center = values - jnp.mean(values, axis=-1, keepdims=True)
    spread = jnp.mean(center * center, axis=-1, keepdims=True)
    return center * lax.rsqrt(spread + 1e-06)


def modulate(values, shift, scale):
    return layer_norm(values) * (1.0 + scale[:, None, :]) + shift[:, None, :]


def gelu_tanh(values):
    return jax.nn.gelu(values, approximate=True)


def plan(step_ids):
    fraction = (step_ids.astype(F32) / TIMESTEPS + 0.008) / 1.008
    kept_share = jnp.cos(fraction * (math.pi / 2.0)) ** 2
    return (jnp.sqrt(kept_share), jnp.sqrt(1.0 - kept_share))


def patchify(field):
    img_count, chan_count, row_count, col_count = field.shape
    shaped = field.reshape(img_count, chan_count, row_count // 2, 2, col_count // 2, 2)
    shaped = shaped.transpose(0, 2, 4, 1, 3, 5)
    return shaped.reshape(img_count, row_count // 2 * (col_count // 2), chan_count * 4)


def adam_update(weight, gradient, first_mom, second_mom, clip_factor):
    clipped = gradient * clip_factor
    first_new = 0.9 * first_mom + 0.1 * clipped
    second_new = 0.999 * second_mom + 0.001 * clipped * clipped
    corr_first = 1.0 - 0.9**ADAM_STEP
    corr_second = 1.0 - 0.999**ADAM_STEP
    direction = first_new / corr_first / (jnp.sqrt(second_new / corr_second) + 1e-08)
    return (weight - 0.04 * (direction + 0.01 * weight), first_new, second_new)


def swap(value, axis, mask):
    count = lax.axis_size(axis)
    return lax.ppermute(value, axis, [(i, i ^ mask) for i in range(count)])


def pull(value, k):
    count = lax.axis_size("fsdp")
    return lax.ppermute(value, "fsdp", [((i + k) % count, i) for i in range(count)])


def push(value, k):
    count = lax.axis_size("fsdp")
    return lax.ppermute(value, "fsdp", [(i, (i + k) % count) for i in range(count)])


def is_ring():
    return lax.axis_size("fsdp") == 4


def pick(pair, bit, axis=0):
    low = lax.index_in_dim(pair, 0, axis, keepdims=False)
    high = lax.index_in_dim(pair, 1, axis, keepdims=False)
    return jnp.where(bit == 1, high, low)


def ordered(own, other, bit, axis=0):
    return jnp.stack([jnp.where(bit == 0, own, other), jnp.where(bit == 0, other, own)], axis)


def bits(count):
    return [1 << b for b in range(count.bit_length() - 1)]


def by_xor(stack, rank):
    for mask in (1, 2):
        other = jnp.stack([stack[i ^ mask] for i in range(4)])
        stack = jnp.where(rank & mask == mask, other, stack)
    return stack


def sum_over(value, axes, pace=lambda v: v):
    for axis in axes:
        count = lax.axis_size(axis)
        if count > 4:
            value = lax.psum(value, axis)
            continue
        for mask in bits(count):
            value = value + swap(pace(value), axis, mask)
    return value


def scatter_fc(blocks, pace=lambda v: v):
    if not is_ring():
        return lax.psum_scatter(blocks, ("fsdp", "ctx"), scatter_dimension=0, tiled=False)
    f, c = lax.axis_index("fsdp"), lax.axis_index("ctx")
    shape = blocks.shape[1:]
    held = blocks.reshape((4, 2) + shape)
    held = pick(held, c, 1) + swap(pace(pick(held, 1 - c, 1)), "ctx", 1)
    held = held.reshape((2, 2) + shape)
    high, low = f >> 1, f & 1
    held = pick(held, high) + swap(pace(pick(held, 1 - high)), "fsdp", 2)
    return pick(held, low) + swap(pace(pick(held, 1 - low)), "fsdp", 1)


def gather_fc(value, pace=lambda v: v):
    if not is_ring():
        return lax.all_gather(value, ("fsdp", "ctx"), axis=0, tiled=False)
    f, c = lax.axis_index("fsdp"), lax.axis_index("ctx")
    shape = value.shape
    held = ordered(value, swap(pace(value), "fsdp", 1), f & 1)
    held = ordered(held, swap(pace(held), "fsdp", 2), f >> 1)
    held = held.reshape((4,) + shape)
    held = ordered(held, swap(pace(held), "ctx", 1), c, 1)
    return held.reshape((8,) + shape)


def exchange_tp(blocks):
    t = lax.axis_index("tp")
    mine = by_xor(blocks, t)
    got = jnp.stack([mine[0]] + [swap(mine[k], "tp", k) for k in (1, 2, 3)])
    return by_xor(got, t)


class Lane:
    def __init__(self, depth):
        self.depth = depth
        self.ended = []

    def __call__(self, value, move):
        if len(self.ended) >= self.depth:
            value, _ = lax.optimization_barrier((value, self.ended[-self.depth]))
        moved = move(value)
        self.ended.append(moved)
        return moved


class Pace:
    def __init__(self, lanes):
        self.waiting = list(lanes.ended)

    def __call__(self, value):
        if self.waiting:
            value, _ = lax.optimization_barrier((value, self.waiting.pop(0)))
        return value


class Lanes:
    def __init__(self, x, y, z):
        self.ended = []
        self.lane_x, self.lane_y, self.lane_z = Lane(x), Lane(y), Lane(z)

    def note(self, moved):
        self.ended.append(moved)
        return moved

    def x(self, value):
        return self.note(self.lane_x(value, lambda v: swap(v, "tp", 1)))

    def y(self, value):
        return self.note(self.lane_y(value, lambda v: swap(v, "tp", 2)))

    def pull(self, value, k):
        return self.note(self.lane_z(value, lambda v: pull(v, k)))

    def push(self, value, k):
        return self.note(self.lane_z(value, lambda v: push(v, k)))


def gather_grid(lanes, shard):
    if not is_ring():
        parts = [lax.all_gather(shard, "fsdp", axis=0, tiled=True)]
    else:
        one = lanes.pull(shard, 1)
        x_0, y_0 = lanes.x(shard), lanes.y(shard)
        three = lanes.pull(shard, 3)
        x_1, y_1 = lanes.x(one), lanes.y(one)
        two = lanes.pull(one, 1)
        d_0 = lanes.x(y_0)
        d_1 = lanes.y(x_1)
        x_3, y_3 = lanes.x(three), lanes.y(three)
        x_2, y_2 = lanes.x(two), lanes.y(two)
        d_3 = lanes.x(y_3)
        d_2 = lanes.y(x_2)
        return [
            [shard, x_0, y_0, d_0],
            [one, x_1, y_1, d_1],
            [two, x_2, y_2, d_2],
            [three, x_3, y_3, d_3],
        ]
    near = swap(parts[0], "tp", 1)
    return [[parts[0], near, swap(parts[0], "tp", 2), swap(near, "tp", 2)]]


def add(left, right):
    return left.astype(F32) + right.astype(F32)


def add_low(left, right):
    return add(left, right).astype(BF)


def reduce_grid(lanes, main):
    if not is_ring():
        parts = main[0]
        along_x = swap(parts[1], "tp", 1)
        along_y = swap(add_low(parts[2], swap(parts[3], "tp", 1)), "tp", 2)
        both = add_low(add(parts[0], along_x), along_y)
        return lax.psum_scatter(both, "fsdp", scatter_dimension=0, tiled=True).astype(F32)
    far_2, far_1 = lanes.y(main[2][3]), None
    far_3 = lanes.x(main[3][3])
    y_2 = lanes.y(main[2][2])
    x_2 = lanes.x(add_low(main[2][1], far_2))
    far_1 = lanes.y(main[1][3])
    x_3 = lanes.x(main[3][1])
    y_3 = lanes.y(add_low(main[3][2], far_3))
    sum_2 = lanes.push(add_low(add(main[2][0], x_2), y_2), 1)
    y_1 = lanes.y(main[1][2])
    x_1 = lanes.x(add_low(main[1][1], far_1))
    far_0 = lanes.x(main[0][3])
    sum_3 = lanes.push(add_low(add(main[3][0], x_3), y_3), 3)
    x_0 = lanes.x(main[0][1])
    sum_1 = add(add(add(main[1][0], x_1), y_1), sum_2).astype(BF)
    sum_1 = lanes.push(sum_1, 1)
    y_0 = lanes.y(add_low(main[0][2], far_0))
    return add(add(add(main[0][0], x_0), y_0), sum_3) + sum_1.astype(F32)


def rows_of(table, start, count):
    pad = jnp.zeros((count,) + table.shape[1:], table.dtype)
    padded = jnp.concatenate([pad, table, pad], axis=0)
    return lax.dynamic_slice_in_dim(padded, jnp.clip(start + count, 0, table.shape[0] + count), count, 0)


def call(body, outs, args, flops):
    flat, tree = jax.tree.flatten(args)
    held = sum(a.size * a.dtype.itemsize for a in list(flat) + list(outs))

    def kernel(*refs):
        body(*jax.tree.unflatten(tree, refs[: len(flat)]), *refs[len(flat) :])

    vmem = pl.BlockSpec(memory_space=pltpu.VMEM)
    return pl.pallas_call(
        kernel,
        out_shape=outs,
        in_specs=[vmem] * len(flat),
        out_specs=[vmem] * len(outs),
        compiler_params=pltpu.CompilerParams(vmem_limit_bytes=held + 16 * 1024 * 1024),
        cost_estimate=pl.CostEstimate(flops=flops, bytes_accessed=held, transcendentals=0),
    )(*flat)


def shape(rows, cols, dtype):
    return jax.ShapeDtypeStruct((rows, cols), dtype)


def lanes_of(ref, start, count):
    return ref[:, start : start + count]


def down_rows(parts, k_t, start, stop):
    return jnp.concatenate([row[k_t][:, start:stop] for row in parts], axis=0)


def along_cols(row, start, stop):
    return jnp.concatenate([p[:, start:stop] for p in row], axis=1)


def head_masks(half):
    at = lax.broadcasted_iota(jnp.int32, (1, half), 1) // HEAD_DIM
    return [at == h for h in range(half // HEAD_DIM)]


def softmax_rows(scores):
    top = jnp.max(scores, axis=-1, keepdims=True)
    grown = jnp.exp(scores - top)
    return grown / jnp.sum(grown, axis=-1, keepdims=True)


def merged(masks, values):
    total = values[-1]
    for mask, value in zip(masks[:-1], values[:-1]):
        total = jnp.where(mask, value, total)
    return total


def col_block(ref, starts, k_f, size):
    if starts is None:
        return (slice(None), slice(0, size))
    return (slice(None), pl.ds(pl.multiple_of(starts[k_f], size), size))


def kernel_starts(parts):
    if len(parts) == 1:
        return None
    size = parts[0][0].shape[0]
    f = lax.axis_index("fsdp")
    return [((f + k) & 3) * size for k in range(4)]


def qkv_kernel(tok_count, half, own_ref, other_ref, parts, bias_ref, qkv_ref, attended_ref):
    rows = own_ref.shape[0]
    size = parts[0][0].shape[0]
    masks = head_masks(half)
    starts = kernel_starts(parts)
    for i, ref in enumerate((own_ref, other_ref)):
        turned = jnp.concatenate(
            [ref[col_block(ref, starts, k_f, size)] for k_f in range(len(parts))], axis=1
        )
        for k_t in range(4):
            cols = slice(k_t * 3 * half, (k_t + 1) * 3 * half)
            weight = down_rows(parts, k_t, 0, 3 * half)
            qkv_ref[i * rows : (i + 1) * rows, cols] = (
                mm(turned, weight) + bias_ref[:, cols]
            ).astype(BF)
    for k_t in range(4):
        at = k_t * 3 * half
        for row in range(0, 2 * rows, tok_count):
            here = slice(row, row + tok_count)
            query = qkv_ref[here, at : at + half]
            key = qkv_ref[here, at + half : at + 2 * half]
            value = qkv_ref[here, at + 2 * half : at + 3 * half]
            got = []
            for mask in masks:
                masked = jnp.where(mask, query, jnp.zeros_like(query))
                probs = softmax_rows(mm_nt(masked, key) * 0.125).astype(BF)
                got.append(mm(probs, value))
            attended_ref[here, k_t * half : (k_t + 1) * half] = merged(masks, got).astype(BF)


def attention_back_kernel(tok_count, half, own_ref, other_ref, parts, qkv_ref, out_ref, sum_ref):
    rows = own_ref.shape[0]
    size = parts[0][0].shape[0]
    masks = head_masks(half)
    starts = kernel_starts(parts)
    turned = [
        jnp.concatenate(
            [ref[col_block(ref, starts, k_f, size)] for k_f in range(len(parts))], axis=1
        )
        for ref in (own_ref, other_ref)
    ]
    for k_t in range(4):
        at = k_t * 3 * half
        weight = down_rows(parts, k_t, 3 * half, 4 * half)
        for i in range(2):
            grad_half = mm(turned[i], weight).astype(BF)
            for row in range(0, rows, tok_count):
                here = slice(i * rows + row, i * rows + row + tok_count)
                grad = grad_half[row : row + tok_count]
                query = qkv_ref[here, at : at + half]
                key = qkv_ref[here, at + half : at + 2 * half]
                value = qkv_ref[here, at + 2 * half : at + 3 * half]
                grad_q, grad_k, grad_v = [], [], []
                for mask in masks:
                    zero = jnp.zeros_like(query)
                    probs = softmax_rows(mm_nt(jnp.where(mask, query, zero), key) * 0.125)
                    grad_p = mm_nt(jnp.where(mask, grad, zero), value)
                    grad_s = (
                        probs * (grad_p - jnp.sum(grad_p * probs, axis=-1, keepdims=True))
                    ).astype(BF)
                    grad_q.append(mm(grad_s, key))
                    grad_k.append(mm_tn(grad_s, query))
                    grad_v.append(mm_tn(probs.astype(BF), grad))
                out_ref[here, at : at + half] = (merged(masks, grad_q) * 0.125).astype(BF)
                out_ref[here, at + half : at + 2 * half] = (merged(masks, grad_k) * 0.125).astype(BF)
                out_ref[here, at + 2 * half : at + 3 * half] = merged(masks, grad_v).astype(BF)
        cols = slice(at, at + 3 * half)
        sum_ref[:, cols] = jnp.sum(out_ref[:, cols].astype(F32), axis=0, keepdims=True)


def to_features(left_ref, parts, start, stop, own_ref, other_ref):
    rows = own_ref.shape[0]
    size = parts[0][0].shape[0]
    starts = kernel_starts(parts)
    for k_f, row in enumerate(parts):
        weight = along_cols(row, start, stop)
        own_ref[col_block(own_ref, starts, k_f, size)] = mm_nt(left_ref[:rows], weight)
        other_ref[col_block(other_ref, starts, k_f, size)] = mm_nt(left_ref[rows:], weight)


def proj_kernel(half, attended_ref, parts, own_ref, other_ref):
    to_features(attended_ref, parts, 3 * half, 4 * half, own_ref, other_ref)


def qkv_back_kernel(half, grad_ref, parts, own_ref, other_ref):
    to_features(grad_ref, parts, 0, 3 * half, own_ref, other_ref)


def up_kernel(own_ref, other_ref, weight_ref, bias_ref, pre_ref, act_ref):
    rows, width = own_ref.shape
    size = weight_ref.shape[1] // 2
    for i in range(4):
        cols = slice(i * size, (i + 1) * size)
        weight = weight_ref[i * width : (i + 1) * width, :size]
        for j, ref in enumerate((own_ref, other_ref)):
            pre = mm(ref[...], weight) + bias_ref[:, cols]
            pre_ref[j * rows : (j + 1) * rows, cols] = pre
            act_ref[j * rows : (j + 1) * rows, cols] = gelu_tanh(pre).astype(BF)


def from_hidden(left_ref, weight_ref, at, own_ref, other_ref):
    rows, width = own_ref.shape
    size = weight_ref.shape[1] // 2
    block = width // 4
    for k in range(4):
        cols = slice(k * block, (k + 1) * block)
        weight = jnp.concatenate(
            [
                weight_ref[i * width + k * block : i * width + (k + 1) * block, at * size : (at + 1) * size]
                for i in range(4)
            ],
            axis=1,
        )
        own_ref[:, cols] = mm_nt(left_ref[:rows], weight)
        other_ref[:, cols] = mm_nt(left_ref[rows:], weight)


def down_kernel(act_ref, weight_ref, own_ref, other_ref):
    from_hidden(act_ref, weight_ref, 1, own_ref, other_ref)


def up_back_kernel(grad_ref, weight_ref, own_ref, other_ref):
    from_hidden(grad_ref, weight_ref, 0, own_ref, other_ref)


def gelu_slope(values):
    scale = math.sqrt(2.0 / math.pi)
    bent = jnp.tanh(scale * (values + 0.044715 * (values * values * values)))
    inner = scale * (1.0 + 3.0 * 0.044715 * (values * values))
    return 0.5 * (1.0 + bent) + 0.5 * values * (1.0 - bent * bent) * inner


def down_back_kernel(own_ref, other_ref, weight_ref, pre_ref, grad_ref, sum_ref):
    rows, width = own_ref.shape
    size = weight_ref.shape[1] // 2
    for i in range(4):
        cols = slice(i * size, (i + 1) * size)
        weight = weight_ref[i * width : (i + 1) * width, size:]
        total = 0.0
        for j, ref in enumerate((own_ref, other_ref)):
            here = slice(j * rows, (j + 1) * rows)
            grad = (mm(ref[...], weight) * gelu_slope(pre_ref[here, cols])).astype(BF)
            grad_ref[here, cols] = grad
            total = total + jnp.sum(grad.astype(F32), axis=0, keepdims=True)
        sum_ref[:, cols] = total


def block_starts(width):
    if not is_ring():
        return [0], width
    rows = width // 4
    f = lax.axis_index("fsdp")
    return [((f + k) & 3) * rows for k in range(4)], rows


def on_device(
    latents,
    noise_sample,
    timesteps,
    class_labels,
    w_block,
    w_output,
    w_top,
    w_head,
    w_embed,
    biases,
    m_block,
    m_output,
    m_top,
    m_head,
    m_embed,
    m_biases,
    v_block,
    v_output,
    v_top,
    v_head,
    v_embed,
    v_biases,
):
    f, c, t = lax.axis_index("fsdp"), lax.axis_index("ctx"), lax.axis_index("tp")
    nt = lax.axis_size("tp")
    places = lax.axis_size("fsdp") * lax.axis_size("ctx")
    place = f * lax.axis_size("ctx") + c
    row_count, block_count, local_width = w_block.shape
    half = local_width // 2
    width = local_width * nt
    group_images = latents.shape[0]
    images_all = group_images * places
    img_count = group_images // nt
    grid_side = latents.shape[3] // 2
    tok_count = latents.shape[2] // 2 * grid_side
    embed_rows = w_embed.shape[0]
    top_cols = w_top.shape[1]

    block_low = jnp.transpose(w_block, (1, 0, 2)).astype(BF)
    output_low = jnp.transpose(w_output, (0, 2, 1)).astype(BF)
    top_low = w_top.astype(BF)
    embed_low = w_embed.astype(BF)

    def core_half(blocks):
        low, high = blocks[:, :, :half], blocks[:, :, half:]
        return jnp.where(c == 0, low, high), jnp.where(c == 0, high, low)

    def beside(blocks):
        return jnp.concatenate([blocks[i] for i in range(blocks.shape[0])], axis=1)

    mixed = jnp.concatenate(
        [block_low[0:3], output_low[0:1], block_low[3:7], output_low[1:5]], axis=0
    )
    mine, other = core_half(mixed)
    mine, other = beside(mine), swap(beside(other), "ctx", 1)
    shards = jnp.concatenate(
        [jnp.where(c == 0, mine, other), jnp.where(c == 0, other, mine)], axis=0
    )
    lanes = Lanes(1, 1, 1)
    hidden_full = lax.all_gather(shards[:, 4 * half :], ("tp", "fsdp"), axis=0, tiled=True)
    parts = gather_grid(lanes, shards[:, : 4 * half])
    pace = Pace(lanes)

    patch_rows = rows_of(embed_low, FREQ + CLASSES - embed_rows * t, PATCH_ROWS)
    ids = jnp.concatenate([timesteps, class_labels]).astype(F32)
    ids = jnp.concatenate([ids, jnp.zeros((row_count - 2 * group_images % row_count,), F32)])[None]
    ids = ids.reshape(-1, row_count)
    small = jnp.concatenate([ids, patch_rows.astype(F32), w_head.T.astype(BF).astype(F32)], axis=0)
    small = gather_fc(small, pace)
    ids_all = small[:, : ids.shape[0]].reshape(places, -1)
    steps_all = ids_all[:, :group_images].reshape(images_all)
    labels_all = ids_all[:, group_images : 2 * group_images].reshape(images_all).astype(jnp.int32)
    small = small[:, ids.shape[0] :].transpose(1, 0, 2).reshape(2 * PATCH_ROWS, width)
    patch_part, w_head_t = small[:PATCH_ROWS], small[PATCH_ROWS:].astype(BF)
    embed_at = embed_rows * t + jnp.arange(embed_rows, dtype=jnp.int32)
    half_freq = FREQ // 2
    rates = jnp.exp(-math.log(10000.0) * (embed_at % half_freq).astype(F32) / half_freq)
    angles = steps_all[:, None] * rates[None, :]
    waves = jnp.where(embed_at[None, :] < half_freq, jnp.cos(angles), jnp.sin(angles))
    freq_low = jnp.where(embed_at[None, :] < FREQ, waves, 0.0).astype(BF)
    one_hot = (labels_all[:, None] + FREQ == embed_at[None, :]).astype(BF)
    own_cols = lambda row: lax.dynamic_slice_in_dim(row, place * row_count, row_count, 0)
    over_tp = jnp.concatenate([mm(freq_low, embed_low), patch_part.reshape(-1, row_count)], axis=0)
    over_tp = sum_over(over_tp, ("tp",), pace)
    t_pre = over_tp[:images_all] + own_cols(biases[1])
    w_patch = over_tp[images_all:].reshape(PATCH_ROWS, width).astype(BF)
    t_hidden = jax.nn.silu(t_pre).astype(BF)
    table_part = mm(one_hot, embed_low)
    top_at = top_cols * t + jnp.arange(top_cols, dtype=jnp.int32)
    cond_cols = mm(t_hidden, top_low)
    cond_cols = jnp.where(top_at[None, :] < width, cond_cols, 0.0)
    cond_wide = jnp.concatenate(
        [jnp.zeros((images_all, width), F32), cond_cols, jnp.zeros((images_all, width), F32)], axis=1
    )
    cond_wide = lax.dynamic_slice_in_dim(
        cond_wide, jnp.clip(width - top_cols * t, 0, width + top_cols), width, 1
    )
    cond_blocks = cond_wide.reshape(images_all, places, row_count).transpose(1, 0, 2)
    cond = sum_over(scatter_fc(cond_blocks, pace) + table_part, ("tp",), pace) + own_cols(biases[2])
    cond_low = jax.nn.silu(cond).astype(BF)
    mod_low = block_low[7:13]
    mod_cols = jnp.concatenate([mm(cond_low, mod_low[j]) for j in range(6)], axis=1)
    final_cols = jnp.where(top_at[None, :] < width, 0.0, mm(cond_low, top_low))
    all_cols = jnp.concatenate([mod_cols, final_cols], axis=1)
    group_cols = scatter_fc(all_cols.reshape(places, group_images, all_cols.shape[1]), pace)
    own_parts = exchange_tp(group_cols.reshape(nt, img_count, -1))
    mod_width = 6 * local_width
    modulation = (
        own_parts[:, :, :mod_width]
        .reshape(nt, img_count, 6, local_width)
        .transpose(1, 2, 0, 3)
        .reshape(img_count, 6, width)
    ) + biases[3:9][None]
    final_mod = own_parts[:, :, mod_width:].transpose(1, 0, 2).reshape(img_count, 3 * width)
    final_mod = final_mod[:, width:].reshape(img_count, 2, width) + biases[17:19][None]
    shift_f, scale_f = final_mod[:, 0], final_mod[:, 1]

    def own_images(values):
        return lax.dynamic_slice_in_dim(values, t * img_count, img_count, 0)

    latent_vals = own_images(latents).astype(F32)
    noise_vals = own_images(noise_sample).astype(F32)
    keep_rate, drop_rate = plan(own_images(timesteps))
    noisy = (
        keep_rate[:, None, None, None] * latent_vals + drop_rate[:, None, None, None] * noise_vals
    )
    patches = patchify(noisy).astype(BF)
    target = patchify(noise_vals)

    quarter = width // 4
    pos_rates = jnp.exp(-math.log(10000.0) * jnp.arange(quarter, dtype=F32) / quarter)
    side_angle = jnp.arange(grid_side, dtype=F32)[:, None] * pos_rates[None, :]
    side = jnp.concatenate([jnp.sin(side_angle), jnp.cos(side_angle)], axis=-1)
    rows_side = jnp.broadcast_to(side[:, None, :], (tok_count // grid_side, grid_side, 2 * quarter))
    cols_side = jnp.broadcast_to(side[None, :, :], (tok_count // grid_side, grid_side, 2 * quarter))
    positions = jnp.concatenate([rows_side, cols_side], axis=-1).reshape(tok_count, width)

    bias_width = jnp.stack([biases[0], biases[11], biases[16]])

    def heads_bias(rows):
        shaped = rows.reshape(-1, nt, 2, half)
        mine = jnp.where(c == 0, shaped[:, :, 0], shaped[:, :, 1])
        return by_xor(mine.transpose(1, 0, 2), t)

    bias_qv = heads_bias(biases[9:11])
    bias_qkv = jnp.stack([bias_qv[:, 0], jnp.zeros_like(bias_qv[:, 0]), bias_qv[:, 1]], axis=1).reshape(-1)
    bias_up = biases[12:16].reshape(4, nt, 2, half)
    bias_up = jnp.where(c == 0, bias_up[:, :, 0], bias_up[:, :, 1]).transpose(1, 0, 2).reshape(-1)

    own_count = img_count * tok_count
    core_width = nt * half
    matrix_flops = 4 * own_count * width * half

    def tokens(values):
        flat = values.reshape(own_count, width)
        return flat, swap(flat, "ctx", 1)

    def core_sum(own, other):
        return (own + swap(other, "ctx", 1)).reshape(img_count, tok_count, width)

    two_sums = [shape(own_count, width, F32)] * 2

    def run(body, outs, blocks, *args):
        return call(body, outs, args, blocks * nt * matrix_flops)

    resid_in = (
        jnp.einsum("btc,cd->btd", patches, w_patch, preferred_element_type=F32)
        + bias_width[0]
        + positions[None]
    )
    attn_in = modulate(resid_in, modulation[:, 0], modulation[:, 1]).astype(BF)
    attn_own, attn_other = tokens(attn_in)
    qkv_low, attended = run(
        functools.partial(qkv_kernel, tok_count, half),
        [shape(2 * own_count, 3 * core_width, BF), shape(2 * own_count, core_width, BF)],
        4,
        attn_own,
        attn_other,
        parts,
        bias_qkv[None],
    )
    attn_out = core_sum(
        *run(functools.partial(proj_kernel, half), two_sums, 1, attended, parts)
    ) + bias_width[1]
    resid_mid = resid_in + modulation[:, 2][:, None, :] * attn_out
    mlp_own, mlp_other = tokens(modulate(resid_mid, modulation[:, 3], modulation[:, 4]).astype(BF))
    up_pre, up_act = run(
        up_kernel,
        [shape(2 * own_count, 4 * core_width, F32), shape(2 * own_count, 4 * core_width, BF)],
        4,
        mlp_own,
        mlp_other,
        hidden_full,
        bias_up[None],
    )
    mlp_out = core_sum(
        *run(down_kernel, two_sums, 4, up_act, hidden_full)
    ) + bias_width[2]
    resid_out = resid_mid + modulation[:, 5][:, None, :] * mlp_out
    head_in = modulate(resid_out, shift_f, scale_f).astype(BF)
    predicted = jnp.einsum("btd,cd->btc", head_in, w_head_t, preferred_element_type=F32)
    error = predicted - target
    loss_part = jnp.sum(error * error) / images_all

    grad_pred = (2.0 / images_all * error).astype(BF)
    grad_head_in = jnp.einsum("btc,cd->btd", grad_pred, w_head_t, preferred_element_type=F32)
    grad_head = jnp.einsum("btc,btd->cd", grad_pred, head_in, preferred_element_type=F32)
    grad_resid, grad_shift_f, grad_scale_f = jax.vjp(modulate, resid_out, shift_f, scale_f)[1](
        grad_head_in
    )
    grad_gate_b = jnp.sum(grad_resid * mlp_out, axis=1)
    grad_mlp_own = (grad_resid * modulation[:, 5][:, None, :]).astype(BF)
    grad_b_down = jnp.sum(grad_mlp_own.astype(F32), axis=(0, 1))
    grad_mlp, grad_mlp_other = tokens(grad_mlp_own)
    both_mlp = jnp.concatenate([grad_mlp, grad_mlp_other], axis=0)
    hidden = 4 * half

    def by_hidden(left, right):
        return jnp.concatenate(
            [mm_tn(left, right[:, i * hidden : (i + 1) * hidden]).astype(BF) for i in range(4)], axis=0
        )

    grad_down = by_hidden(both_mlp, up_act)
    down_sum = lax.psum_scatter(grad_down, ("tp", "fsdp"), scatter_dimension=0, tiled=True)
    down_sum = down_sum.astype(F32)
    grad_mlp, grad_mlp_other, _ = lax.optimization_barrier((grad_mlp, grad_mlp_other, grad_down))
    grad_up, grad_b_up = run(
        down_back_kernel,
        [shape(2 * own_count, 4 * core_width, BF), shape(1, 4 * core_width, F32)],
        4,
        grad_mlp,
        grad_mlp_other,
        hidden_full,
        up_pre,
    )
    grad_b_up = grad_b_up[0]
    grad_mlp_in = core_sum(
        *run(up_back_kernel, two_sums, 4, grad_up, hidden_full)
    )
    grad_norm_b = jax.vjp(modulate, resid_mid, modulation[:, 3], modulation[:, 4])[1](grad_mlp_in)
    grad_resid = grad_resid + grad_norm_b[0]
    grad_gate_a = jnp.sum(grad_resid * attn_out, axis=1)
    grad_attn_own = (grad_resid * modulation[:, 2][:, None, :]).astype(BF)
    grad_b_proj = jnp.sum(grad_attn_own.astype(F32), axis=(0, 1))
    grad_attn, grad_attn_other = tokens(grad_attn_own)
    grad_qkv, grad_b_qkv = run(
        functools.partial(attention_back_kernel, tok_count, half),
        [shape(2 * own_count, 3 * core_width, BF), shape(1, 3 * core_width, F32)],
        2,
        grad_attn,
        grad_attn_other,
        parts,
        qkv_low,
    )
    grad_b_qkv = grad_b_qkv[0]
    attn_in = jnp.concatenate([attn_own, attn_other], axis=0)
    mlp_in = jnp.concatenate([mlp_own, mlp_other], axis=0)
    grad_attn = jnp.concatenate([grad_attn, grad_attn_other], axis=0)
    grad_up_w = by_hidden(mlp_in, grad_up)
    starts, block_rows = block_starts(width)
    firsts = [
        (
            mm_tn(attn_in, grad_qkv[:, i * 3 * half : (i + 1) * 3 * half]).astype(BF),
            mm_tn(grad_attn, attended[:, i * half : (i + 1) * half]).astype(BF),
        )
        for i in range(4)
    ]
    pieces = []
    for start in starts:
        line = []
        for k_t in range(4):
            cuts = [lax.dynamic_slice_in_dim(m, start, block_rows, 0) for m in firsts[k_t]]
            hidden_at = (t ^ k_t) * width + start
            cuts.append(lax.dynamic_slice_in_dim(grad_up_w, hidden_at, block_rows, 0))
            line.append(jnp.concatenate(cuts, axis=1))
        pieces.append(line)
    lanes = Lanes(1, 1, 1)
    first_sum = reduce_grid(lanes, pieces)
    grad_attn_in = core_sum(
        *run(functools.partial(qkv_back_kernel, half), two_sums, 3, grad_qkv, parts)
    )
    grad_norm_a = jax.vjp(modulate, resid_in, modulation[:, 0], modulation[:, 1])[1](grad_attn_in)
    grad_resid_low = (grad_resid + grad_norm_a[0]).astype(BF)
    grad_b_patch = jnp.sum(grad_resid_low.astype(F32), axis=(0, 1))
    grad_patch = jnp.einsum("btc,btd->cd", patches, grad_resid_low, preferred_element_type=F32)

    grad_mod = (
        jnp.stack(
            [
                grad_norm_a[1],
                grad_norm_a[2],
                grad_gate_a,
                grad_norm_b[1],
                grad_norm_b[2],
                grad_gate_b,
            ],
            axis=1,
        )
    )
    grad_final = (jnp.stack([grad_shift_f, grad_scale_f], axis=1))
    final_flat = jnp.concatenate(
        [jnp.zeros((img_count, width), F32), grad_final.reshape(img_count, 2 * width)], axis=1
    )
    to_tp = jnp.concatenate(
        [
            grad_mod.reshape(img_count, 6, nt, local_width)
            .transpose(2, 0, 1, 3)
            .reshape(nt, img_count, mod_width),
            final_flat.reshape(img_count, nt, top_cols).transpose(1, 0, 2),
        ],
        axis=-1,
    )
    group_grad = exchange_tp(to_tp).reshape(group_images, -1)
    all_grad = gather_fc(group_grad).reshape(images_all, -1)
    all_mod, all_final = all_grad[:, :mod_width], all_grad[:, mod_width:]
    cond_rows = cond_low.astype(F32)
    grad_w_mod = exact_dot(cond_rows.T, all_mod)
    mod_flat = mod_low.astype(F32).transpose(1, 0, 2).reshape(row_count, mod_width)
    top_rows = top_low.astype(F32)
    grad_cond_act = sum_over(
        exact_dot(all_mod, mod_flat.T) + exact_dot(all_final, top_rows.T), ("tp",)
    )
    grad_cond = jax.vjp(jax.nn.silu, cond)[1](grad_cond_act)[0]
    cond_all = gather_fc(grad_cond).transpose(1, 0, 2).reshape(images_all, width)
    grad_b_cond = jnp.sum(cond_all, axis=0)
    cond_padded = jnp.concatenate([cond_all, jnp.zeros((images_all, 2 * width), F32)], axis=1)
    cond_top = lax.dynamic_slice_in_dim(cond_padded, top_cols * t, top_cols, 1)
    top_grad = exact_dot(cond_rows.T, all_final) + exact_dot(t_hidden.astype(F32).T, cond_top)
    grad_hidden = sum_over(exact_dot(cond_top, top_rows.T), ("tp",))
    grad_t_pre = jax.vjp(jax.nn.silu, t_pre)[1](grad_hidden)[0]

    def heads_place(grad_rows):
        rows = by_xor(grad_rows, t).transpose(1, 0, 2)
        empty = jnp.zeros_like(rows)
        return jnp.stack(
            [jnp.where(c == 0, rows, empty), jnp.where(c == 0, empty, rows)], axis=2
        ).reshape(-1, width)

    qkv_rows = grad_b_qkv.reshape(nt, 3, half)
    up_rows = grad_b_up.reshape(nt, 4, half).transpose(1, 0, 2)
    empty_rows = jnp.zeros_like(up_rows)
    up_rows = jnp.stack(
        [jnp.where(c == 0, up_rows, empty_rows), jnp.where(c == 0, empty_rows, up_rows)], axis=2
    ).reshape(4, width)
    width_rows = (
        jnp.concatenate(
            [grad_b_patch[None], grad_b_proj[None], grad_b_down[None], grad_patch, grad_head], axis=0
        )
    )
    loss_row = jnp.broadcast_to(loss_part, (1, width))
    payload = jnp.concatenate(
        [
            width_rows[0:1],
            loss_row,
            jnp.zeros((1, width), F32),
            jnp.sum(grad_mod, axis=0),
            heads_place(jnp.stack([qkv_rows[:, 0], qkv_rows[:, 2]], axis=1)),
            width_rows[1:2],
            up_rows,
            width_rows[2:3],
            jnp.sum(grad_final, axis=0),
            width_rows[3:],
        ],
        axis=0,
    )
    payload = sum_over(payload, ("ctx", "tp", "fsdp"))
    loss_total = payload[1, 0]
    small_sum = lax.dynamic_slice_in_dim(payload[19:], place * row_count, row_count, 1)
    patch_sum, head_sum = small_sum[:PATCH_ROWS], small_sum[PATCH_ROWS:]
    head_grad_sum = head_sum.T

    def from_cores(total):
        low, high = total[:row_count], total[row_count:]
        own = jnp.where(c == 0, low, high)
        got = swap(jnp.where(c == 0, high, low), "ctx", 1)
        left, right = jnp.where(c == 0, own, got), jnp.where(c == 0, got, own)
        return [
            jnp.concatenate([left[:, i : i + half], right[:, i : i + half]], axis=1)
            for i in range(0, total.shape[1], half)
        ]

    first_own = from_cores(first_sum)
    down_own = from_cores(down_sum)
    block_sum = jnp.stack(first_own[0:3] + first_own[4:8])
    output_sum = jnp.transpose(jnp.stack(first_own[3:4] + down_own), (0, 2, 1))
    block_sum = jnp.concatenate(
        [block_sum, grad_w_mod.reshape(row_count, 6, local_width).transpose(1, 0, 2)], axis=0
    )
    embed_sum = exact_dot(one_hot.astype(F32).T, grad_cond) + exact_dot(
        freq_low.astype(F32).T, grad_t_pre
    )
    patch_padded = jnp.concatenate(
        [jnp.zeros((embed_rows, row_count), F32), patch_sum, jnp.zeros((embed_rows, row_count), F32)],
        axis=0,
    )
    patch_start = embed_rows * t + embed_rows - (FREQ + CLASSES)
    embed_sum = embed_sum + lax.dynamic_slice_in_dim(
        patch_padded, jnp.clip(patch_start, 0, embed_rows + PATCH_ROWS), embed_rows, 0
    )

    head_squares = jnp.where(t == 0, jnp.sum(head_grad_sum * head_grad_sum), 0.0)
    shard_squares = (
        jnp.sum(block_sum * block_sum)
        + jnp.sum(output_sum * output_sum)
        + jnp.sum(embed_sum * embed_sum)
        + jnp.sum(top_grad * top_grad)
        + head_squares
    )
    b1_part = jnp.where(t == 0, jnp.sum(grad_t_pre, axis=0), 0.0)
    b1_row = lax.dynamic_update_slice_in_dim(jnp.zeros((width,), F32), b1_part, place * row_count, 0)
    last = jnp.concatenate([b1_row, jnp.broadcast_to(shard_squares, (128,))])
    last = sum_over(last, ("ctx", "tp", "fsdp"))
    bias_sum = jnp.concatenate(
        [payload[0:1], last[None, :width], grad_b_cond[None], payload[3:19]], axis=0
    )
    grad_norm = jnp.sqrt(last[width] + jnp.sum(bias_sum * bias_sum))
    clip_factor = jnp.minimum(1.0, 1.0 / (grad_norm + 1e-06))
    upd_block = [
        jnp.transpose(u, (1, 0, 2))
        for u in adam_update(
            jnp.transpose(w_block, (1, 0, 2)),
            block_sum,
            jnp.transpose(m_block, (1, 0, 2)),
            jnp.transpose(v_block, (1, 0, 2)),
            clip_factor,
        )
    ]
    upd_output = adam_update(w_output, output_sum, m_output, v_output, clip_factor)
    upd_top = adam_update(w_top, top_grad, m_top, v_top, clip_factor)
    upd_head = adam_update(w_head, head_grad_sum, m_head, v_head, clip_factor)
    upd_embed = adam_update(w_embed, embed_sum, m_embed, v_embed, clip_factor)
    upd_biases = adam_update(biases, bias_sum, m_biases, v_biases, clip_factor)
    updates = (upd_block, upd_output, upd_top, upd_head, upd_embed, upd_biases)
    return (
        (loss_total, grad_norm)
        + tuple(u[0] for u in updates)
        + tuple(u[1] for u in updates)
        + tuple(u[2] for u in updates)
        + (bias_sum * clip_factor,)
    )


def solution(mesh):
    both = ("fsdp", "ctx")
    weights = (
        P(both, None, "tp"),
        P(None, "tp", both),
        P(both, "tp"),
        P(both, None),
        P("tp", both),
        P(),
    )
    images = (P(both, None, None, None), P(both, None, None, None), P(both), P(both))
    return jax.shard_map(
        on_device,
        mesh=mesh,
        in_specs=images + weights * 3,
        out_specs=(P(), P()) + weights * 3 + (P(),),
        check_vma=False,
    )
```

```python
import functools
import math

import jax
import jax.numpy as jnp
from jax import lax
from jax.experimental import pallas as pl
from jax.experimental.pallas import tpu as pltpu
from jax.sharding import PartitionSpec as P

HEAD_DIM = 64
CLASSES = 1000
FREQ = 256
TIMESTEPS = 1000
ADAM_STEP = 10
PATCH_ROWS = 16
PINS = (None, 1, 3, 4, 7)
CHAIN = (16, 1)
BIASES = (14, 1)

PRECISE = lax.Precision.HIGHEST
BF = jnp.bfloat16
F32 = jnp.float32


def exact_dot(left, right):
    return jnp.dot(left, right, precision=PRECISE)


def mm(left, right):
    return jnp.dot(left, right, preferred_element_type=F32)


def mm_nt(left, right):
    return lax.dot_general(left, right, (((1,), (1,)), ((), ())), preferred_element_type=F32)


def mm_tn(left, right):
    return lax.dot_general(left, right, (((0,), (0,)), ((), ())), preferred_element_type=F32)


def gelu_tanh(values):
    return jax.nn.gelu(values, approximate=True)


def plan(step_ids):
    fraction = (step_ids.astype(F32) / TIMESTEPS + 0.008) / 1.008
    kept_share = jnp.cos(fraction * (math.pi / 2.0)) ** 2
    return (jnp.sqrt(kept_share), jnp.sqrt(1.0 - kept_share))


def patchify(field):
    img_count, chan_count, row_count, col_count = field.shape
    shaped = field.reshape(img_count, chan_count, row_count // 2, 2, col_count // 2, 2)
    shaped = shaped.transpose(0, 2, 4, 1, 3, 5)
    return shaped.reshape(img_count, row_count // 2 * (col_count // 2), chan_count * 4)


def adam_update(weight, gradient, first_mom, second_mom, clip_factor):
    clipped = gradient * clip_factor
    first_new = 0.9 * first_mom + 0.1 * clipped
    second_new = 0.999 * second_mom + 0.001 * clipped * clipped
    corr_first = 1.0 - 0.9**ADAM_STEP
    corr_second = 1.0 - 0.999**ADAM_STEP
    direction = first_new / corr_first / (jnp.sqrt(second_new / corr_second) + 1e-08)
    return (weight - 0.04 * (direction + 0.01 * weight), first_new, second_new)


def swap(value, axis, mask):
    count = lax.axis_size(axis)
    return lax.ppermute(value, axis, [(i, i ^ mask) for i in range(count)])


def pull(value, k):
    count = lax.axis_size("fsdp")
    return lax.ppermute(value, "fsdp", [((i + k) % count, i) for i in range(count)])


def push(value, k):
    count = lax.axis_size("fsdp")
    return lax.ppermute(value, "fsdp", [(i, (i + k) % count) for i in range(count)])


def is_ring():
    return lax.axis_size("fsdp") == 4


def pick(pair, bit, axis=0):
    low = lax.index_in_dim(pair, 0, axis, keepdims=False)
    high = lax.index_in_dim(pair, 1, axis, keepdims=False)
    return jnp.where(bit == 1, high, low)


def ordered(own, other, bit, axis=0):
    return jnp.stack([jnp.where(bit == 0, own, other), jnp.where(bit == 0, other, own)], axis)


def bits(count):
    return [1 << b for b in range(count.bit_length() - 1)]


def by_xor(stack, rank):
    for mask in (1, 2):
        other = jnp.stack([stack[i ^ mask] for i in range(4)])
        stack = jnp.where(rank & mask == mask, other, stack)
    return stack


def free(value):
    return value


def sum_over(value, axes, pace=free):
    for axis in axes:
        count = lax.axis_size(axis)
        if count == 2:
            value = value + swap(pace(value), axis, 1)
        elif count == 4:
            sent = pace(value)
            one, two, three = [swap(sent, axis, k) for k in (1, 2, 3)]
            value = (value + one) + (two + three)
        else:
            value = lax.psum(value, axis)
    return value


def sum_slow(value, axes, pace, steps):
    for axis in axes:
        count = lax.axis_size(axis)
        if count > 4:
            value = lax.psum(value, axis)
            continue
        for mask in bits(count):
            moved = swap(pace(value), axis, mask)
            steps.append(moved)
            value = value + moved
    return value


def roll_lead(stack, steps):
    for mask in (1, 2):
        moved = jnp.stack([stack[(i + mask) % 4] for i in range(4)])
        stack = jnp.where(steps & mask == mask, moved, stack)
    return stack


def scatter_fc(blocks, pace=free):
    if not is_ring():
        return lax.psum_scatter(blocks, ("fsdp", "ctx"), scatter_dimension=0, tiled=False)
    f, c = lax.axis_index("fsdp"), lax.axis_index("ctx")
    held = blocks.reshape((4, 2) + blocks.shape[1:])
    held = pick(held, c, 1) + swap(pace(pick(held, 1 - c, 1)), "ctx", 1)
    held = pace(roll_lead(held, f))
    return (held[0] + push(held[2], 2)) + (push(held[1], 1) + push(held[3], 3))


def gather_fc(value, pace=free):
    if not is_ring():
        return lax.all_gather(value, ("fsdp", "ctx"), axis=0, tiled=False)
    f, c = lax.axis_index("fsdp"), lax.axis_index("ctx")
    sent = pace(value)
    held = jnp.stack([value] + [pull(sent, k) for k in (1, 2, 3)])
    held = roll_lead(held, (4 - f) & 3)
    held = ordered(held, swap(pace(held), "ctx", 1), c, 1)
    return held.reshape((8,) + value.shape)


def exchange_tp(blocks, pace=free):
    t = lax.axis_index("tp")
    mine = pace(by_xor(blocks, t))
    got = jnp.stack([mine[0]] + [swap(mine[k], "tp", k) for k in (1, 2, 3)])
    return by_xor(got, t)


class Lane:
    def __init__(self, depth):
        self.depth = depth
        self.ended = []

    def __call__(self, value, move):
        if len(self.ended) >= self.depth:
            value, _ = lax.optimization_barrier((value, self.ended[-self.depth]))
        moved = move(value)
        self.ended.append(moved)
        return moved


class Pace:
    def __init__(self, lanes, first, step, others=()):
        self.ended = list(lanes.ended)
        self.next, self.step = first, step
        self.others = list(others)

    def __call__(self, value):
        at = min(self.next, len(self.ended) - 1)
        if at >= 0:
            value, _ = lax.optimization_barrier((value, self.ended[at]))
        self.next += self.step
        other = self.others.pop(0) if self.others else None
        if other is not None:
            value, _ = lax.optimization_barrier((value, other))
        return value


class Lanes:
    def __init__(self, x, y, z):
        self.ended = []
        self.lane_x, self.lane_y, self.lane_z = Lane(x), Lane(y), Lane(z)

    def note(self, moved):
        self.ended.append(moved)
        return moved

    def x(self, value):
        return self.note(self.lane_x(value, lambda v: swap(v, "tp", 1)))

    def y(self, value):
        return self.note(self.lane_y(value, lambda v: swap(v, "tp", 2)))

    def pull(self, value, k):
        return self.note(self.lane_z(value, lambda v: pull(v, k)))

    def push(self, value, k):
        return self.note(self.lane_z(value, lambda v: push(v, k)))


def add(left, right):
    return left.astype(F32) + right.astype(F32)


def add_low(left, right):
    return add(left, right).astype(BF)


def reduce_grid(lanes, main):
    if not is_ring():
        parts = main[0]
        along_x = swap(parts[1], "tp", 1)
        along_y = swap(add_low(parts[2], swap(parts[3], "tp", 1)), "tp", 2)
        both = add_low(add(parts[0], along_x), along_y)
        return lax.psum_scatter(both, "fsdp", scatter_dimension=0, tiled=True).astype(F32)
    far_2, far_1 = lanes.y(main[2][3]), None
    far_3 = lanes.x(main[3][3])
    y_2 = lanes.y(main[2][2])
    x_2 = lanes.x(add_low(main[2][1], far_2))
    far_1 = lanes.y(main[1][3])
    x_3 = lanes.x(main[3][1])
    y_3 = lanes.y(add_low(main[3][2], far_3))
    sum_2 = lanes.push(add_low(add(main[2][0], x_2), y_2), 1)
    y_1 = lanes.y(main[1][2])
    x_1 = lanes.x(add_low(main[1][1], far_1))
    far_0 = lanes.x(main[0][3])
    sum_3 = lanes.push(add_low(add(main[3][0], x_3), y_3), 3)
    x_0 = lanes.x(main[0][1])
    sum_1 = add(add(add(main[1][0], x_1), y_1), sum_2).astype(BF)
    sum_1 = lanes.push(sum_1, 1)
    y_0 = lanes.y(add_low(main[0][2], far_0))
    return add(add(add(main[0][0], x_0), y_0), sum_3) + sum_1.astype(F32)


def rows_of(table, start, count):
    pad = jnp.zeros((count,) + table.shape[1:], table.dtype)
    padded = jnp.concatenate([pad, table, pad], axis=0)
    return lax.dynamic_slice_in_dim(padded, jnp.clip(start + count, 0, table.shape[0] + count), count, 0)


class View:
    def __init__(self, array, width, index):
        self.array, self.width, self.index = array, width, index


def whole_block(dims):
    return pl.BlockSpec(dims, lambda i: (0,) * len(dims), pipeline_mode=pl.Buffered(1))


def call(body, outs, args, flops, scratch=()):
    flat, tree = jax.tree.flatten(args)
    arrays, specs, held = [], [], 0
    for leaf in flat:
        if isinstance(leaf, View):
            dims = (leaf.array.shape[0], leaf.width)
            at = leaf.index
            specs.append(
                pl.BlockSpec(dims, lambda i, at=at: (0, at), pipeline_mode=pl.Buffered(1))
            )
            arrays.append(leaf.array)
        else:
            dims = leaf.shape
            specs.append(whole_block(dims))
            arrays.append(leaf)
        held += math.prod(dims) * arrays[-1].dtype.itemsize
    held += sum(o.size * o.dtype.itemsize for o in outs)
    room = 2 * held + sum(4 * math.prod(a.shape) for a in scratch) + 8 * 1024 * 1024

    def kernel(*refs):
        body(*jax.tree.unflatten(tree, refs[: len(flat)]), *refs[len(flat) :])

    return pl.pallas_call(
        kernel,
        grid=(1,),
        out_shape=outs,
        in_specs=specs,
        out_specs=[whole_block(o.shape) for o in outs],
        scratch_shapes=list(scratch),
        compiler_params=pltpu.CompilerParams(vmem_limit_bytes=56 * 1024 * 1024),
        cost_estimate=pl.CostEstimate(flops=flops, bytes_accessed=held, transcendentals=0),
    )(*arrays)


def shape(rows, cols, dtype):
    return jax.ShapeDtypeStruct((rows, cols), dtype)


def down_rows(parts, k_t, start, stop):
    return jnp.concatenate([row[k_t][:, start:stop] for row in parts], axis=0)


def head_masks(half):
    at = lax.broadcasted_iota(jnp.int32, (1, half), 1) // HEAD_DIM
    return [at == h for h in range(half // HEAD_DIM)]


def softmax_rows(scores):
    top = jnp.max(scores, axis=-1, keepdims=True)
    grown = jnp.exp(scores - top)
    return grown / jnp.sum(grown, axis=-1, keepdims=True)


def merged(masks, values):
    total = values[-1]
    for mask, value in zip(masks[:-1], values[:-1]):
        total = jnp.where(mask, value, total)
    return total


def split_t(ref):
    width = ref.shape[0] // 4
    return [[ref.at[i * width : (i + 1) * width] for i in range(4)]]


def qkv_kernel(tok_count, half, own_ref, other_ref, weight_ref, bias_ref, qkv_ref, attended_ref):
    parts = split_t(weight_ref)
    rows = own_ref.shape[0]
    masks = head_masks(half)
    for i, ref in enumerate((own_ref, other_ref)):
        left = ref[...]
        for k_t in range(4):
            cols = slice(k_t * 3 * half, (k_t + 1) * 3 * half)
            weight = down_rows(parts, k_t, 0, 3 * half)
            qkv_ref[i * rows : (i + 1) * rows, cols] = (
                mm(left, weight) + bias_ref[:, cols]
            ).astype(BF)
    for k_t in range(4):
        at = k_t * 3 * half
        for row in range(0, 2 * rows, tok_count):
            here = slice(row, row + tok_count)
            query = qkv_ref[here, at : at + half]
            key = qkv_ref[here, at + half : at + 2 * half]
            value = qkv_ref[here, at + 2 * half : at + 3 * half]
            got = []
            for mask in masks:
                masked = jnp.where(mask, query, jnp.zeros_like(query))
                probs = softmax_rows(mm_nt(masked, key) * 0.125).astype(BF)
                got.append(mm(probs, value))
            attended_ref[here, k_t * half : (k_t + 1) * half] = merged(masks, got).astype(BF)


def attention_back_kernel(
    tok_count, half, own_ref, other_ref, weight_ref, qkv_ref, out_ref, sum_ref
):
    parts = split_t(weight_ref)
    rows = own_ref.shape[0]
    masks = head_masks(half)
    left = [ref[...] for ref in (own_ref, other_ref)]
    for k_t in range(4):
        at = k_t * 3 * half
        weight = down_rows(parts, k_t, 0, half)
        for i in range(2):
            grad_half = mm(left[i], weight).astype(BF)
            for row in range(0, rows, tok_count):
                here = slice(i * rows + row, i * rows + row + tok_count)
                grad = grad_half[row : row + tok_count]
                query = qkv_ref[here, at : at + half]
                key = qkv_ref[here, at + half : at + 2 * half]
                value = qkv_ref[here, at + 2 * half : at + 3 * half]
                grad_q, grad_k, grad_v = [], [], []
                for mask in masks:
                    zero = jnp.zeros_like(query)
                    probs = softmax_rows(mm_nt(jnp.where(mask, query, zero), key) * 0.125)
                    grad_p = mm_nt(jnp.where(mask, grad, zero), value)
                    grad_s = (
                        probs * (grad_p - jnp.sum(grad_p * probs, axis=-1, keepdims=True))
                    ).astype(BF)
                    grad_q.append(mm(grad_s, key))
                    grad_k.append(mm_tn(grad_s, query))
                    grad_v.append(mm_tn(probs.astype(BF), grad))
                out_ref[here, at : at + half] = (merged(masks, grad_q) * 0.125).astype(BF)
                out_ref[here, at + half : at + 2 * half] = (merged(masks, grad_k) * 0.125).astype(BF)
                out_ref[here, at + 2 * half : at + 3 * half] = merged(masks, grad_v).astype(BF)
        cols = slice(at, at + 3 * half)
        sum_ref[:, cols] = jnp.sum(out_ref[:, cols].astype(F32), axis=0, keepdims=True)


def features_kernel(left_ref, weight_ref, own_ref, other_ref):
    parts = split_t(weight_ref)
    rows, size = own_ref.shape
    block = size // 4
    for k in range(4):
        cols = slice(k * block, (k + 1) * block)
        weight = jnp.concatenate([p[cols, :] for p in parts[0]], axis=1)
        own_ref[:, cols] = mm_nt(left_ref[:rows], weight)
        other_ref[:, cols] = mm_nt(left_ref[rows:], weight)


def gelu_slope(values):
    scale = math.sqrt(2.0 / math.pi)
    bent = jnp.tanh(scale * (values + 0.044715 * (values * values * values)))
    inner = scale * (1.0 + 3.0 * 0.044715 * (values * values))
    return 0.5 * (1.0 + bent) + 0.5 * values * (1.0 - bent * bent) * inner


def mlp_kernel(own_ref, other_ref, up_ref, down_ref, bias_ref, pre_ref, act_ref, own_out, other_out):
    rows = own_ref.shape[0]

    @pl.when(pl.program_id(0) == 0)
    def _():
        own_out[...] = jnp.zeros_like(own_out)
        other_out[...] = jnp.zeros_like(other_out)

    for i, (ref, out) in enumerate(((own_ref, own_out), (other_ref, other_out))):
        here = slice(i * rows, (i + 1) * rows)
        pre = mm(ref[...], up_ref[...]) + bias_ref[...]
        pre_ref[here, :] = pre
        act = gelu_tanh(pre).astype(BF)
        act_ref[here, :] = act
        out[...] += mm_nt(act, down_ref[...])


def mlp_back_kernel(
    own_ref,
    other_ref,
    own_in,
    other_in,
    up_ref,
    down_ref,
    pre_ref,
    act_ref,
    grad_ref,
    sum_ref,
    own_out,
    other_out,
    flipped,
):
    rows, width = own_ref.shape
    size = up_ref.shape[1]

    @pl.when(pl.program_id(0) == 0)
    def _():
        own_out[...] = jnp.zeros_like(own_out)
        other_out[...] = jnp.zeros_like(other_out)
        for i, ref in enumerate((own_in, other_in, own_ref, other_ref)):
            flipped[
                i // 2 * width : (i // 2 + 1) * width, i % 2 * rows : (i % 2 + 1) * rows
            ] = ref[...].T

    total, grads = 0.0, []
    for i, (ref, out) in enumerate(((own_ref, own_out), (other_ref, other_out))):
        here = slice(i * rows, (i + 1) * rows)
        grad = (mm(ref[...], down_ref[...]) * gelu_slope(pre_ref[here, :])).astype(BF)
        total = total + col_sum(grad.astype(F32))
        out[...] += mm_nt(grad, up_ref[...])
        grads.append(grad)
    sum_ref[...] = total
    grad_ref[:, :size] = mm(flipped[:width, :], jnp.concatenate(grads, axis=0)).astype(BF)
    grad_ref[:, size:] = mm(flipped[width:, :], act_ref[...]).astype(BF)


def over_hidden(kernel, counts, outs, args, flops, scratch=()):
    def spec(block, index):
        return pl.BlockSpec(block, index)

    return pl.pallas_call(
        kernel,
        grid=(counts,),
        out_shape=[o[0] for o in outs],
        in_specs=[spec(a[1], a[2]) for a in args],
        out_specs=[spec(o[1], o[2]) for o in outs],
        scratch_shapes=list(scratch),
        compiler_params=pltpu.CompilerParams(vmem_limit_bytes=56 * 1024 * 1024),
        cost_estimate=pl.CostEstimate(
            flops=flops, bytes_accessed=32 * 1024 * 1024, transcendentals=0
        ),
    )(*[a[0] for a in args])


def piece_kernel(half, places, attn, grad_attn, grad_qkv_ref, attended_ref, *refs):
    outs, flipped = refs[:-1], refs[-1]
    t = lax.axis_index("tp")
    size = outs[0].shape[0]
    width = attn[0].shape[1]
    tokens = attn[0].shape[0]
    for i, pair in enumerate((attn, grad_attn)):
        for j, ref in enumerate(pair):
            flipped[i * width : (i + 1) * width, j * tokens : (j + 1) * tokens] = ref[...].T
    for i, k_f in enumerate(places):
        if size == width:
            start = 0
        else:
            start = pl.multiple_of(((lax.axis_index("fsdp") + k_f) & 3) * size, size)
        left = [flipped[pl.ds(i * width + start, size), :] for i in range(2)]
        for k_t in range(4):
            out = outs[i * 4 + k_t]
            place = t ^ k_t

            def cols(count):
                return pl.ds(pl.multiple_of(place * count, count), count)

            out[:, : 3 * half] = mm(left[0], grad_qkv_ref[:, cols(3 * half)]).astype(BF)
            out[:, 3 * half :] = mm(left[1], attended_ref[:, cols(half)]).astype(BF)


def normed(values):
    center = values - jnp.mean(values, axis=-1, keepdims=True)
    spread = jnp.mean(center * center, axis=-1, keepdims=True)
    inverse = lax.rsqrt(spread + 1e-06)
    return center * inverse, inverse


def norm_back(grad, norm, inverse):
    mean = jnp.mean(grad, axis=-1, keepdims=True)
    slope = jnp.mean(grad * norm, axis=-1, keepdims=True)
    return inverse * (grad - mean - norm * slope)


def col_sum(values):
    return jnp.sum(values, axis=0, keepdims=True)


def enter_kernel(images, patch_ref, w_ref, place_ref, mod_ref, resid_ref, attn_ref):
    count = patch_ref.shape[0] // images
    for i in range(images):
        here = slice(i * count, (i + 1) * count)
        resid = mm(patch_ref[here], w_ref[...]) + place_ref[...]
        resid_ref[here] = resid
        mod = mod_ref[i]
        attn_ref[here] = (normed(resid)[0] * (1.0 + mod[1:2]) + mod[0:1]).astype(BF)


def middle_kernel(images, own_ref, got_ref, bias_ref, resid_ref, mod_ref, out_ref, mid_ref, mlp_ref):
    count = own_ref.shape[0] // images
    for i in range(images):
        here = slice(i * count, (i + 1) * count)
        mod = mod_ref[i]
        out = own_ref[here] + got_ref[here] + bias_ref[...]
        out_ref[here] = out
        mid = resid_ref[here] + mod[2:3] * out
        mid_ref[here] = mid
        mlp_ref[here] = (normed(mid)[0] * (1.0 + mod[4:5]) + mod[3:4]).astype(BF)


def top_kernel(
    images,
    own_ref,
    got_ref,
    bias_ref,
    mid_ref,
    mod_ref,
    final_ref,
    head_ref,
    target_ref,
    resid_ref,
    mlp_ref,
    rows_ref,
    head_grad_ref,
    loss_ref,
    images_all,
):
    count = own_ref.shape[0] // images
    loss, head_grad = 0.0, 0.0
    for i in range(images):
        here = slice(i * count, (i + 1) * count)
        gate = mod_ref[i][5:6]
        shift, scale = final_ref[i][0:1], final_ref[i][1:2]
        out = own_ref[here] + got_ref[here] + bias_ref[...]
        norm, inverse = normed(mid_ref[here] + gate * out)
        head_in = (norm * (1.0 + scale) + shift).astype(BF)
        error = mm_nt(head_in, head_ref[...]) - target_ref[here]
        loss = loss + jnp.sum(col_sum(error * error), axis=1, keepdims=True) / images_all
        grad_pred = (2.0 / images_all * error).astype(BF)
        grad = mm(grad_pred, head_ref[...])
        head_grad = head_grad + mm_tn(grad_pred, head_in)
        resid = norm_back(grad * (1.0 + scale), norm, inverse)
        resid_ref[here] = resid
        mlp = (resid * gate).astype(BF)
        mlp_ref[here] = mlp
        rows_ref[i] = jnp.concatenate(
            [col_sum(grad), col_sum(grad * norm), col_sum(resid * out), col_sum(mlp.astype(F32))], axis=0
        )
    head_grad_ref[...] = head_grad
    loss_ref[...] = jnp.broadcast_to(loss, loss_ref.shape)


def middle_back_kernel(
    images, own_ref, got_ref, mid_ref, mod_ref, resid_ref, out_ref, new_ref, attn_ref, rows_ref
):
    count = own_ref.shape[0] // images
    for i in range(images):
        here = slice(i * count, (i + 1) * count)
        mod = mod_ref[i]
        grad = own_ref[here] + got_ref[here]
        norm, inverse = normed(mid_ref[here])
        resid = resid_ref[here] + norm_back(grad * (1.0 + mod[4:5]), norm, inverse)
        new_ref[here] = resid
        attn = (resid * mod[2:3]).astype(BF)
        attn_ref[here] = attn
        rows_ref[i] = jnp.concatenate(
            [
                col_sum(grad),
                col_sum(grad * norm),
                col_sum(resid * out_ref[here]),
                col_sum(attn.astype(F32)),
            ],
            axis=0,
        )


def enter_back_kernel(
    images, own_ref, got_ref, in_ref, mod_ref, resid_ref, patch_ref, rows_ref, patch_grad_ref
):
    count = own_ref.shape[0] // images
    patch_grad = 0.0
    for i in range(images):
        here = slice(i * count, (i + 1) * count)
        grad = own_ref[here] + got_ref[here]
        norm, inverse = normed(in_ref[here])
        resid = resid_ref[here] + norm_back(grad * (1.0 + mod_ref[i][1:2]), norm, inverse)
        low = resid.astype(BF)
        rows_ref[i] = jnp.concatenate(
            [col_sum(grad), col_sum(grad * norm), col_sum(low.astype(F32))], axis=0
        )
        patch_grad = patch_grad + mm_tn(patch_ref[here], low)
    patch_grad_ref[...] = patch_grad


def adam_kernel(clip_ref, w_ref, g_ref, m_ref, v_ref, new_ref, first_ref, second_ref):
    new_ref[...], first_ref[...], second_ref[...] = adam_update(
        w_ref[...], g_ref[...], m_ref[...], v_ref[...], clip_ref[0, 0]
    )


def adam_blocks(weight, gradient, first_mom, second_mom, clip_factor):
    rows, cols = weight.shape
    count = 4 if rows % 32 == 0 else 1
    block = pl.BlockSpec((rows // count, cols), lambda i: (i, 0))
    return pl.pallas_call(
        adam_kernel,
        grid=(count,),
        out_shape=[jax.ShapeDtypeStruct(weight.shape, F32)] * 3,
        in_specs=[pl.BlockSpec(memory_space=pltpu.SMEM)] + [block] * 4,
        out_specs=[block] * 3,
        compiler_params=pltpu.CompilerParams(vmem_limit_bytes=32 * 1024 * 1024),
        cost_estimate=pl.CostEstimate(flops=0, bytes_accessed=28 * weight.size, transcendentals=0),
    )(clip_factor.reshape(1, 1), weight, gradient, first_mom, second_mom)


def shards_kernel(half, first_ref, first_got, down_ref, down_got, mod_ref, block_ref, output_ref, square_ref):
    c = lax.axis_index("ctx")
    count = first_ref.shape[0]
    total = 0.0

    def joined(own_ref, got_ref, i):
        own, got = own_ref[:, i * half : (i + 1) * half], got_ref[:, i * half : (i + 1) * half]
        both = jnp.concatenate([jnp.where(c == 0, own, got), jnp.where(c == 0, got, own)], axis=1)
        return both, col_sum(both * both)

    for i in range(7):
        both, squares = joined(first_ref, first_got, i) if i < 3 else joined(down_ref, down_got, i - 3)
        block_ref[i * count : (i + 1) * count, :] = both
        total = total + squares
    for i in range(5):
        both, squares = joined(first_ref, first_got, 3) if i == 0 else joined(down_ref, down_got, i + 3)
        output_ref[i * 2 * half : (i + 1) * 2 * half, :] = both.T
        total = total + squares
    for i in range(6):
        part = mod_ref[:, i * 2 * half : (i + 1) * 2 * half]
        block_ref[(7 + i) * count : (8 + i) * count, :] = part
        total = total + col_sum(part * part)
    square_ref[...] = total


def on_device(
    latents,
    noise_sample,
    timesteps,
    class_labels,
    w_block,
    w_output,
    w_top,
    w_head,
    w_embed,
    biases,
    m_block,
    m_output,
    m_top,
    m_head,
    m_embed,
    m_biases,
    v_block,
    v_output,
    v_top,
    v_head,
    v_embed,
    v_biases,
):
    f, c, t = lax.axis_index("fsdp"), lax.axis_index("ctx"), lax.axis_index("tp")
    nt = lax.axis_size("tp")
    places = lax.axis_size("fsdp") * lax.axis_size("ctx")
    place = f * lax.axis_size("ctx") + c
    row_count, block_count, local_width = w_block.shape
    half = local_width // 2
    width = local_width * nt
    group_images = latents.shape[0]
    images_all = group_images * places
    img_count = group_images // nt
    grid_side = latents.shape[3] // 2
    tok_count = latents.shape[2] // 2 * grid_side
    embed_rows = w_embed.shape[0]
    top_cols = w_top.shape[1]

    block_low = jnp.transpose(w_block, (1, 0, 2)).astype(BF)
    output_low = jnp.transpose(w_output, (0, 2, 1)).astype(BF)
    top_low = w_top.astype(BF)
    embed_low = w_embed.astype(BF)

    def core_half(blocks):
        low, high = blocks[:, :, :half], blocks[:, :, half:]
        return jnp.where(c == 0, low, high), jnp.where(c == 0, high, low)

    def beside(blocks):
        return jnp.concatenate([blocks[i] for i in range(blocks.shape[0])], axis=1)

    mixed = jnp.concatenate(
        [block_low[0:3], output_low[0:1], block_low[3:7], output_low[1:5]], axis=0
    )
    mine, other = core_half(mixed)
    mine, other = beside(mine), swap(beside(other), "ctx", 1)
    shards = jnp.concatenate(
        [jnp.where(c == 0, mine, other), jnp.where(c == 0, other, mine)], axis=0
    )
    full = lax.all_gather(shards, ("tp", "fsdp"), axis=0, tiled=True)
    pace = free

    patch_rows = rows_of(embed_low, FREQ + CLASSES - embed_rows * t, PATCH_ROWS)
    ids = jnp.concatenate([timesteps, class_labels]).astype(F32)
    ids = jnp.concatenate([ids, jnp.zeros((row_count - 2 * group_images % row_count,), F32)])[None]
    ids = ids.reshape(-1, row_count)
    small = jnp.concatenate([ids, patch_rows.astype(F32), w_head.T.astype(BF).astype(F32)], axis=0)
    small = gather_fc(small, pace)
    ids_all = small[:, : ids.shape[0]].reshape(places, -1)
    steps_all = ids_all[:, :group_images].reshape(images_all)
    labels_all = ids_all[:, group_images : 2 * group_images].reshape(images_all).astype(jnp.int32)
    small = small[:, ids.shape[0] :].transpose(1, 0, 2).reshape(2 * PATCH_ROWS, width)
    patch_part, w_head_t = small[:PATCH_ROWS], small[PATCH_ROWS:].astype(BF)
    embed_at = embed_rows * t + jnp.arange(embed_rows, dtype=jnp.int32)
    half_freq = FREQ // 2
    rates = jnp.exp(-math.log(10000.0) * (embed_at % half_freq).astype(F32) / half_freq)
    angles = steps_all[:, None] * rates[None, :]
    waves = jnp.where(embed_at[None, :] < half_freq, jnp.cos(angles), jnp.sin(angles))
    freq_low = jnp.where(embed_at[None, :] < FREQ, waves, 0.0).astype(BF)
    one_hot = (labels_all[:, None] + FREQ == embed_at[None, :]).astype(BF)
    own_cols = lambda row: lax.dynamic_slice_in_dim(row, place * row_count, row_count, 0)
    over_tp = jnp.concatenate([mm(freq_low, embed_low), patch_part.reshape(-1, row_count)], axis=0)
    over_tp = sum_over(over_tp, ("tp",), pace)
    t_pre = over_tp[:images_all] + own_cols(biases[1])
    w_patch = over_tp[images_all:].reshape(PATCH_ROWS, width).astype(BF)
    t_hidden = jax.nn.silu(t_pre).astype(BF)
    table_part = mm(one_hot, embed_low)
    top_at = top_cols * t + jnp.arange(top_cols, dtype=jnp.int32)
    cond_cols = mm(t_hidden, top_low)
    cond_cols = jnp.where(top_at[None, :] < width, cond_cols, 0.0)
    cond_wide = jnp.concatenate(
        [jnp.zeros((images_all, width), F32), cond_cols, jnp.zeros((images_all, width), F32)], axis=1
    )
    cond_wide = lax.dynamic_slice_in_dim(
        cond_wide, jnp.clip(width - top_cols * t, 0, width + top_cols), width, 1
    )
    cond_blocks = cond_wide.reshape(images_all, places, row_count).transpose(1, 0, 2)
    cond = sum_over(scatter_fc(cond_blocks, pace) + table_part, ("tp",), pace) + own_cols(biases[2])
    cond_low = jax.nn.silu(cond).astype(BF)
    mod_low = block_low[7:13]
    mod_cols = jnp.concatenate([mm(cond_low, mod_low[j]) for j in range(6)], axis=1)
    final_cols = jnp.where(top_at[None, :] < width, 0.0, mm(cond_low, top_low))
    all_cols = jnp.concatenate([mod_cols, final_cols], axis=1)
    group_cols = scatter_fc(all_cols.reshape(places, group_images, all_cols.shape[1]), pace)
    own_parts = exchange_tp(group_cols.reshape(nt, img_count, -1), pace)
    mod_width = 6 * local_width
    modulation = (
        own_parts[:, :, :mod_width]
        .reshape(nt, img_count, 6, local_width)
        .transpose(1, 2, 0, 3)
        .reshape(img_count, 6, width)
    ) + biases[3:9][None]
    final_mod = own_parts[:, :, mod_width:].transpose(1, 0, 2).reshape(img_count, 3 * width)
    final_mod = final_mod[:, width:].reshape(img_count, 2, width) + biases[17:19][None]
    shift_f, scale_f = final_mod[:, 0], final_mod[:, 1]

    def own_images(values):
        return lax.dynamic_slice_in_dim(values, t * img_count, img_count, 0)

    latent_vals = own_images(latents).astype(F32)
    noise_vals = own_images(noise_sample).astype(F32)
    keep_rate, drop_rate = plan(own_images(timesteps))
    noisy = (
        keep_rate[:, None, None, None] * latent_vals + drop_rate[:, None, None, None] * noise_vals
    )
    patches = patchify(noisy).astype(BF)
    target = patchify(noise_vals)

    quarter = width // 4
    pos_rates = jnp.exp(-math.log(10000.0) * jnp.arange(quarter, dtype=F32) / quarter)
    side_angle = jnp.arange(grid_side, dtype=F32)[:, None] * pos_rates[None, :]
    side = jnp.concatenate([jnp.sin(side_angle), jnp.cos(side_angle)], axis=-1)
    rows_side = jnp.broadcast_to(side[:, None, :], (tok_count // grid_side, grid_side, 2 * quarter))
    cols_side = jnp.broadcast_to(side[None, :, :], (tok_count // grid_side, grid_side, 2 * quarter))
    positions = jnp.concatenate([rows_side, cols_side], axis=-1).reshape(tok_count, width)

    bias_width = jnp.stack([biases[0], biases[11], biases[16]])

    def heads_bias(rows):
        shaped = rows.reshape(-1, nt, 2, half)
        return jnp.where(c == 0, shaped[:, :, 0], shaped[:, :, 1]).transpose(1, 0, 2)

    bias_qv = heads_bias(biases[9:11])
    bias_qkv = jnp.stack([bias_qv[:, 0], jnp.zeros_like(bias_qv[:, 0]), bias_qv[:, 1]], axis=1).reshape(-1)
    bias_up = heads_bias(biases[12:16]).reshape(-1)
    qkv_view, proj_view = View(full, 3 * half, 0), View(full, half, 3)

    own_count = img_count * tok_count
    core_width = nt * half
    matrix_flops = 4 * own_count * width * half

    two_sums = [shape(own_count, width, F32)] * 2

    def run(body, outs, blocks, *args):
        return call(body, outs, args, blocks * nt * matrix_flops)

    def small_run(body, outs, *args):
        return call(functools.partial(body, img_count), outs, args, 0)

    def cube(rows):
        return jax.ShapeDtypeStruct((img_count, rows, width), F32)

    flat_f32, flat_low = shape(own_count, width, F32), shape(own_count, width, BF)

    patches = patches.reshape(own_count, PATCH_ROWS)
    resid_in, attn_own = small_run(
        enter_kernel,
        [flat_f32, flat_low],
        patches,
        w_patch,
        positions + bias_width[0],
        modulation,
    )
    attn_other = swap(attn_own, "ctx", 1)
    qkv_low, attended = run(
        functools.partial(qkv_kernel, tok_count, half),
        [shape(2 * own_count, 3 * core_width, BF), shape(2 * own_count, core_width, BF)],
        4,
        attn_own,
        attn_other,
        qkv_view,
        bias_qkv[None],
    )
    own, other = run(features_kernel, two_sums, 1, attended, proj_view)
    attn_out, resid_mid, mlp_own = small_run(
        middle_kernel,
        [flat_f32, flat_f32, flat_low],
        own,
        swap(other, "ctx", 1),
        bias_width[1:2],
        resid_in,
        modulation,
    )
    mlp_other = swap(mlp_own, "ctx", 1)
    hidden = 4 * half
    fixed = lambda i: (0, 0)
    column = lambda i: (0, i)
    wide_rows = (own_count, width)
    up_pre, up_act, own, other = over_hidden(
        mlp_kernel,
        nt,
        [
            (shape(2 * own_count, nt * hidden, F32), (2 * own_count, hidden), column),
            (shape(2 * own_count, nt * hidden, BF), (2 * own_count, hidden), column),
            (flat_f32, wide_rows, fixed),
            (flat_f32, wide_rows, fixed),
        ],
        [
            (mlp_own, wide_rows, fixed),
            (mlp_other, wide_rows, fixed),
            (full, (width, hidden), lambda i: (i, 1)),
            (full, (width, hidden), lambda i: (i, 2)),
            (bias_up[None], (1, hidden), column),
        ],
        8 * nt * matrix_flops,
    )
    grad_resid, grad_mlp, top_rows_grad, grad_head, loss_part = small_run(
        functools.partial(top_kernel, images_all=images_all),
        [flat_f32, flat_low, cube(4), shape(PATCH_ROWS, width, F32), shape(1, 128, F32)],
        own,
        swap(other, "ctx", 1),
        bias_width[2:3],
        resid_mid,
        modulation,
        final_mod,
        w_head_t,
        target.reshape(own_count, PATCH_ROWS),
    )
    loss_part = loss_part[0, 0]

    grad_mlp_other = swap(grad_mlp, "ctx", 1)
    grad_hidden_w, grad_b_up, own, other = over_hidden(
        mlp_back_kernel,
        nt,
        [
            (shape(nt * width, 2 * hidden, BF), (width, 2 * hidden), lambda i: (i, 0)),
            (shape(1, nt * hidden, F32), (1, hidden), column),
            (flat_f32, wide_rows, fixed),
            (flat_f32, wide_rows, fixed),
        ],
        [
            (grad_mlp, wide_rows, fixed),
            (grad_mlp_other, wide_rows, fixed),
            (mlp_own, wide_rows, fixed),
            (mlp_other, wide_rows, fixed),
            (full, (width, hidden), lambda i: (i, 1)),
            (full, (width, hidden), lambda i: (i, 2)),
            (up_pre, (2 * own_count, hidden), column),
            (up_act, (2 * own_count, hidden), column),
        ],
        16 * nt * matrix_flops,
        [pltpu.VMEM((2 * width, 2 * own_count), BF)],
    )
    grad_b_up = grad_b_up[0]
    lanes = Lanes(2, 2, 1)
    count = 4 if is_ring() else 1
    block_rows = width // count
    hidden_pieces = [
        [
            lax.dynamic_slice_in_dim(
                grad_hidden_w, (t ^ k_t) * width + ((f + k_f) & (count - 1)) * block_rows, block_rows, 0
            )
            for k_t in range(4)
        ]
        for k_f in range(count)
    ]
    hidden_sum = reduce_grid(lanes, hidden_pieces)

    def pin(value, at):
        if lanes.ended and at is not None:
            value, _ = lax.optimization_barrier((value, lanes.ended[at]))
        return value

    own = pin(own, PINS[0])
    grad_resid, grad_attn, middle_rows = small_run(
        middle_back_kernel,
        [flat_f32, flat_low, cube(4)],
        own,
        swap(other, "ctx", 1),
        resid_mid,
        modulation,
        grad_resid,
        attn_out,
    )
    grad_attn_other = swap(grad_attn, "ctx", 1)
    grad_qkv, grad_b_qkv = run(
        functools.partial(attention_back_kernel, tok_count, half),
        [shape(2 * own_count, 3 * core_width, BF), shape(1, 3 * core_width, F32)],
        2,
        pin(grad_attn, PINS[1]),
        grad_attn_other,
        proj_view,
        qkv_low,
    )
    grad_b_qkv = grad_b_qkv[0]
    lists = [(2, 3), (1, 0)] if is_ring() else [(0,)]
    pieces = [None] * (4 if is_ring() else 1)
    piece_size = shape(width // len(pieces), 4 * half, BF)
    for at, distances in enumerate(lists):
        made = call(
            functools.partial(piece_kernel, half, distances),
            [piece_size] * (4 * len(distances)),
            (
                (attn_own, attn_other),
                (grad_attn, grad_attn_other),
                pin(grad_qkv, PINS[2 + at]),
                attended,
            ),
            4 * nt * matrix_flops // len(lists),
            [pltpu.VMEM((2 * width, 2 * own_count), BF)],
        )
        for i, k_f in enumerate(distances):
            pieces[k_f] = made[4 * i : 4 * i + 4]
    first_sum = reduce_grid(lanes, pieces)
    grad_qkv, _ = lax.optimization_barrier((grad_qkv, pieces[0][0]))
    grad_qkv = pin(grad_qkv, PINS[4])
    own, other = run(features_kernel, two_sums, 3, grad_qkv, qkv_view)
    enter_rows, grad_patch = small_run(
        enter_back_kernel,
        [cube(3), shape(PATCH_ROWS, width, F32)],
        own,
        swap(other, "ctx", 1),
        resid_in,
        modulation,
        grad_resid,
        patches,
    )
    grad_b_patch = jnp.sum(enter_rows[:, 2], axis=0)
    grad_b_proj = jnp.sum(middle_rows[:, 3], axis=0)
    grad_b_down = jnp.sum(top_rows_grad[:, 3], axis=0)

    grad_mod = jnp.concatenate(
        [enter_rows[:, 0:2], middle_rows[:, 2:3], middle_rows[:, 0:2], top_rows_grad[:, 2:3]], axis=1
    )
    grad_final = top_rows_grad[:, 0:2]
    def heads_place(grad_rows):
        rows = grad_rows.transpose(1, 0, 2)
        empty = jnp.zeros_like(rows)
        return jnp.stack(
            [jnp.where(c == 0, rows, empty), jnp.where(c == 0, empty, rows)], axis=2
        ).reshape(-1, width)

    qkv_rows = grad_b_qkv.reshape(nt, 3, half)
    up_rows = heads_place(grad_b_up.reshape(nt, 4, half))
    width_rows = (
        jnp.concatenate(
            [grad_b_patch[None], grad_b_proj[None], grad_b_down[None], grad_patch, grad_head], axis=0
        )
    )
    loss_row = jnp.broadcast_to(loss_part, (1, width))
    payload = jnp.concatenate(
        [
            width_rows[0:1],
            loss_row,
            jnp.zeros((1, width), F32),
            jnp.sum(grad_mod, axis=0),
            heads_place(jnp.stack([qkv_rows[:, 0], qkv_rows[:, 2]], axis=1)),
            width_rows[1:2],
            up_rows,
            width_rows[2:3],
            jnp.sum(grad_final, axis=0),
            width_rows[3:],
        ],
        axis=0,
    )
    steps = []
    payload = sum_slow(payload, ("ctx", "tp", "fsdp"), Pace(lanes, *BIASES), steps)
    chain = Pace(lanes, *CHAIN, [None, None] + steps)
    final_flat = jnp.concatenate(
        [jnp.zeros((img_count, width), F32), grad_final.reshape(img_count, 2 * width)], axis=1
    )
    to_tp = jnp.concatenate(
        [
            grad_mod.reshape(img_count, 6, nt, local_width)
            .transpose(2, 0, 1, 3)
            .reshape(nt, img_count, mod_width),
            final_flat.reshape(img_count, nt, top_cols).transpose(1, 0, 2),
        ],
        axis=-1,
    )
    group_grad = exchange_tp(to_tp, chain).reshape(group_images, -1)
    all_grad = gather_fc(group_grad, chain).reshape(images_all, -1)
    all_mod, all_final = all_grad[:, :mod_width], all_grad[:, mod_width:]
    cond_rows = cond_low.astype(F32)
    grad_w_mod = exact_dot(cond_rows.T, all_mod)
    mod_flat = mod_low.astype(F32).transpose(1, 0, 2).reshape(row_count, mod_width)
    top_rows = top_low.astype(F32)
    grad_cond_act = sum_over(
        exact_dot(all_mod, mod_flat.T) + exact_dot(all_final, top_rows.T), ("tp",), chain
    )
    grad_cond = jax.vjp(jax.nn.silu, cond)[1](grad_cond_act)[0]
    cond_all = gather_fc(grad_cond, chain).transpose(1, 0, 2).reshape(images_all, width)
    grad_b_cond = jnp.sum(cond_all, axis=0)
    cond_padded = jnp.concatenate([cond_all, jnp.zeros((images_all, 2 * width), F32)], axis=1)
    cond_top = lax.dynamic_slice_in_dim(cond_padded, top_cols * t, top_cols, 1)
    top_grad = exact_dot(cond_rows.T, all_final) + exact_dot(t_hidden.astype(F32).T, cond_top)
    grad_hidden = sum_over(exact_dot(cond_top, top_rows.T), ("tp",), chain)
    grad_t_pre = jax.vjp(jax.nn.silu, t_pre)[1](grad_hidden)[0]

    loss_total = payload[1, 0]
    small_sum = lax.dynamic_slice_in_dim(payload[19:], place * row_count, row_count, 1)
    patch_sum, head_sum = small_sum[:PATCH_ROWS], small_sum[PATCH_ROWS:]
    head_grad_sum = head_sum.T

    def from_cores(total):
        low, high = total[:row_count], total[row_count:]
        return jnp.where(c == 0, low, high), swap(jnp.where(c == 0, high, low), "ctx", 1)

    block_sum, output_sum, shard_squares = call(
        functools.partial(shards_kernel, half),
        [
            shape(block_count * row_count, local_width, F32),
            shape(5 * local_width, row_count, F32),
            shape(1, local_width, F32),
        ],
        from_cores(first_sum) + from_cores(hidden_sum) + (grad_w_mod,),
        0,
    )
    embed_sum = exact_dot(one_hot.astype(F32).T, grad_cond) + exact_dot(
        freq_low.astype(F32).T, grad_t_pre
    )
    patch_padded = jnp.concatenate(
        [jnp.zeros((embed_rows, row_count), F32), patch_sum, jnp.zeros((embed_rows, row_count), F32)],
        axis=0,
    )
    patch_start = embed_rows * t + embed_rows - (FREQ + CLASSES)
    embed_sum = embed_sum + lax.dynamic_slice_in_dim(
        patch_padded, jnp.clip(patch_start, 0, embed_rows + PATCH_ROWS), embed_rows, 0
    )

    head_squares = jnp.where(t == 0, jnp.sum(head_grad_sum * head_grad_sum), 0.0)
    shard_squares = (
        jnp.sum(shard_squares)
        + jnp.sum(embed_sum * embed_sum)
        + jnp.sum(top_grad * top_grad)
        + head_squares
    )
    b1_part = jnp.where(t == 0, jnp.sum(grad_t_pre, axis=0), 0.0)
    b1_row = lax.dynamic_update_slice_in_dim(jnp.zeros((width,), F32), b1_part, place * row_count, 0)
    last = jnp.concatenate([b1_row, jnp.broadcast_to(shard_squares, (128,))])
    last = sum_over(last, ("ctx", "tp", "fsdp"))
    bias_sum = jnp.concatenate(
        [payload[0:1], last[None, :width], grad_b_cond[None], payload[3:19]], axis=0
    )
    grad_norm = jnp.sqrt(last[width] + jnp.sum(bias_sum * bias_sum))
    clip_factor = jnp.minimum(1.0, 1.0 / (grad_norm + 1e-06))
    def tall(values):
        return jnp.transpose(values, (1, 0, 2)).reshape(block_count * row_count, local_width)

    upd_block = [
        jnp.transpose(u.reshape(block_count, row_count, local_width), (1, 0, 2))
        for u in adam_blocks(tall(w_block), block_sum, tall(m_block), tall(v_block), clip_factor)
    ]
    upd_output = [
        u.reshape(w_output.shape)
        for u in adam_blocks(
            *[m.reshape(output_sum.shape) if m.ndim == 3 else m for m in (w_output, output_sum, m_output, v_output)],
            clip_factor,
        )
    ]
    upd_top = adam_update(w_top, top_grad, m_top, v_top, clip_factor)
    upd_head = adam_update(w_head, head_grad_sum, m_head, v_head, clip_factor)
    upd_embed = adam_update(w_embed, embed_sum, m_embed, v_embed, clip_factor)
    upd_biases = adam_update(biases, bias_sum, m_biases, v_biases, clip_factor)
    updates = (upd_block, upd_output, upd_top, upd_head, upd_embed, upd_biases)
    return (
        (loss_total, grad_norm)
        + tuple(u[0] for u in updates)
        + tuple(u[1] for u in updates)
        + tuple(u[2] for u in updates)
        + (bias_sum * clip_factor,)
    )


def solution(mesh):
    both = ("fsdp", "ctx")
    weights = (
        P(both, None, "tp"),
        P(None, "tp", both),
        P(both, "tp"),
        P(both, None),
        P("tp", both),
        P(),
    )
    images = (P(both, None, None, None), P(both, None, None, None), P(both), P(both))
    return jax.shard_map(
        on_device,
        mesh=mesh,
        in_specs=images + weights * 3,
        out_specs=(P(), P()) + weights * 3 + (P(),),
        check_vma=False,
    )
```

```python
import functools
import math

import jax
import jax.numpy as jnp
from jax import lax
from jax.experimental import pallas as pl
from jax.experimental.pallas import tpu as pltpu
from jax.sharding import PartitionSpec as P

HEAD_DIM = 64
CLASSES = 1000
FREQ = 256
TIMESTEPS = 1000
ADAM_STEP = 10
PATCH_ROWS = 16
PINS = (None, 1, 3, 4, 7)
CHAIN = (20, 1)

PRECISE = lax.Precision.HIGHEST
BF = jnp.bfloat16
F32 = jnp.float32


def exact_dot(left, right):
    return jnp.dot(left, right, precision=PRECISE)


def mm(left, right):
    return jnp.dot(left, right, preferred_element_type=F32)


def mm_nt(left, right):
    return lax.dot_general(left, right, (((1,), (1,)), ((), ())), preferred_element_type=F32)


def mm_tn(left, right):
    return lax.dot_general(left, right, (((0,), (0,)), ((), ())), preferred_element_type=F32)


def gelu_tanh(values):
    return jax.nn.gelu(values, approximate=True)


def plan(step_ids):
    fraction = (step_ids.astype(F32) / TIMESTEPS + 0.008) / 1.008
    kept_share = jnp.cos(fraction * (math.pi / 2.0)) ** 2
    return (jnp.sqrt(kept_share), jnp.sqrt(1.0 - kept_share))


def patchify(field):
    img_count, chan_count, row_count, col_count = field.shape
    shaped = field.reshape(img_count, chan_count, row_count // 2, 2, col_count // 2, 2)
    shaped = shaped.transpose(0, 2, 4, 1, 3, 5)
    return shaped.reshape(img_count, row_count // 2 * (col_count // 2), chan_count * 4)


def adam_update(weight, gradient, first_mom, second_mom, clip_factor):
    clipped = gradient * clip_factor
    first_new = 0.9 * first_mom + 0.1 * clipped
    second_new = 0.999 * second_mom + 0.001 * clipped * clipped
    corr_first = 1.0 - 0.9**ADAM_STEP
    corr_second = 1.0 - 0.999**ADAM_STEP
    direction = first_new / corr_first / (jnp.sqrt(second_new / corr_second) + 1e-08)
    return (weight - 0.04 * (direction + 0.01 * weight), first_new, second_new)


def swap(value, axis, mask):
    count = lax.axis_size(axis)
    return lax.ppermute(value, axis, [(i, i ^ mask) for i in range(count)])


def pull(value, k):
    count = lax.axis_size("fsdp")
    return lax.ppermute(value, "fsdp", [((i + k) % count, i) for i in range(count)])


def push(value, k):
    count = lax.axis_size("fsdp")
    return lax.ppermute(value, "fsdp", [(i, (i + k) % count) for i in range(count)])


def is_ring():
    return lax.axis_size("fsdp") == 4


def pick(pair, bit, axis=0):
    low = lax.index_in_dim(pair, 0, axis, keepdims=False)
    high = lax.index_in_dim(pair, 1, axis, keepdims=False)
    return jnp.where(bit == 1, high, low)


def ordered(own, other, bit, axis=0):
    return jnp.stack([jnp.where(bit == 0, own, other), jnp.where(bit == 0, other, own)], axis)


def bits(count):
    return [1 << b for b in range(count.bit_length() - 1)]


def by_xor(stack, rank):
    for mask in (1, 2):
        other = jnp.stack([stack[i ^ mask] for i in range(4)])
        stack = jnp.where(rank & mask == mask, other, stack)
    return stack


def free(value):
    return value


def sum_over(value, axes, pace=free):
    for axis in axes:
        count = lax.axis_size(axis)
        if count == 2:
            value = value + swap(pace(value), axis, 1)
        elif count == 4:
            sent = pace(value)
            one, two, three = [swap(sent, axis, k) for k in (1, 2, 3)]
            value = (value + one) + (two + three)
        else:
            value = lax.psum(value, axis)
    return value


def roll_lead(stack, steps):
    for mask in (1, 2):
        moved = jnp.stack([stack[(i + mask) % 4] for i in range(4)])
        stack = jnp.where(steps & mask == mask, moved, stack)
    return stack


def scatter_fc(blocks, pace=free):
    if not is_ring():
        return lax.psum_scatter(blocks, ("fsdp", "ctx"), scatter_dimension=0, tiled=False)
    f, c = lax.axis_index("fsdp"), lax.axis_index("ctx")
    held = blocks.reshape((4, 2) + blocks.shape[1:])
    held = pick(held, c, 1) + swap(pace(pick(held, 1 - c, 1)), "ctx", 1)
    held = pace(roll_lead(held, f))
    return (held[0] + push(held[2], 2)) + (push(held[1], 1) + push(held[3], 3))


def gather_fc(value, pace=free):
    if not is_ring():
        return lax.all_gather(value, ("fsdp", "ctx"), axis=0, tiled=False)
    f, c = lax.axis_index("fsdp"), lax.axis_index("ctx")
    sent = pace(value)
    held = jnp.stack([value] + [pull(sent, k) for k in (1, 2, 3)])
    held = roll_lead(held, (4 - f) & 3)
    held = ordered(held, swap(pace(held), "ctx", 1), c, 1)
    return held.reshape((8,) + value.shape)


def exchange_tp(blocks, pace=free):
    t = lax.axis_index("tp")
    mine = pace(by_xor(blocks, t))
    got = jnp.stack([mine[0]] + [swap(mine[k], "tp", k) for k in (1, 2, 3)])
    return by_xor(got, t)


def gather_and_sum(to_tp, shared, split, pace):
    f, c, t = lax.axis_index("fsdp"), lax.axis_index("ctx"), lax.axis_index("tp")
    images, wide = to_tp.shape[1:]
    width = shared.shape[1]
    per_image = -(-wide // width)
    padded = jnp.pad(to_tp, ((0, 0), (0, 0), (0, per_image * width - wide)))
    mine = by_xor(padded.reshape(4, images * per_image, width), t)
    kept, sums = images * per_image, shared.shape[0]
    rows = jnp.concatenate([shared, split], axis=0)
    sent = pace(jnp.concatenate([mine.reshape(-1, width), rows], axis=0))
    whole = [sent[i * kept : (i + 1) * kept] for i in range(4)]
    rows = sent[4 * kept :]
    got = [swap(jnp.concatenate([whole[k], rows], axis=0), "tp", k) for k in (1, 2, 3)]
    group = by_xor(jnp.stack([whole[0]] + [g[:kept] for g in got]), t).reshape(-1, width)
    rows = (rows + got[0][kept:]) + (got[1][kept:] + got[2][kept:])

    quarter = width // 4
    shared, split = rows[:sums], rows[sums:]
    blocks = roll_lead(jnp.stack([split[:, i * quarter : (i + 1) * quarter] for i in range(4)]), f)
    same = jnp.concatenate([group, shared], axis=0).reshape(-1, quarter)
    count = same.shape[0]
    sent = pace(jnp.concatenate([same, blocks.reshape(-1, quarter)], axis=0))
    same, blocks = sent[:count], [
        sent[count + i * split.shape[0] : count + (i + 1) * split.shape[0]] for i in range(4)
    ]
    got = [None] + [push(jnp.concatenate([same, blocks[k]], axis=0), k) for k in (1, 2, 3)]
    group_count = 4 * group.shape[0]
    by_sender = jnp.stack([same[:group_count]] + [got[k][:group_count] for k in (3, 2, 1)])
    by_sender = roll_lead(by_sender, (4 - f) & 3)
    shared = same[group_count:]
    shared = (shared + got[2][group_count:count]) + (got[1][group_count:count] + got[3][group_count:count])
    split = (blocks[0] + got[2][count:]) + (got[1][count:] + got[3][count:])

    half = quarter // 2
    low, high = split[:, :half], split[:, half:]
    other_half = jnp.where(c == 0, high, low)
    shared_half = shared.reshape(-1, half)
    sent = pace(
        jnp.concatenate([by_sender.reshape(-1, half), shared_half, other_half], axis=0)
    )
    got = swap(sent, "ctx", 1)
    count = by_sender.size // half
    group = ordered(
        sent[:count].reshape(4, -1), got[:count].reshape(4, -1), c, 1
    ).reshape(-1, per_image * width)[:, :wide]
    shared = (shared_half + got[count : count + shared_half.shape[0]]).reshape(-1, width)
    split = jnp.where(c == 0, low, high) + got[count + shared_half.shape[0] :]
    return group, shared, split


class Lane:
    def __init__(self, depth):
        self.depth = depth
        self.ended = []

    def __call__(self, value, move):
        if len(self.ended) >= self.depth:
            value, _ = lax.optimization_barrier((value, self.ended[-self.depth]))
        moved = move(value)
        self.ended.append(moved)
        return moved


class Pace:
    def __init__(self, lanes, first, step, others=()):
        self.ended = list(lanes.ended)
        self.next, self.step = first, step
        self.others = list(others)

    def __call__(self, value):
        at = min(self.next, len(self.ended) - 1)
        if at >= 0:
            value, _ = lax.optimization_barrier((value, self.ended[at]))
        self.next += self.step
        other = self.others.pop(0) if self.others else None
        if other is not None:
            value, _ = lax.optimization_barrier((value, other))
        return value


class Lanes:
    def __init__(self, x, y, z):
        self.ended = []
        self.lane_x, self.lane_y, self.lane_z = Lane(x), Lane(y), Lane(z)

    def note(self, moved):
        self.ended.append(moved)
        return moved

    def x(self, value):
        return self.note(self.lane_x(value, lambda v: swap(v, "tp", 1)))

    def y(self, value):
        return self.note(self.lane_y(value, lambda v: swap(v, "tp", 2)))

    def pull(self, value, k):
        return self.note(self.lane_z(value, lambda v: pull(v, k)))

    def push(self, value, k):
        return self.note(self.lane_z(value, lambda v: push(v, k)))


def add(left, right):
    return left.astype(F32) + right.astype(F32)


def add_low(left, right):
    return add(left, right).astype(BF)


def reduce_grid(lanes, main):
    if not is_ring():
        parts = main[0]
        along_x = swap(parts[1], "tp", 1)
        along_y = swap(add_low(parts[2], swap(parts[3], "tp", 1)), "tp", 2)
        both = add_low(add(parts[0], along_x), along_y)
        return lax.psum_scatter(both, "fsdp", scatter_dimension=0, tiled=True).astype(F32)
    far_2, far_1 = lanes.y(main[2][3]), None
    far_3 = lanes.x(main[3][3])
    y_2 = lanes.y(main[2][2])
    x_2 = lanes.x(add_low(main[2][1], far_2))
    far_1 = lanes.y(main[1][3])
    x_3 = lanes.x(main[3][1])
    y_3 = lanes.y(add_low(main[3][2], far_3))
    sum_2 = lanes.push(add_low(add(main[2][0], x_2), y_2), 1)
    y_1 = lanes.y(main[1][2])
    x_1 = lanes.x(add_low(main[1][1], far_1))
    far_0 = lanes.x(main[0][3])
    sum_3 = lanes.push(add_low(add(main[3][0], x_3), y_3), 3)
    x_0 = lanes.x(main[0][1])
    sum_1 = add(add(add(main[1][0], x_1), y_1), sum_2).astype(BF)
    sum_1 = lanes.push(sum_1, 1)
    y_0 = lanes.y(add_low(main[0][2], far_0))
    return add(add(add(main[0][0], x_0), y_0), sum_3) + sum_1.astype(F32)


def rows_of(table, start, count):
    pad = jnp.zeros((count,) + table.shape[1:], table.dtype)
    padded = jnp.concatenate([pad, table, pad], axis=0)
    return lax.dynamic_slice_in_dim(padded, jnp.clip(start + count, 0, table.shape[0] + count), count, 0)


class View:
    def __init__(self, array, width, index):
        self.array, self.width, self.index = array, width, index


def whole_block(dims):
    return pl.BlockSpec(dims, lambda i: (0,) * len(dims), pipeline_mode=pl.Buffered(1))


def call(body, outs, args, flops, scratch=()):
    flat, tree = jax.tree.flatten(args)
    arrays, specs, held = [], [], 0
    for leaf in flat:
        if isinstance(leaf, View):
            dims = (leaf.array.shape[0], leaf.width)
            at = leaf.index
            specs.append(
                pl.BlockSpec(dims, lambda i, at=at: (0, at), pipeline_mode=pl.Buffered(1))
            )
            arrays.append(leaf.array)
        else:
            dims = leaf.shape
            specs.append(whole_block(dims))
            arrays.append(leaf)
        held += math.prod(dims) * arrays[-1].dtype.itemsize
    held += sum(o.size * o.dtype.itemsize for o in outs)
    room = 2 * held + sum(4 * math.prod(a.shape) for a in scratch) + 8 * 1024 * 1024

    def kernel(*refs):
        body(*jax.tree.unflatten(tree, refs[: len(flat)]), *refs[len(flat) :])

    return pl.pallas_call(
        kernel,
        grid=(1,),
        out_shape=outs,
        in_specs=specs,
        out_specs=[whole_block(o.shape) for o in outs],
        scratch_shapes=list(scratch),
        compiler_params=pltpu.CompilerParams(vmem_limit_bytes=56 * 1024 * 1024),
        cost_estimate=pl.CostEstimate(flops=flops, bytes_accessed=held, transcendentals=0),
    )(*arrays)


def shape(rows, cols, dtype):
    return jax.ShapeDtypeStruct((rows, cols), dtype)


def down_rows(parts, k_t, start, stop):
    return jnp.concatenate([row[k_t][:, start:stop] for row in parts], axis=0)


def head_masks(half):
    at = lax.broadcasted_iota(jnp.int32, (1, half), 1) // HEAD_DIM
    return [at == h for h in range(half // HEAD_DIM)]


def softmax_rows(scores):
    top = jnp.max(scores, axis=-1, keepdims=True)
    grown = jnp.exp(scores - top)
    return grown / jnp.sum(grown, axis=-1, keepdims=True)


def merged(masks, values):
    total = values[-1]
    for mask, value in zip(masks[:-1], values[:-1]):
        total = jnp.where(mask, value, total)
    return total


def split_t(ref):
    width = ref.shape[0] // 4
    return [[ref.at[i * width : (i + 1) * width] for i in range(4)]]


def qkv_kernel(tok_count, half, own_ref, other_ref, weight_ref, bias_ref, qkv_ref, attended_ref):
    parts = split_t(weight_ref)
    rows = own_ref.shape[0]
    masks = head_masks(half)
    for i, ref in enumerate((own_ref, other_ref)):
        left = ref[...]
        for k_t in range(4):
            cols = slice(k_t * 3 * half, (k_t + 1) * 3 * half)
            weight = down_rows(parts, k_t, 0, 3 * half)
            qkv_ref[i * rows : (i + 1) * rows, cols] = (
                mm(left, weight) + bias_ref[:, cols]
            ).astype(BF)
    for k_t in range(4):
        at = k_t * 3 * half
        for row in range(0, 2 * rows, tok_count):
            here = slice(row, row + tok_count)
            query = qkv_ref[here, at : at + half]
            key = qkv_ref[here, at + half : at + 2 * half]
            value = qkv_ref[here, at + 2 * half : at + 3 * half]
            got = []
            for mask in masks:
                masked = jnp.where(mask, query, jnp.zeros_like(query))
                probs = softmax_rows(mm_nt(masked, key) * 0.125).astype(BF)
                got.append(mm(probs, value))
            attended_ref[here, k_t * half : (k_t + 1) * half] = merged(masks, got).astype(BF)


def attention_back_kernel(
    tok_count, half, own_ref, other_ref, weight_ref, qkv_ref, out_ref, sum_ref
):
    parts = split_t(weight_ref)
    rows = own_ref.shape[0]
    masks = head_masks(half)
    left = [ref[...] for ref in (own_ref, other_ref)]
    for k_t in range(4):
        at = k_t * 3 * half
        weight = down_rows(parts, k_t, 0, half)
        for i in range(2):
            grad_half = mm(left[i], weight).astype(BF)
            for row in range(0, rows, tok_count):
                here = slice(i * rows + row, i * rows + row + tok_count)
                grad = grad_half[row : row + tok_count]
                query = qkv_ref[here, at : at + half]
                key = qkv_ref[here, at + half : at + 2 * half]
                value = qkv_ref[here, at + 2 * half : at + 3 * half]
                grad_q, grad_k, grad_v = [], [], []
                for mask in masks:
                    zero = jnp.zeros_like(query)
                    probs = softmax_rows(mm_nt(jnp.where(mask, query, zero), key) * 0.125)
                    grad_p = mm_nt(jnp.where(mask, grad, zero), value)
                    grad_s = (
                        probs * (grad_p - jnp.sum(grad_p * probs, axis=-1, keepdims=True))
                    ).astype(BF)
                    grad_q.append(mm(grad_s, key))
                    grad_k.append(mm_tn(grad_s, query))
                    grad_v.append(mm_tn(probs.astype(BF), grad))
                out_ref[here, at : at + half] = (merged(masks, grad_q) * 0.125).astype(BF)
                out_ref[here, at + half : at + 2 * half] = (merged(masks, grad_k) * 0.125).astype(BF)
                out_ref[here, at + 2 * half : at + 3 * half] = merged(masks, grad_v).astype(BF)
        cols = slice(at, at + 3 * half)
        sum_ref[:, cols] = jnp.sum(out_ref[:, cols].astype(F32), axis=0, keepdims=True)


def features_kernel(left_ref, weight_ref, own_ref, other_ref):
    parts = split_t(weight_ref)
    rows, size = own_ref.shape
    block = size // 4
    for k in range(4):
        cols = slice(k * block, (k + 1) * block)
        weight = jnp.concatenate([p[cols, :] for p in parts[0]], axis=1)
        own_ref[:, cols] = mm_nt(left_ref[:rows], weight)
        other_ref[:, cols] = mm_nt(left_ref[rows:], weight)


def gelu_slope(values):
    scale = math.sqrt(2.0 / math.pi)
    bent = jnp.tanh(scale * (values + 0.044715 * (values * values * values)))
    inner = scale * (1.0 + 3.0 * 0.044715 * (values * values))
    return 0.5 * (1.0 + bent) + 0.5 * values * (1.0 - bent * bent) * inner


def mlp_kernel(own_ref, other_ref, up_ref, down_ref, bias_ref, pre_ref, act_ref, own_out, other_out):
    rows = own_ref.shape[0]

    @pl.when(pl.program_id(0) == 0)
    def _():
        own_out[...] = jnp.zeros_like(own_out)
        other_out[...] = jnp.zeros_like(other_out)

    for i, (ref, out) in enumerate(((own_ref, own_out), (other_ref, other_out))):
        here = slice(i * rows, (i + 1) * rows)
        pre = mm(ref[...], up_ref[...]) + bias_ref[...]
        pre_ref[here, :] = pre
        act = gelu_tanh(pre).astype(BF)
        act_ref[here, :] = act
        out[...] += mm_nt(act, down_ref[...])


def mlp_back_kernel(
    own_ref,
    other_ref,
    own_in,
    other_in,
    up_ref,
    down_ref,
    pre_ref,
    act_ref,
    grad_ref,
    sum_ref,
    own_out,
    other_out,
    flipped,
):
    rows, width = own_ref.shape
    size = up_ref.shape[1]

    @pl.when(pl.program_id(0) == 0)
    def _():
        own_out[...] = jnp.zeros_like(own_out)
        other_out[...] = jnp.zeros_like(other_out)
        for i, ref in enumerate((own_in, other_in, own_ref, other_ref)):
            flipped[
                i // 2 * width : (i // 2 + 1) * width, i % 2 * rows : (i % 2 + 1) * rows
            ] = ref[...].T

    total, grads = 0.0, []
    for i, (ref, out) in enumerate(((own_ref, own_out), (other_ref, other_out))):
        here = slice(i * rows, (i + 1) * rows)
        grad = (mm(ref[...], down_ref[...]) * gelu_slope(pre_ref[here, :])).astype(BF)
        total = total + col_sum(grad.astype(F32))
        out[...] += mm_nt(grad, up_ref[...])
        grads.append(grad)
    sum_ref[...] = total
    grad_ref[:, :size] = mm(flipped[:width, :], jnp.concatenate(grads, axis=0)).astype(BF)
    grad_ref[:, size:] = mm(flipped[width:, :], act_ref[...]).astype(BF)


def over_hidden(kernel, counts, outs, args, flops, scratch=()):
    def spec(block, index):
        return pl.BlockSpec(block, index)

    return pl.pallas_call(
        kernel,
        grid=(counts,),
        out_shape=[o[0] for o in outs],
        in_specs=[spec(a[1], a[2]) for a in args],
        out_specs=[spec(o[1], o[2]) for o in outs],
        scratch_shapes=list(scratch),
        compiler_params=pltpu.CompilerParams(vmem_limit_bytes=56 * 1024 * 1024),
        cost_estimate=pl.CostEstimate(
            flops=flops, bytes_accessed=32 * 1024 * 1024, transcendentals=0
        ),
    )(*[a[0] for a in args])


def piece_kernel(half, places, attn, grad_attn, grad_qkv_ref, attended_ref, *refs):
    outs, flipped = refs[:-1], refs[-1]
    t = lax.axis_index("tp")
    size = outs[0].shape[0]
    width = attn[0].shape[1]
    tokens = attn[0].shape[0]
    for i, pair in enumerate((attn, grad_attn)):
        for j, ref in enumerate(pair):
            flipped[i * width : (i + 1) * width, j * tokens : (j + 1) * tokens] = ref[...].T
    for i, k_f in enumerate(places):
        if size == width:
            start = 0
        else:
            start = pl.multiple_of(((lax.axis_index("fsdp") + k_f) & 3) * size, size)
        left = [flipped[pl.ds(i * width + start, size), :] for i in range(2)]
        for k_t in range(4):
            out = outs[i * 4 + k_t]
            place = t ^ k_t

            def cols(count):
                return pl.ds(pl.multiple_of(place * count, count), count)

            out[:, : 3 * half] = mm(left[0], grad_qkv_ref[:, cols(3 * half)]).astype(BF)
            out[:, 3 * half :] = mm(left[1], attended_ref[:, cols(half)]).astype(BF)


def normed(values):
    center = values - jnp.mean(values, axis=-1, keepdims=True)
    spread = jnp.mean(center * center, axis=-1, keepdims=True)
    inverse = lax.rsqrt(spread + 1e-06)
    return center * inverse, inverse


def norm_back(grad, norm, inverse):
    mean = jnp.mean(grad, axis=-1, keepdims=True)
    slope = jnp.mean(grad * norm, axis=-1, keepdims=True)
    return inverse * (grad - mean - norm * slope)


def col_sum(values):
    return jnp.sum(values, axis=0, keepdims=True)


def enter_kernel(images, patch_ref, w_ref, place_ref, mod_ref, resid_ref, attn_ref):
    count = patch_ref.shape[0] // images
    for i in range(images):
        here = slice(i * count, (i + 1) * count)
        resid = mm(patch_ref[here], w_ref[...]) + place_ref[...]
        resid_ref[here] = resid
        mod = mod_ref[i]
        attn_ref[here] = (normed(resid)[0] * (1.0 + mod[1:2]) + mod[0:1]).astype(BF)


def middle_kernel(images, own_ref, got_ref, bias_ref, resid_ref, mod_ref, out_ref, mid_ref, mlp_ref):
    count = own_ref.shape[0] // images
    for i in range(images):
        here = slice(i * count, (i + 1) * count)
        mod = mod_ref[i]
        out = own_ref[here] + got_ref[here] + bias_ref[...]
        out_ref[here] = out
        mid = resid_ref[here] + mod[2:3] * out
        mid_ref[here] = mid
        mlp_ref[here] = (normed(mid)[0] * (1.0 + mod[4:5]) + mod[3:4]).astype(BF)


def top_kernel(
    images,
    own_ref,
    got_ref,
    bias_ref,
    mid_ref,
    mod_ref,
    final_ref,
    head_ref,
    target_ref,
    resid_ref,
    mlp_ref,
    rows_ref,
    head_grad_ref,
    loss_ref,
    images_all,
):
    count = own_ref.shape[0] // images
    loss, head_grad = 0.0, 0.0
    for i in range(images):
        here = slice(i * count, (i + 1) * count)
        gate = mod_ref[i][5:6]
        shift, scale = final_ref[i][0:1], final_ref[i][1:2]
        out = own_ref[here] + got_ref[here] + bias_ref[...]
        norm, inverse = normed(mid_ref[here] + gate * out)
        head_in = (norm * (1.0 + scale) + shift).astype(BF)
        error = mm_nt(head_in, head_ref[...]) - target_ref[here]
        loss = loss + jnp.sum(col_sum(error * error), axis=1, keepdims=True) / images_all
        grad_pred = (2.0 / images_all * error).astype(BF)
        grad = mm(grad_pred, head_ref[...])
        head_grad = head_grad + mm_tn(grad_pred, head_in)
        resid = norm_back(grad * (1.0 + scale), norm, inverse)
        resid_ref[here] = resid
        mlp = (resid * gate).astype(BF)
        mlp_ref[here] = mlp
        rows_ref[i] = jnp.concatenate(
            [col_sum(grad), col_sum(grad * norm), col_sum(resid * out), col_sum(mlp.astype(F32))], axis=0
        )
    head_grad_ref[...] = head_grad
    loss_ref[...] = jnp.broadcast_to(loss, loss_ref.shape)


def middle_back_kernel(
    images, own_ref, got_ref, mid_ref, mod_ref, resid_ref, out_ref, new_ref, attn_ref, rows_ref
):
    count = own_ref.shape[0] // images
    for i in range(images):
        here = slice(i * count, (i + 1) * count)
        mod = mod_ref[i]
        grad = own_ref[here] + got_ref[here]
        norm, inverse = normed(mid_ref[here])
        resid = resid_ref[here] + norm_back(grad * (1.0 + mod[4:5]), norm, inverse)
        new_ref[here] = resid
        attn = (resid * mod[2:3]).astype(BF)
        attn_ref[here] = attn
        rows_ref[i] = jnp.concatenate(
            [
                col_sum(grad),
                col_sum(grad * norm),
                col_sum(resid * out_ref[here]),
                col_sum(attn.astype(F32)),
            ],
            axis=0,
        )


def enter_back_kernel(
    images, own_ref, got_ref, in_ref, mod_ref, resid_ref, patch_ref, rows_ref, patch_grad_ref
):
    count = own_ref.shape[0] // images
    patch_grad = 0.0
    for i in range(images):
        here = slice(i * count, (i + 1) * count)
        grad = own_ref[here] + got_ref[here]
        norm, inverse = normed(in_ref[here])
        resid = resid_ref[here] + norm_back(grad * (1.0 + mod_ref[i][1:2]), norm, inverse)
        low = resid.astype(BF)
        rows_ref[i] = jnp.concatenate(
            [col_sum(grad), col_sum(grad * norm), col_sum(low.astype(F32))], axis=0
        )
        patch_grad = patch_grad + mm_tn(patch_ref[here], low)
    patch_grad_ref[...] = patch_grad


def adam_kernel(clip_ref, w_ref, g_ref, m_ref, v_ref, new_ref, first_ref, second_ref):
    new_ref[...], first_ref[...], second_ref[...] = adam_update(
        w_ref[...], g_ref[...], m_ref[...], v_ref[...], clip_ref[0, 0]
    )


def adam_blocks(weight, gradient, first_mom, second_mom, clip_factor):
    rows, cols = weight.shape
    count = 4 if rows % 32 == 0 else 1
    block = pl.BlockSpec((rows // count, cols), lambda i: (i, 0))
    return pl.pallas_call(
        adam_kernel,
        grid=(count,),
        out_shape=[jax.ShapeDtypeStruct(weight.shape, F32)] * 3,
        in_specs=[pl.BlockSpec(memory_space=pltpu.SMEM)] + [block] * 4,
        out_specs=[block] * 3,
        compiler_params=pltpu.CompilerParams(vmem_limit_bytes=32 * 1024 * 1024),
        cost_estimate=pl.CostEstimate(flops=0, bytes_accessed=28 * weight.size, transcendentals=0),
    )(clip_factor.reshape(1, 1), weight, gradient, first_mom, second_mom)


def shards_kernel(half, first_ref, first_got, down_ref, down_got, mod_ref, block_ref, output_ref, square_ref):
    c = lax.axis_index("ctx")
    count = first_ref.shape[0]
    total = 0.0

    def joined(own_ref, got_ref, i):
        own, got = own_ref[:, i * half : (i + 1) * half], got_ref[:, i * half : (i + 1) * half]
        both = jnp.concatenate([jnp.where(c == 0, own, got), jnp.where(c == 0, got, own)], axis=1)
        return both, col_sum(both * both)

    for i in range(7):
        both, squares = joined(first_ref, first_got, i) if i < 3 else joined(down_ref, down_got, i - 3)
        block_ref[i * count : (i + 1) * count, :] = both
        total = total + squares
    for i in range(5):
        both, squares = joined(first_ref, first_got, 3) if i == 0 else joined(down_ref, down_got, i + 3)
        output_ref[i * 2 * half : (i + 1) * 2 * half, :] = both.T
        total = total + squares
    for i in range(6):
        part = mod_ref[:, i * 2 * half : (i + 1) * 2 * half]
        block_ref[(7 + i) * count : (8 + i) * count, :] = part
        total = total + col_sum(part * part)
    square_ref[...] = total


def on_device(
    latents,
    noise_sample,
    timesteps,
    class_labels,
    w_block,
    w_output,
    w_top,
    w_head,
    w_embed,
    biases,
    m_block,
    m_output,
    m_top,
    m_head,
    m_embed,
    m_biases,
    v_block,
    v_output,
    v_top,
    v_head,
    v_embed,
    v_biases,
):
    f, c, t = lax.axis_index("fsdp"), lax.axis_index("ctx"), lax.axis_index("tp")
    nt = lax.axis_size("tp")
    places = lax.axis_size("fsdp") * lax.axis_size("ctx")
    place = f * lax.axis_size("ctx") + c
    row_count, block_count, local_width = w_block.shape
    half = local_width // 2
    width = local_width * nt
    group_images = latents.shape[0]
    images_all = group_images * places
    img_count = group_images // nt
    grid_side = latents.shape[3] // 2
    tok_count = latents.shape[2] // 2 * grid_side
    embed_rows = w_embed.shape[0]
    top_cols = w_top.shape[1]

    block_low = jnp.transpose(w_block, (1, 0, 2)).astype(BF)
    output_low = jnp.transpose(w_output, (0, 2, 1)).astype(BF)
    top_low = w_top.astype(BF)
    embed_low = w_embed.astype(BF)

    def core_half(blocks):
        low, high = blocks[:, :, :half], blocks[:, :, half:]
        return jnp.where(c == 0, low, high), jnp.where(c == 0, high, low)

    def beside(blocks):
        return jnp.concatenate([blocks[i] for i in range(blocks.shape[0])], axis=1)

    mixed = jnp.concatenate(
        [block_low[0:3], output_low[0:1], block_low[3:7], output_low[1:5]], axis=0
    )
    mine, other = core_half(mixed)
    mine, other = beside(mine), swap(beside(other), "ctx", 1)
    shards = jnp.concatenate(
        [jnp.where(c == 0, mine, other), jnp.where(c == 0, other, mine)], axis=0
    )
    full = lax.all_gather(shards, ("tp", "fsdp"), axis=0, tiled=True)
    pace = free

    patch_rows = rows_of(embed_low, FREQ + CLASSES - embed_rows * t, PATCH_ROWS)
    ids = jnp.concatenate([timesteps, class_labels]).astype(F32)
    ids = jnp.concatenate([ids, jnp.zeros((row_count - 2 * group_images % row_count,), F32)])[None]
    ids = ids.reshape(-1, row_count)
    small = jnp.concatenate([ids, patch_rows.astype(F32), w_head.T.astype(BF).astype(F32)], axis=0)
    small = gather_fc(small, pace)
    ids_all = small[:, : ids.shape[0]].reshape(places, -1)
    steps_all = ids_all[:, :group_images].reshape(images_all)
    labels_all = ids_all[:, group_images : 2 * group_images].reshape(images_all).astype(jnp.int32)
    small = small[:, ids.shape[0] :].transpose(1, 0, 2).reshape(2 * PATCH_ROWS, width)
    patch_part, w_head_t = small[:PATCH_ROWS], small[PATCH_ROWS:].astype(BF)
    embed_at = embed_rows * t + jnp.arange(embed_rows, dtype=jnp.int32)
    half_freq = FREQ // 2
    rates = jnp.exp(-math.log(10000.0) * (embed_at % half_freq).astype(F32) / half_freq)
    angles = steps_all[:, None] * rates[None, :]
    waves = jnp.where(embed_at[None, :] < half_freq, jnp.cos(angles), jnp.sin(angles))
    freq_low = jnp.where(embed_at[None, :] < FREQ, waves, 0.0).astype(BF)
    one_hot = (labels_all[:, None] + FREQ == embed_at[None, :]).astype(BF)
    own_cols = lambda row: lax.dynamic_slice_in_dim(row, place * row_count, row_count, 0)
    over_tp = jnp.concatenate([mm(freq_low, embed_low), patch_part.reshape(-1, row_count)], axis=0)
    over_tp = sum_over(over_tp, ("tp",), pace)
    t_pre = over_tp[:images_all] + own_cols(biases[1])
    w_patch = over_tp[images_all:].reshape(PATCH_ROWS, width).astype(BF)
    t_hidden = jax.nn.silu(t_pre).astype(BF)
    table_part = mm(one_hot, embed_low)
    top_at = top_cols * t + jnp.arange(top_cols, dtype=jnp.int32)
    cond_cols = mm(t_hidden, top_low)
    cond_cols = jnp.where(top_at[None, :] < width, cond_cols, 0.0)
    cond_wide = jnp.concatenate(
        [jnp.zeros((images_all, width), F32), cond_cols, jnp.zeros((images_all, width), F32)], axis=1
    )
    cond_wide = lax.dynamic_slice_in_dim(
        cond_wide, jnp.clip(width - top_cols * t, 0, width + top_cols), width, 1
    )
    cond_blocks = cond_wide.reshape(images_all, places, row_count).transpose(1, 0, 2)
    cond = sum_over(scatter_fc(cond_blocks, pace) + table_part, ("tp",), pace) + own_cols(biases[2])
    cond_low = jax.nn.silu(cond).astype(BF)
    mod_low = block_low[7:13]
    mod_cols = jnp.concatenate([mm(cond_low, mod_low[j]) for j in range(6)], axis=1)
    final_cols = jnp.where(top_at[None, :] < width, 0.0, mm(cond_low, top_low))
    all_cols = jnp.concatenate([mod_cols, final_cols], axis=1)
    group_cols = scatter_fc(all_cols.reshape(places, group_images, all_cols.shape[1]), pace)
    own_parts = exchange_tp(group_cols.reshape(nt, img_count, -1), pace)
    mod_width = 6 * local_width
    modulation = (
        own_parts[:, :, :mod_width]
        .reshape(nt, img_count, 6, local_width)
        .transpose(1, 2, 0, 3)
        .reshape(img_count, 6, width)
    ) + biases[3:9][None]
    final_mod = own_parts[:, :, mod_width:].transpose(1, 0, 2).reshape(img_count, 3 * width)
    final_mod = final_mod[:, width:].reshape(img_count, 2, width) + biases[17:19][None]
    shift_f, scale_f = final_mod[:, 0], final_mod[:, 1]

    def own_images(values):
        return lax.dynamic_slice_in_dim(values, t * img_count, img_count, 0)

    latent_vals = own_images(latents).astype(F32)
    noise_vals = own_images(noise_sample).astype(F32)
    keep_rate, drop_rate = plan(own_images(timesteps))
    noisy = (
        keep_rate[:, None, None, None] * latent_vals + drop_rate[:, None, None, None] * noise_vals
    )
    patches = patchify(noisy).astype(BF)
    target = patchify(noise_vals)

    quarter = width // 4
    pos_rates = jnp.exp(-math.log(10000.0) * jnp.arange(quarter, dtype=F32) / quarter)
    side_angle = jnp.arange(grid_side, dtype=F32)[:, None] * pos_rates[None, :]
    side = jnp.concatenate([jnp.sin(side_angle), jnp.cos(side_angle)], axis=-1)
    rows_side = jnp.broadcast_to(side[:, None, :], (tok_count // grid_side, grid_side, 2 * quarter))
    cols_side = jnp.broadcast_to(side[None, :, :], (tok_count // grid_side, grid_side, 2 * quarter))
    positions = jnp.concatenate([rows_side, cols_side], axis=-1).reshape(tok_count, width)

    bias_width = jnp.stack([biases[0], biases[11], biases[16]])

    def heads_bias(rows):
        shaped = rows.reshape(-1, nt, 2, half)
        return jnp.where(c == 0, shaped[:, :, 0], shaped[:, :, 1]).transpose(1, 0, 2)

    bias_qv = heads_bias(biases[9:11])
    bias_qkv = jnp.stack([bias_qv[:, 0], jnp.zeros_like(bias_qv[:, 0]), bias_qv[:, 1]], axis=1).reshape(-1)
    bias_up = heads_bias(biases[12:16]).reshape(-1)
    qkv_view, proj_view = View(full, 3 * half, 0), View(full, half, 3)

    own_count = img_count * tok_count
    core_width = nt * half
    matrix_flops = 4 * own_count * width * half

    two_sums = [shape(own_count, width, F32)] * 2

    def run(body, outs, blocks, *args):
        return call(body, outs, args, blocks * nt * matrix_flops)

    def small_run(body, outs, *args):
        return call(functools.partial(body, img_count), outs, args, 0)

    def cube(rows):
        return jax.ShapeDtypeStruct((img_count, rows, width), F32)

    flat_f32, flat_low = shape(own_count, width, F32), shape(own_count, width, BF)

    patches = patches.reshape(own_count, PATCH_ROWS)
    resid_in, attn_own = small_run(
        enter_kernel,
        [flat_f32, flat_low],
        patches,
        w_patch,
        positions + bias_width[0],
        modulation,
    )
    attn_other = swap(attn_own, "ctx", 1)
    qkv_low, attended = run(
        functools.partial(qkv_kernel, tok_count, half),
        [shape(2 * own_count, 3 * core_width, BF), shape(2 * own_count, core_width, BF)],
        4,
        attn_own,
        attn_other,
        qkv_view,
        bias_qkv[None],
    )
    own, other = run(features_kernel, two_sums, 1, attended, proj_view)
    attn_out, resid_mid, mlp_own = small_run(
        middle_kernel,
        [flat_f32, flat_f32, flat_low],
        own,
        swap(other, "ctx", 1),
        bias_width[1:2],
        resid_in,
        modulation,
    )
    mlp_other = swap(mlp_own, "ctx", 1)
    hidden = 4 * half
    fixed = lambda i: (0, 0)
    column = lambda i: (0, i)
    wide_rows = (own_count, width)
    up_pre, up_act, own, other = over_hidden(
        mlp_kernel,
        nt,
        [
            (shape(2 * own_count, nt * hidden, F32), (2 * own_count, hidden), column),
            (shape(2 * own_count, nt * hidden, BF), (2 * own_count, hidden), column),
            (flat_f32, wide_rows, fixed),
            (flat_f32, wide_rows, fixed),
        ],
        [
            (mlp_own, wide_rows, fixed),
            (mlp_other, wide_rows, fixed),
            (full, (width, hidden), lambda i: (i, 1)),
            (full, (width, hidden), lambda i: (i, 2)),
            (bias_up[None], (1, hidden), column),
        ],
        8 * nt * matrix_flops,
    )
    grad_resid, grad_mlp, top_rows_grad, grad_head, loss_part = small_run(
        functools.partial(top_kernel, images_all=images_all),
        [flat_f32, flat_low, cube(4), shape(PATCH_ROWS, width, F32), shape(1, 128, F32)],
        own,
        swap(other, "ctx", 1),
        bias_width[2:3],
        resid_mid,
        modulation,
        final_mod,
        w_head_t,
        target.reshape(own_count, PATCH_ROWS),
    )
    loss_part = loss_part[0, 0]

    grad_mlp_other = swap(grad_mlp, "ctx", 1)
    grad_hidden_w, grad_b_up, own, other = over_hidden(
        mlp_back_kernel,
        nt,
        [
            (shape(nt * width, 2 * hidden, BF), (width, 2 * hidden), lambda i: (i, 0)),
            (shape(1, nt * hidden, F32), (1, hidden), column),
            (flat_f32, wide_rows, fixed),
            (flat_f32, wide_rows, fixed),
        ],
        [
            (grad_mlp, wide_rows, fixed),
            (grad_mlp_other, wide_rows, fixed),
            (mlp_own, wide_rows, fixed),
            (mlp_other, wide_rows, fixed),
            (full, (width, hidden), lambda i: (i, 1)),
            (full, (width, hidden), lambda i: (i, 2)),
            (up_pre, (2 * own_count, hidden), column),
            (up_act, (2 * own_count, hidden), column),
        ],
        16 * nt * matrix_flops,
        [pltpu.VMEM((2 * width, 2 * own_count), BF)],
    )
    grad_b_up = grad_b_up[0]
    lanes = Lanes(2, 2, 1)
    count = 4 if is_ring() else 1
    block_rows = width // count
    hidden_pieces = [
        [
            lax.dynamic_slice_in_dim(
                grad_hidden_w, (t ^ k_t) * width + ((f + k_f) & (count - 1)) * block_rows, block_rows, 0
            )
            for k_t in range(4)
        ]
        for k_f in range(count)
    ]
    hidden_sum = reduce_grid(lanes, hidden_pieces)

    def pin(value, at):
        if lanes.ended and at is not None:
            value, _ = lax.optimization_barrier((value, lanes.ended[at]))
        return value

    own = pin(own, PINS[0])
    grad_resid, grad_attn, middle_rows = small_run(
        middle_back_kernel,
        [flat_f32, flat_low, cube(4)],
        own,
        swap(other, "ctx", 1),
        resid_mid,
        modulation,
        grad_resid,
        attn_out,
    )
    grad_attn_other = swap(grad_attn, "ctx", 1)
    grad_qkv, grad_b_qkv = run(
        functools.partial(attention_back_kernel, tok_count, half),
        [shape(2 * own_count, 3 * core_width, BF), shape(1, 3 * core_width, F32)],
        2,
        pin(grad_attn, PINS[1]),
        grad_attn_other,
        proj_view,
        qkv_low,
    )
    grad_b_qkv = grad_b_qkv[0]
    lists = [(2, 3), (1, 0)] if is_ring() else [(0,)]
    pieces = [None] * (4 if is_ring() else 1)
    piece_size = shape(width // len(pieces), 4 * half, BF)
    for at, distances in enumerate(lists):
        made = call(
            functools.partial(piece_kernel, half, distances),
            [piece_size] * (4 * len(distances)),
            (
                (attn_own, attn_other),
                (grad_attn, grad_attn_other),
                pin(grad_qkv, PINS[2 + at]),
                attended,
            ),
            4 * nt * matrix_flops // len(lists),
            [pltpu.VMEM((2 * width, 2 * own_count), BF)],
        )
        for i, k_f in enumerate(distances):
            pieces[k_f] = made[4 * i : 4 * i + 4]
    first_sum = reduce_grid(lanes, pieces)
    grad_qkv, _ = lax.optimization_barrier((grad_qkv, pieces[0][0]))
    grad_qkv = pin(grad_qkv, PINS[4])
    own, other = run(features_kernel, two_sums, 3, grad_qkv, qkv_view)
    enter_rows, grad_patch = small_run(
        enter_back_kernel,
        [cube(3), shape(PATCH_ROWS, width, F32)],
        own,
        swap(other, "ctx", 1),
        resid_in,
        modulation,
        grad_resid,
        patches,
    )
    grad_b_patch = jnp.sum(enter_rows[:, 2], axis=0)
    grad_b_proj = jnp.sum(middle_rows[:, 3], axis=0)
    grad_b_down = jnp.sum(top_rows_grad[:, 3], axis=0)

    grad_mod = jnp.concatenate(
        [enter_rows[:, 0:2], middle_rows[:, 2:3], middle_rows[:, 0:2], top_rows_grad[:, 2:3]], axis=1
    )
    grad_final = top_rows_grad[:, 0:2]
    def heads_place(grad_rows):
        rows = grad_rows.transpose(1, 0, 2)
        empty = jnp.zeros_like(rows)
        return jnp.stack(
            [jnp.where(c == 0, rows, empty), jnp.where(c == 0, empty, rows)], axis=2
        ).reshape(-1, width)

    qkv_rows = grad_b_qkv.reshape(nt, 3, half)
    up_rows = heads_place(grad_b_up.reshape(nt, 4, half))
    loss_row = jnp.broadcast_to(loss_part, (1, width))
    shared = jnp.concatenate(
        [
            heads_place(jnp.stack([qkv_rows[:, 0], qkv_rows[:, 2]], axis=1)),
            grad_b_proj[None],
            up_rows,
            grad_b_down[None],
            loss_row,
        ],
        axis=0,
    )
    split = jnp.concatenate([grad_patch, grad_head, grad_b_patch[None]], axis=0)
    chain = Pace(lanes, *CHAIN)
    final_flat = jnp.concatenate(
        [jnp.zeros((img_count, width), F32), grad_final.reshape(img_count, 2 * width)], axis=1
    )
    to_tp = jnp.concatenate(
        [
            grad_mod.reshape(img_count, 6, nt, local_width)
            .transpose(2, 0, 1, 3)
            .reshape(nt, img_count, mod_width),
            final_flat.reshape(img_count, nt, top_cols).transpose(1, 0, 2),
        ],
        axis=-1,
    )
    if is_ring():
        all_grad, shared, split = gather_and_sum(to_tp, shared, split, chain)
    else:
        group_grad = exchange_tp(to_tp).reshape(group_images, -1)
        all_grad = gather_fc(group_grad).reshape(images_all, -1)
        shared = sum_over(shared, ("tp", "fsdp", "ctx"))
        split = split.reshape(split.shape[0], places, row_count).transpose(1, 0, 2)
        split = scatter_fc(sum_over(split, ("tp",)))
    all_mod, all_final = all_grad[:, :mod_width], all_grad[:, mod_width:]
    cond_rows = cond_low.astype(F32)
    grad_w_mod = exact_dot(cond_rows.T, all_mod)
    mod_flat = mod_low.astype(F32).transpose(1, 0, 2).reshape(row_count, mod_width)
    top_rows = top_low.astype(F32)
    part = exact_dot(all_mod, mod_flat.T) + exact_dot(all_final, top_rows.T)
    sent = chain(jnp.concatenate([part, jnp.sum(all_grad, axis=0).reshape(-1, row_count)], axis=0))
    got = [sent] + [swap(sent, "tp", k) for k in (1, 2, 3)]
    grad_cond_act = (got[0] + got[1])[:images_all] + (got[2] + got[3])[:images_all]
    col_sums = by_xor(jnp.stack([g[images_all:] for g in got]), t).reshape(nt, -1)
    bias_mod = col_sums[:, :mod_width].reshape(nt, 6, local_width).transpose(1, 0, 2).reshape(6, width)
    bias_final = col_sums[:, mod_width:].reshape(-1)[width:].reshape(2, width)
    grad_cond = jax.vjp(jax.nn.silu, cond)[1](grad_cond_act)[0]
    rows_all = gather_fc(jnp.concatenate([grad_cond, split[2 * PATCH_ROWS :]], axis=0), chain)
    rows_all = rows_all.transpose(1, 0, 2).reshape(-1, width)
    cond_all, bias_patch = rows_all[:images_all], rows_all[images_all:]
    grad_b_cond = jnp.sum(cond_all, axis=0)
    cond_padded = jnp.concatenate([cond_all, jnp.zeros((images_all, 2 * width), F32)], axis=1)
    cond_top = lax.dynamic_slice_in_dim(cond_padded, top_cols * t, top_cols, 1)
    top_grad = exact_dot(cond_rows.T, all_final) + exact_dot(t_hidden.astype(F32).T, cond_top)
    grad_hidden = sum_over(exact_dot(cond_top, top_rows.T), ("tp",), chain)
    grad_t_pre = jax.vjp(jax.nn.silu, t_pre)[1](grad_hidden)[0]

    loss_total = shared[8, 0]
    patch_sum, head_sum = split[:PATCH_ROWS], split[PATCH_ROWS : 2 * PATCH_ROWS]
    head_grad_sum = head_sum.T

    def from_cores(total):
        low, high = total[:row_count], total[row_count:]
        return jnp.where(c == 0, low, high), swap(jnp.where(c == 0, high, low), "ctx", 1)

    block_sum, output_sum, shard_squares = call(
        functools.partial(shards_kernel, half),
        [
            shape(block_count * row_count, local_width, F32),
            shape(5 * local_width, row_count, F32),
            shape(1, local_width, F32),
        ],
        from_cores(first_sum) + from_cores(hidden_sum) + (grad_w_mod,),
        0,
    )
    embed_sum = exact_dot(one_hot.astype(F32).T, grad_cond) + exact_dot(
        freq_low.astype(F32).T, grad_t_pre
    )
    patch_padded = jnp.concatenate(
        [jnp.zeros((embed_rows, row_count), F32), patch_sum, jnp.zeros((embed_rows, row_count), F32)],
        axis=0,
    )
    patch_start = embed_rows * t + embed_rows - (FREQ + CLASSES)
    embed_sum = embed_sum + lax.dynamic_slice_in_dim(
        patch_padded, jnp.clip(patch_start, 0, embed_rows + PATCH_ROWS), embed_rows, 0
    )

    head_squares = jnp.where(t == 0, jnp.sum(head_grad_sum * head_grad_sum), 0.0)
    shard_squares = (
        jnp.sum(shard_squares)
        + jnp.sum(embed_sum * embed_sum)
        + jnp.sum(top_grad * top_grad)
        + head_squares
    )
    b1_part = jnp.where(t == 0, jnp.sum(grad_t_pre, axis=0), 0.0)
    b1_row = lax.dynamic_update_slice_in_dim(jnp.zeros((width,), F32), b1_part, place * row_count, 0)
    last = jnp.concatenate([b1_row, jnp.broadcast_to(shard_squares, (128,))])
    last = sum_over(last, ("ctx", "tp", "fsdp"))
    bias_sum = jnp.concatenate(
        [bias_patch, last[None, :width], grad_b_cond[None], bias_mod, shared[:8], bias_final], axis=0
    )
    grad_norm = jnp.sqrt(last[width] + jnp.sum(bias_sum * bias_sum))
    clip_factor = jnp.minimum(1.0, 1.0 / (grad_norm + 1e-06))
    def tall(values):
        return jnp.transpose(values, (1, 0, 2)).reshape(block_count * row_count, local_width)

    upd_block = [
        jnp.transpose(u.reshape(block_count, row_count, local_width), (1, 0, 2))
        for u in adam_blocks(tall(w_block), block_sum, tall(m_block), tall(v_block), clip_factor)
    ]
    upd_output = [
        u.reshape(w_output.shape)
        for u in adam_blocks(
            *[m.reshape(output_sum.shape) if m.ndim == 3 else m for m in (w_output, output_sum, m_output, v_output)],
            clip_factor,
        )
    ]
    upd_top = adam_update(w_top, top_grad, m_top, v_top, clip_factor)
    upd_head = adam_update(w_head, head_grad_sum, m_head, v_head, clip_factor)
    upd_embed = adam_update(w_embed, embed_sum, m_embed, v_embed, clip_factor)
    upd_biases = adam_update(biases, bias_sum, m_biases, v_biases, clip_factor)
    updates = (upd_block, upd_output, upd_top, upd_head, upd_embed, upd_biases)
    return (
        (loss_total, grad_norm)
        + tuple(u[0] for u in updates)
        + tuple(u[1] for u in updates)
        + tuple(u[2] for u in updates)
        + (bias_sum * clip_factor,)
    )


def solution(mesh):
    both = ("fsdp", "ctx")
    weights = (
        P(both, None, "tp"),
        P(None, "tp", both),
        P(both, "tp"),
        P(both, None),
        P("tp", both),
        P(),
    )
    images = (P(both, None, None, None), P(both, None, None, None), P(both), P(both))
    return jax.shard_map(
        on_device,
        mesh=mesh,
        in_specs=images + weights * 3,
        out_specs=(P(), P()) + weights * 3 + (P(),),
        check_vma=False,
    )
```

```python
import functools
import math

import jax
import jax.numpy as jnp
from jax import lax
from jax.experimental import pallas as pl
from jax.experimental.pallas import tpu as pltpu
from jax.sharding import PartitionSpec as P

HEAD_DIM = 64
CLASSES = 1000
FREQ = 256
TIMESTEPS = 1000
ADAM_STEP = 10
PATCH_ROWS = 16
PINS = (None, 1, 3, 4, 6)
CHAIN = (18, 1)

PRECISE = lax.Precision.HIGHEST
BF = jnp.bfloat16
F32 = jnp.float32


def exact_dot(left, right):
    return jnp.dot(left, right, precision=PRECISE)


def mm(left, right):
    return jnp.dot(left, right, preferred_element_type=F32)


def mm_nt(left, right):
    return lax.dot_general(left, right, (((1,), (1,)), ((), ())), preferred_element_type=F32)


def mm_tn(left, right):
    return lax.dot_general(left, right, (((0,), (0,)), ((), ())), preferred_element_type=F32)


def gelu_tanh(values):
    return jax.nn.gelu(values, approximate=True)


def plan(step_ids):
    fraction = (step_ids.astype(F32) / TIMESTEPS + 0.008) / 1.008
    kept_share = jnp.cos(fraction * (math.pi / 2.0)) ** 2
    return (jnp.sqrt(kept_share), jnp.sqrt(1.0 - kept_share))


def patchify(field):
    img_count, chan_count, row_count, col_count = field.shape
    shaped = field.reshape(img_count, chan_count, row_count // 2, 2, col_count // 2, 2)
    shaped = shaped.transpose(0, 2, 4, 1, 3, 5)
    return shaped.reshape(img_count, row_count // 2 * (col_count // 2), chan_count * 4)


def adam_update(weight, gradient, first_mom, second_mom, clip_factor):
    clipped = gradient * clip_factor
    first_new = 0.9 * first_mom + 0.1 * clipped
    second_new = 0.999 * second_mom + 0.001 * clipped * clipped
    corr_first = 1.0 - 0.9**ADAM_STEP
    corr_second = 1.0 - 0.999**ADAM_STEP
    direction = first_new / corr_first / (jnp.sqrt(second_new / corr_second) + 1e-08)
    return (weight - 0.04 * (direction + 0.01 * weight), first_new, second_new)


def swap(value, axis, mask):
    count = lax.axis_size(axis)
    return lax.ppermute(value, axis, [(i, i ^ mask) for i in range(count)])


def pull(value, k):
    count = lax.axis_size("fsdp")
    return lax.ppermute(value, "fsdp", [((i + k) % count, i) for i in range(count)])


def push(value, k):
    count = lax.axis_size("fsdp")
    return lax.ppermute(value, "fsdp", [(i, (i + k) % count) for i in range(count)])


def is_ring():
    return lax.axis_size("fsdp") == 4


def pick(pair, bit, axis=0):
    low = lax.index_in_dim(pair, 0, axis, keepdims=False)
    high = lax.index_in_dim(pair, 1, axis, keepdims=False)
    return jnp.where(bit == 1, high, low)


def ordered(own, other, bit, axis=0):
    return jnp.stack([jnp.where(bit == 0, own, other), jnp.where(bit == 0, other, own)], axis)


def bits(count):
    return [1 << b for b in range(count.bit_length() - 1)]


def by_xor(stack, rank):
    for mask in (1, 2):
        other = jnp.stack([stack[i ^ mask] for i in range(4)])
        stack = jnp.where(rank & mask == mask, other, stack)
    return stack


def free(value):
    return value


def sum_over(value, axes, pace=free):
    for axis in axes:
        count = lax.axis_size(axis)
        if count == 2:
            value = value + swap(pace(value), axis, 1)
        elif count == 4:
            sent = pace(value)
            one, two, three = [swap(sent, axis, k) for k in (1, 2, 3)]
            value = (value + one) + (two + three)
        else:
            value = lax.psum(value, axis)
    return value


def roll_lead(stack, steps):
    for mask in (1, 2):
        moved = jnp.stack([stack[(i + mask) % 4] for i in range(4)])
        stack = jnp.where(steps & mask == mask, moved, stack)
    return stack


def scatter_fc(blocks, pace=free):
    if not is_ring():
        return lax.psum_scatter(blocks, ("fsdp", "ctx"), scatter_dimension=0, tiled=False)
    f, c = lax.axis_index("fsdp"), lax.axis_index("ctx")
    held = blocks.reshape((4, 2) + blocks.shape[1:])
    held = pick(held, c, 1) + swap(pace(pick(held, 1 - c, 1)), "ctx", 1)
    held = pace(roll_lead(held, f))
    return (held[0] + push(held[2], 2)) + (push(held[1], 1) + push(held[3], 3))


def gather_fc(value, pace=free):
    if not is_ring():
        return lax.all_gather(value, ("fsdp", "ctx"), axis=0, tiled=False)
    f, c = lax.axis_index("fsdp"), lax.axis_index("ctx")
    sent = pace(value)
    held = jnp.stack([value] + [pull(sent, k) for k in (1, 2, 3)])
    held = roll_lead(held, (4 - f) & 3)
    held = ordered(held, swap(pace(held), "ctx", 1), c, 1)
    return held.reshape((8,) + value.shape)


def exchange_tp(blocks, pace=free):
    t = lax.axis_index("tp")
    mine = pace(by_xor(blocks, t))
    got = jnp.stack([mine[0]] + [swap(mine[k], "tp", k) for k in (1, 2, 3)])
    return by_xor(got, t)


def gather_and_sum(to_tp, shared, split, pace):
    f, c, t = lax.axis_index("fsdp"), lax.axis_index("ctx"), lax.axis_index("tp")
    images, wide = to_tp.shape[1:]
    width = shared.shape[1]
    per_image = -(-wide // width)
    padded = jnp.pad(to_tp, ((0, 0), (0, 0), (0, per_image * width - wide)))
    mine = by_xor(padded.reshape(4, images * per_image, width), t)
    kept, sums = images * per_image, shared.shape[0]
    rows = jnp.concatenate([shared, split], axis=0)
    sent = pace(jnp.concatenate([mine.reshape(-1, width), rows], axis=0))
    whole = [sent[i * kept : (i + 1) * kept] for i in range(4)]
    rows = sent[4 * kept :]
    got = [swap(jnp.concatenate([whole[k], rows], axis=0), "tp", k) for k in (1, 2, 3)]
    group = by_xor(jnp.stack([whole[0]] + [g[:kept] for g in got]), t).reshape(-1, width)
    rows = (rows + got[0][kept:]) + (got[1][kept:] + got[2][kept:])

    quarter = width // 4
    shared, split = rows[:sums], rows[sums:]
    blocks = roll_lead(jnp.stack([split[:, i * quarter : (i + 1) * quarter] for i in range(4)]), f)
    same = jnp.concatenate([group, shared], axis=0).reshape(-1, quarter)
    count = same.shape[0]
    sent = pace(jnp.concatenate([same, blocks.reshape(-1, quarter)], axis=0))
    same, blocks = sent[:count], [
        sent[count + i * split.shape[0] : count + (i + 1) * split.shape[0]] for i in range(4)
    ]
    got = [None] + [push(jnp.concatenate([same, blocks[k]], axis=0), k) for k in (1, 2, 3)]
    group_count = 4 * group.shape[0]
    by_sender = jnp.stack([same[:group_count]] + [got[k][:group_count] for k in (3, 2, 1)])
    by_sender = roll_lead(by_sender, (4 - f) & 3)
    shared = same[group_count:]
    shared = (shared + got[2][group_count:count]) + (got[1][group_count:count] + got[3][group_count:count])
    split = (blocks[0] + got[2][count:]) + (got[1][count:] + got[3][count:])

    half = quarter // 2
    low, high = split[:, :half], split[:, half:]
    other_half = jnp.where(c == 0, high, low)
    shared_half = shared.reshape(-1, half)
    sent = pace(
        jnp.concatenate([by_sender.reshape(-1, half), shared_half, other_half], axis=0)
    )
    got = swap(sent, "ctx", 1)
    count = by_sender.size // half
    group = ordered(
        sent[:count].reshape(4, -1), got[:count].reshape(4, -1), c, 1
    ).reshape(-1, per_image * width)[:, :wide]
    shared = (shared_half + got[count : count + shared_half.shape[0]]).reshape(-1, width)
    split = jnp.where(c == 0, low, high) + got[count + shared_half.shape[0] :]
    return group, shared, split


class Lane:
    def __init__(self, depth):
        self.depth = depth
        self.ended = []

    def __call__(self, value, move):
        if len(self.ended) >= self.depth:
            value, _ = lax.optimization_barrier((value, self.ended[-self.depth]))
        moved = move(value)
        self.ended.append(moved)
        return moved


class Pace:
    def __init__(self, lanes, first, step, others=()):
        self.ended = list(lanes.ended)
        self.next, self.step = first, step
        self.others = list(others)

    def __call__(self, value):
        at = min(self.next, len(self.ended) - 1)
        if at >= 0:
            value, _ = lax.optimization_barrier((value, self.ended[at]))
        self.next += self.step
        other = self.others.pop(0) if self.others else None
        if other is not None:
            value, _ = lax.optimization_barrier((value, other))
        return value


class Lanes:
    def __init__(self, x, y, z):
        self.ended = []
        self.lane_x, self.lane_y, self.lane_z = Lane(x), Lane(y), Lane(z)

    def note(self, moved):
        self.ended.append(moved)
        return moved

    def x(self, value):
        return self.note(self.lane_x(value, lambda v: swap(v, "tp", 1)))

    def y(self, value):
        return self.note(self.lane_y(value, lambda v: swap(v, "tp", 2)))

    def pull(self, value, k):
        return self.note(self.lane_z(value, lambda v: pull(v, k)))

    def push(self, value, k):
        return self.note(self.lane_z(value, lambda v: push(v, k)))


def add(left, right):
    return left.astype(F32) + right.astype(F32)


def add_low(left, right):
    return add(left, right).astype(BF)


def reduce_grid(lanes, main):
    if not is_ring():
        parts = main[0]
        along_x = swap(parts[1], "tp", 1)
        along_y = swap(add_low(parts[2], swap(parts[3], "tp", 1)), "tp", 2)
        both = add_low(add(parts[0], along_x), along_y)
        return lax.psum_scatter(both, "fsdp", scatter_dimension=0, tiled=True).astype(F32)
    far_2, far_1 = lanes.y(main[2][3]), None
    far_3 = lanes.x(main[3][3])
    y_2 = lanes.y(main[2][2])
    x_2 = lanes.x(add_low(main[2][1], far_2))
    far_1 = lanes.y(main[1][3])
    x_3 = lanes.x(main[3][1])
    y_3 = lanes.y(add_low(main[3][2], far_3))
    sum_2 = lanes.push(add_low(add(main[2][0], x_2), y_2), 1)
    y_1 = lanes.y(main[1][2])
    x_1 = lanes.x(add_low(main[1][1], far_1))
    far_0 = lanes.x(main[0][3])
    sum_3 = lanes.push(add_low(add(main[3][0], x_3), y_3), 3)
    x_0 = lanes.x(main[0][1])
    sum_1 = add(add(add(main[1][0], x_1), y_1), sum_2).astype(BF)
    sum_1 = lanes.push(sum_1, 1)
    y_0 = lanes.y(add_low(main[0][2], far_0))
    return add(add(add(main[0][0], x_0), y_0), sum_3) + sum_1.astype(F32)


def rows_of(table, start, count):
    pad = jnp.zeros((count,) + table.shape[1:], table.dtype)
    padded = jnp.concatenate([pad, table, pad], axis=0)
    return lax.dynamic_slice_in_dim(padded, jnp.clip(start + count, 0, table.shape[0] + count), count, 0)


class View:
    def __init__(self, array, width, index):
        self.array, self.width, self.index = array, width, index


def whole_block(dims):
    return pl.BlockSpec(dims, lambda i: (0,) * len(dims), pipeline_mode=pl.Buffered(1))


def call(body, outs, args, flops, scratch=()):
    flat, tree = jax.tree.flatten(args)
    arrays, specs, held = [], [], 0
    for leaf in flat:
        if isinstance(leaf, View):
            dims = (leaf.array.shape[0], leaf.width)
            at = leaf.index
            specs.append(
                pl.BlockSpec(dims, lambda i, at=at: (0, at), pipeline_mode=pl.Buffered(1))
            )
            arrays.append(leaf.array)
        else:
            dims = leaf.shape
            specs.append(whole_block(dims))
            arrays.append(leaf)
        held += math.prod(dims) * arrays[-1].dtype.itemsize
    held += sum(o.size * o.dtype.itemsize for o in outs)
    room = 2 * held + sum(4 * math.prod(a.shape) for a in scratch) + 8 * 1024 * 1024

    def kernel(*refs):
        body(*jax.tree.unflatten(tree, refs[: len(flat)]), *refs[len(flat) :])

    return pl.pallas_call(
        kernel,
        grid=(1,),
        out_shape=outs,
        in_specs=specs,
        out_specs=[whole_block(o.shape) for o in outs],
        scratch_shapes=list(scratch),
        compiler_params=pltpu.CompilerParams(vmem_limit_bytes=56 * 1024 * 1024),
        cost_estimate=pl.CostEstimate(flops=flops, bytes_accessed=held, transcendentals=0),
    )(*arrays)


def shape(rows, cols, dtype):
    return jax.ShapeDtypeStruct((rows, cols), dtype)


def down_rows(parts, k_t, start, stop):
    return jnp.concatenate([row[k_t][:, start:stop] for row in parts], axis=0)


def head_masks(half):
    at = lax.broadcasted_iota(jnp.int32, (1, half), 1) // HEAD_DIM
    return [at == h for h in range(half // HEAD_DIM)]


def softmax_rows(scores):
    top = jnp.max(scores, axis=-1, keepdims=True)
    grown = jnp.exp(scores - top)
    return grown / jnp.sum(grown, axis=-1, keepdims=True)


def merged(masks, values):
    total = values[-1]
    for mask, value in zip(masks[:-1], values[:-1]):
        total = jnp.where(mask, value, total)
    return total


def split_t(ref):
    width = ref.shape[0] // 4
    return [[ref.at[i * width : (i + 1) * width] for i in range(4)]]


def qkv_kernel(tok_count, half, own_ref, other_ref, weight_ref, bias_ref, qkv_ref, attended_ref):
    parts = split_t(weight_ref)
    rows = own_ref.shape[0]
    masks = head_masks(half)
    for i, ref in enumerate((own_ref, other_ref)):
        left = ref[...]
        for k_t in range(4):
            cols = slice(k_t * 3 * half, (k_t + 1) * 3 * half)
            weight = down_rows(parts, k_t, 0, 3 * half)
            qkv_ref[i * rows : (i + 1) * rows, cols] = (
                mm(left, weight) + bias_ref[:, cols]
            ).astype(BF)
    for k_t in range(4):
        at = k_t * 3 * half
        for row in range(0, 2 * rows, tok_count):
            here = slice(row, row + tok_count)
            query = qkv_ref[here, at : at + half]
            key = qkv_ref[here, at + half : at + 2 * half]
            value = qkv_ref[here, at + 2 * half : at + 3 * half]
            got = []
            for mask in masks:
                masked = jnp.where(mask, query, jnp.zeros_like(query))
                probs = softmax_rows(mm_nt(masked, key) * 0.125).astype(BF)
                got.append(mm(probs, value))
            attended_ref[here, k_t * half : (k_t + 1) * half] = merged(masks, got).astype(BF)


def attention_back_kernel(
    tok_count, half, own_ref, other_ref, weight_ref, qkv_ref, out_ref, sum_ref
):
    parts = split_t(weight_ref)
    rows = own_ref.shape[0]
    masks = head_masks(half)
    left = [ref[...] for ref in (own_ref, other_ref)]
    for k_t in range(4):
        at = k_t * 3 * half
        weight = down_rows(parts, k_t, 0, half)
        for i in range(2):
            grad_half = mm(left[i], weight).astype(BF)
            for row in range(0, rows, tok_count):
                here = slice(i * rows + row, i * rows + row + tok_count)
                grad = grad_half[row : row + tok_count]
                query = qkv_ref[here, at : at + half]
                key = qkv_ref[here, at + half : at + 2 * half]
                value = qkv_ref[here, at + 2 * half : at + 3 * half]
                grad_q, grad_k, grad_v = [], [], []
                for mask in masks:
                    zero = jnp.zeros_like(query)
                    probs = softmax_rows(mm_nt(jnp.where(mask, query, zero), key) * 0.125)
                    grad_p = mm_nt(jnp.where(mask, grad, zero), value)
                    grad_s = (
                        probs * (grad_p - jnp.sum(grad_p * probs, axis=-1, keepdims=True))
                    ).astype(BF)
                    grad_q.append(mm(grad_s, key))
                    grad_k.append(mm_tn(grad_s, query))
                    grad_v.append(mm_tn(probs.astype(BF), grad))
                out_ref[here, at : at + half] = (merged(masks, grad_q) * 0.125).astype(BF)
                out_ref[here, at + half : at + 2 * half] = (merged(masks, grad_k) * 0.125).astype(BF)
                out_ref[here, at + 2 * half : at + 3 * half] = merged(masks, grad_v).astype(BF)
        cols = slice(at, at + 3 * half)
        sum_ref[:, cols] = jnp.sum(out_ref[:, cols].astype(F32), axis=0, keepdims=True)


def features_kernel(left_ref, weight_ref, own_ref, other_ref):
    parts = split_t(weight_ref)
    rows, size = own_ref.shape
    block = size // 4
    for k in range(4):
        cols = slice(k * block, (k + 1) * block)
        weight = jnp.concatenate([p[cols, :] for p in parts[0]], axis=1)
        own_ref[:, cols] = mm_nt(left_ref[:rows], weight)
        other_ref[:, cols] = mm_nt(left_ref[rows:], weight).astype(BF)


def gelu_slope(values):
    scale = math.sqrt(2.0 / math.pi)
    bent = jnp.tanh(scale * (values + 0.044715 * (values * values * values)))
    inner = scale * (1.0 + 3.0 * 0.044715 * (values * values))
    return 0.5 * (1.0 + bent) + 0.5 * values * (1.0 - bent * bent) * inner


def mlp_kernel(own_ref, other_ref, up_ref, down_ref, bias_ref, pre_ref, act_ref, own_out, other_out):
    rows = own_ref.shape[0]

    @pl.when(pl.program_id(0) == 0)
    def _():
        own_out[...] = jnp.zeros_like(own_out)
        other_out[...] = jnp.zeros_like(other_out)

    for i, (ref, out) in enumerate(((own_ref, own_out), (other_ref, other_out))):
        here = slice(i * rows, (i + 1) * rows)
        pre = mm(ref[...], up_ref[...]) + bias_ref[...]
        pre_ref[here, :] = pre
        act = gelu_tanh(pre).astype(BF)
        act_ref[here, :] = act
        out[...] += mm_nt(act, down_ref[...])


def mlp_back_kernel(
    own_ref,
    other_ref,
    own_in,
    other_in,
    up_ref,
    down_ref,
    pre_ref,
    act_ref,
    grad_ref,
    sum_ref,
    own_out,
    other_out,
    flipped,
):
    rows, width = own_ref.shape
    size = up_ref.shape[1]

    @pl.when(pl.program_id(0) == 0)
    def _():
        own_out[...] = jnp.zeros_like(own_out)
        other_out[...] = jnp.zeros_like(other_out)
        for i, ref in enumerate((own_in, other_in, own_ref, other_ref)):
            flipped[
                i // 2 * width : (i // 2 + 1) * width, i % 2 * rows : (i % 2 + 1) * rows
            ] = ref[...].T

    total, grads = 0.0, []
    for i, (ref, out) in enumerate(((own_ref, own_out), (other_ref, other_out))):
        here = slice(i * rows, (i + 1) * rows)
        grad = (mm(ref[...], down_ref[...]) * gelu_slope(pre_ref[here, :])).astype(BF)
        total = total + col_sum(grad.astype(F32))
        out[...] += mm_nt(grad, up_ref[...])
        grads.append(grad)
    sum_ref[...] = total
    grad_ref[:, :size] = mm(flipped[:width, :], jnp.concatenate(grads, axis=0)).astype(BF)
    grad_ref[:, size:] = mm(flipped[width:, :], act_ref[...]).astype(BF)


def over_hidden(kernel, counts, outs, args, flops, scratch=()):
    def spec(block, index):
        return pl.BlockSpec(block, index)

    return pl.pallas_call(
        kernel,
        grid=(counts,),
        out_shape=[o[0] for o in outs],
        in_specs=[spec(a[1], a[2]) for a in args],
        out_specs=[spec(o[1], o[2]) for o in outs],
        scratch_shapes=list(scratch),
        compiler_params=pltpu.CompilerParams(vmem_limit_bytes=56 * 1024 * 1024),
        cost_estimate=pl.CostEstimate(
            flops=flops, bytes_accessed=32 * 1024 * 1024, transcendentals=0
        ),
    )(*[a[0] for a in args])


def piece_kernel(half, places, attn, grad_attn, grad_qkv_ref, attended_ref, *refs):
    outs, flipped = refs[:-1], refs[-1]
    t = lax.axis_index("tp")
    size = outs[0].shape[0]
    width = attn[0].shape[1]
    tokens = attn[0].shape[0]
    for i, pair in enumerate((attn, grad_attn)):
        for j, ref in enumerate(pair):
            flipped[i * width : (i + 1) * width, j * tokens : (j + 1) * tokens] = ref[...].T
    for i, k_f in enumerate(places):
        if size == width:
            start = 0
        else:
            start = pl.multiple_of(((lax.axis_index("fsdp") + k_f) & 3) * size, size)
        left = [flipped[pl.ds(i * width + start, size), :] for i in range(2)]
        for k_t in range(4):
            out = outs[i * 4 + k_t]
            place = t ^ k_t

            def cols(count):
                return pl.ds(pl.multiple_of(place * count, count), count)

            out[:, : 3 * half] = mm(left[0], grad_qkv_ref[:, cols(3 * half)]).astype(BF)
            out[:, 3 * half :] = mm(left[1], attended_ref[:, cols(half)]).astype(BF)


def normed(values):
    center = values - jnp.mean(values, axis=-1, keepdims=True)
    spread = jnp.mean(center * center, axis=-1, keepdims=True)
    inverse = lax.rsqrt(spread + 1e-06)
    return center * inverse, inverse


def norm_back(grad, norm, inverse):
    mean = jnp.mean(grad, axis=-1, keepdims=True)
    slope = jnp.mean(grad * norm, axis=-1, keepdims=True)
    return inverse * (grad - mean - norm * slope)


def col_sum(values):
    return jnp.sum(values, axis=0, keepdims=True)


def enter_kernel(images, patch_ref, w_ref, place_ref, mod_ref, resid_ref, attn_ref):
    count = patch_ref.shape[0] // images
    for i in range(images):
        here = slice(i * count, (i + 1) * count)
        resid = mm(patch_ref[here], w_ref[...]) + place_ref[...]
        resid_ref[here] = resid
        mod = mod_ref[i]
        attn_ref[here] = (normed(resid)[0] * (1.0 + mod[1:2]) + mod[0:1]).astype(BF)


def middle_kernel(images, own_ref, got_ref, bias_ref, resid_ref, mod_ref, out_ref, mid_ref, mlp_ref):
    count = own_ref.shape[0] // images
    for i in range(images):
        here = slice(i * count, (i + 1) * count)
        mod = mod_ref[i]
        out = own_ref[here] + got_ref[here] + bias_ref[...]
        out_ref[here] = out
        mid = resid_ref[here] + mod[2:3] * out
        mid_ref[here] = mid
        mlp_ref[here] = (normed(mid)[0] * (1.0 + mod[4:5]) + mod[3:4]).astype(BF)


def top_kernel(
    images,
    own_ref,
    got_ref,
    bias_ref,
    mid_ref,
    mod_ref,
    final_ref,
    head_ref,
    target_ref,
    resid_ref,
    mlp_ref,
    rows_ref,
    head_grad_ref,
    loss_ref,
    images_all,
):
    count = own_ref.shape[0] // images
    loss, head_grad = 0.0, 0.0
    for i in range(images):
        here = slice(i * count, (i + 1) * count)
        gate = mod_ref[i][5:6]
        shift, scale = final_ref[i][0:1], final_ref[i][1:2]
        out = own_ref[here] + got_ref[here] + bias_ref[...]
        norm, inverse = normed(mid_ref[here] + gate * out)
        head_in = (norm * (1.0 + scale) + shift).astype(BF)
        error = mm_nt(head_in, head_ref[...]) - target_ref[here]
        loss = loss + jnp.sum(col_sum(error * error), axis=1, keepdims=True) / images_all
        grad_pred = (2.0 / images_all * error).astype(BF)
        grad = mm(grad_pred, head_ref[...])
        head_grad = head_grad + mm_tn(grad_pred, head_in)
        resid = norm_back(grad * (1.0 + scale), norm, inverse)
        resid_ref[here] = resid
        mlp = (resid * gate).astype(BF)
        mlp_ref[here] = mlp
        rows_ref[i] = jnp.concatenate(
            [col_sum(grad), col_sum(grad * norm), col_sum(resid * out), col_sum(mlp.astype(F32))], axis=0
        )
    head_grad_ref[...] = head_grad
    loss_ref[...] = jnp.broadcast_to(loss, loss_ref.shape)


def middle_back_kernel(
    images, own_ref, got_ref, mid_ref, mod_ref, resid_ref, out_ref, new_ref, attn_ref, rows_ref
):
    count = own_ref.shape[0] // images
    for i in range(images):
        here = slice(i * count, (i + 1) * count)
        mod = mod_ref[i]
        grad = own_ref[here] + got_ref[here]
        norm, inverse = normed(mid_ref[here])
        resid = resid_ref[here] + norm_back(grad * (1.0 + mod[4:5]), norm, inverse)
        new_ref[here] = resid
        attn = (resid * mod[2:3]).astype(BF)
        attn_ref[here] = attn
        rows_ref[i] = jnp.concatenate(
            [
                col_sum(grad),
                col_sum(grad * norm),
                col_sum(resid * out_ref[here]),
                col_sum(attn.astype(F32)),
            ],
            axis=0,
        )


def enter_back_kernel(
    images, own_ref, got_ref, in_ref, mod_ref, resid_ref, patch_ref, rows_ref, patch_grad_ref
):
    count = own_ref.shape[0] // images
    patch_grad = 0.0
    for i in range(images):
        here = slice(i * count, (i + 1) * count)
        grad = own_ref[here] + got_ref[here]
        norm, inverse = normed(in_ref[here])
        resid = resid_ref[here] + norm_back(grad * (1.0 + mod_ref[i][1:2]), norm, inverse)
        low = resid.astype(BF)
        rows_ref[i] = jnp.concatenate(
            [col_sum(grad), col_sum(grad * norm), col_sum(low.astype(F32))], axis=0
        )
        patch_grad = patch_grad + mm_tn(patch_ref[here], low)
    patch_grad_ref[...] = patch_grad


def adam_kernel(clip_ref, w_ref, g_ref, m_ref, v_ref, new_ref, first_ref, second_ref):
    new_ref[...], first_ref[...], second_ref[...] = adam_update(
        w_ref[...], g_ref[...], m_ref[...], v_ref[...], clip_ref[0, 0]
    )


def adam_blocks(weight, gradient, first_mom, second_mom, clip_factor):
    rows, cols = weight.shape
    count = 4 if rows % 32 == 0 else 1
    block = pl.BlockSpec((rows // count, cols), lambda i: (i, 0))
    return pl.pallas_call(
        adam_kernel,
        grid=(count,),
        out_shape=[jax.ShapeDtypeStruct(weight.shape, F32)] * 3,
        in_specs=[pl.BlockSpec(memory_space=pltpu.SMEM)] + [block] * 4,
        out_specs=[block] * 3,
        compiler_params=pltpu.CompilerParams(vmem_limit_bytes=32 * 1024 * 1024),
        cost_estimate=pl.CostEstimate(flops=0, bytes_accessed=28 * weight.size, transcendentals=0),
    )(clip_factor.reshape(1, 1), weight, gradient, first_mom, second_mom)


def shards_kernel(half, first_ref, first_got, down_ref, down_got, mod_ref, block_ref, output_ref, square_ref):
    c = lax.axis_index("ctx")
    count = first_ref.shape[0]
    total = 0.0

    def joined(own_ref, got_ref, i):
        own, got = own_ref[:, i * half : (i + 1) * half], got_ref[:, i * half : (i + 1) * half]
        both = jnp.concatenate([jnp.where(c == 0, own, got), jnp.where(c == 0, got, own)], axis=1)
        return both, col_sum(both * both)

    for i in range(7):
        both, squares = joined(first_ref, first_got, i) if i < 3 else joined(down_ref, down_got, i - 3)
        block_ref[i * count : (i + 1) * count, :] = both
        total = total + squares
    for i in range(5):
        both, squares = joined(first_ref, first_got, 3) if i == 0 else joined(down_ref, down_got, i + 3)
        output_ref[i * 2 * half : (i + 1) * 2 * half, :] = both.T
        total = total + squares
    for i in range(6):
        part = mod_ref[:, i * 2 * half : (i + 1) * 2 * half]
        block_ref[(7 + i) * count : (8 + i) * count, :] = part
        total = total + col_sum(part * part)
    square_ref[...] = total


def on_device(
    latents,
    noise_sample,
    timesteps,
    class_labels,
    w_block,
    w_output,
    w_top,
    w_head,
    w_embed,
    biases,
    m_block,
    m_output,
    m_top,
    m_head,
    m_embed,
    m_biases,
    v_block,
    v_output,
    v_top,
    v_head,
    v_embed,
    v_biases,
):
    f, c, t = lax.axis_index("fsdp"), lax.axis_index("ctx"), lax.axis_index("tp")
    nt = lax.axis_size("tp")
    places = lax.axis_size("fsdp") * lax.axis_size("ctx")
    place = f * lax.axis_size("ctx") + c
    row_count, block_count, local_width = w_block.shape
    half = local_width // 2
    width = local_width * nt
    group_images = latents.shape[0]
    images_all = group_images * places
    img_count = group_images // nt
    grid_side = latents.shape[3] // 2
    tok_count = latents.shape[2] // 2 * grid_side
    embed_rows = w_embed.shape[0]
    top_cols = w_top.shape[1]

    block_low = jnp.transpose(w_block, (1, 0, 2)).astype(BF)
    output_low = jnp.transpose(w_output, (0, 2, 1)).astype(BF)
    top_low = w_top.astype(BF)
    embed_low = w_embed.astype(BF)

    def core_half(blocks):
        low, high = blocks[:, :, :half], blocks[:, :, half:]
        return jnp.where(c == 0, low, high), jnp.where(c == 0, high, low)

    def beside(blocks):
        return jnp.concatenate([blocks[i] for i in range(blocks.shape[0])], axis=1)

    mixed = jnp.concatenate(
        [block_low[0:3], output_low[0:1], block_low[3:7], output_low[1:5]], axis=0
    )
    mine, other = core_half(mixed)
    mine, other = beside(mine), swap(beside(other), "ctx", 1)
    shards = jnp.concatenate(
        [jnp.where(c == 0, mine, other), jnp.where(c == 0, other, mine)], axis=0
    )
    full = lax.all_gather(shards, ("tp", "fsdp"), axis=0, tiled=True)
    pace = free

    patch_rows = rows_of(embed_low, FREQ + CLASSES - embed_rows * t, PATCH_ROWS)
    ids = jnp.concatenate([timesteps, class_labels]).astype(F32)
    ids = jnp.concatenate([ids, jnp.zeros((row_count - 2 * group_images % row_count,), F32)])[None]
    ids = ids.reshape(-1, row_count)
    small = jnp.concatenate([ids, patch_rows.astype(F32), w_head.T.astype(BF).astype(F32)], axis=0)
    small = gather_fc(small, pace)
    ids_all = small[:, : ids.shape[0]].reshape(places, -1)
    steps_all = ids_all[:, :group_images].reshape(images_all)
    labels_all = ids_all[:, group_images : 2 * group_images].reshape(images_all).astype(jnp.int32)
    small = small[:, ids.shape[0] :].transpose(1, 0, 2).reshape(2 * PATCH_ROWS, width)
    patch_part, w_head_t = small[:PATCH_ROWS], small[PATCH_ROWS:].astype(BF)
    embed_at = embed_rows * t + jnp.arange(embed_rows, dtype=jnp.int32)
    half_freq = FREQ // 2
    rates = jnp.exp(-math.log(10000.0) * (embed_at % half_freq).astype(F32) / half_freq)
    angles = steps_all[:, None] * rates[None, :]
    waves = jnp.where(embed_at[None, :] < half_freq, jnp.cos(angles), jnp.sin(angles))
    freq_low = jnp.where(embed_at[None, :] < FREQ, waves, 0.0).astype(BF)
    one_hot = (labels_all[:, None] + FREQ == embed_at[None, :]).astype(BF)
    own_cols = lambda row: lax.dynamic_slice_in_dim(row, place * row_count, row_count, 0)
    over_tp = jnp.concatenate([mm(freq_low, embed_low), patch_part.reshape(-1, row_count)], axis=0)
    over_tp = sum_over(over_tp, ("tp",), pace)
    t_pre = over_tp[:images_all] + own_cols(biases[1])
    w_patch = over_tp[images_all:].reshape(PATCH_ROWS, width).astype(BF)
    t_hidden = jax.nn.silu(t_pre).astype(BF)
    table_part = mm(one_hot, embed_low)
    top_at = top_cols * t + jnp.arange(top_cols, dtype=jnp.int32)
    cond_cols = mm(t_hidden, top_low)
    cond_cols = jnp.where(top_at[None, :] < width, cond_cols, 0.0)
    cond_wide = jnp.concatenate(
        [jnp.zeros((images_all, width), F32), cond_cols, jnp.zeros((images_all, width), F32)], axis=1
    )
    cond_wide = lax.dynamic_slice_in_dim(
        cond_wide, jnp.clip(width - top_cols * t, 0, width + top_cols), width, 1
    )
    cond_blocks = cond_wide.reshape(images_all, places, row_count).transpose(1, 0, 2)
    cond = sum_over(scatter_fc(cond_blocks, pace) + table_part, ("tp",), pace) + own_cols(biases[2])
    cond_low = jax.nn.silu(cond).astype(BF)
    mod_low = block_low[7:13]
    mod_cols = jnp.concatenate([mm(cond_low, mod_low[j]) for j in range(6)], axis=1)
    final_cols = jnp.where(top_at[None, :] < width, 0.0, mm(cond_low, top_low))
    all_cols = jnp.concatenate([mod_cols, final_cols], axis=1)
    group_cols = scatter_fc(all_cols.reshape(places, group_images, all_cols.shape[1]), pace)
    own_parts = exchange_tp(group_cols.reshape(nt, img_count, -1), pace)
    mod_width = 6 * local_width
    modulation = (
        own_parts[:, :, :mod_width]
        .reshape(nt, img_count, 6, local_width)
        .transpose(1, 2, 0, 3)
        .reshape(img_count, 6, width)
    ) + biases[3:9][None]
    final_mod = own_parts[:, :, mod_width:].transpose(1, 0, 2).reshape(img_count, 3 * width)
    final_mod = final_mod[:, width:].reshape(img_count, 2, width) + biases[17:19][None]
    shift_f, scale_f = final_mod[:, 0], final_mod[:, 1]

    def own_images(values):
        return lax.dynamic_slice_in_dim(values, t * img_count, img_count, 0)

    latent_vals = own_images(latents).astype(F32)
    noise_vals = own_images(noise_sample).astype(F32)
    keep_rate, drop_rate = plan(own_images(timesteps))
    noisy = (
        keep_rate[:, None, None, None] * latent_vals + drop_rate[:, None, None, None] * noise_vals
    )
    patches = patchify(noisy).astype(BF)
    target = patchify(noise_vals)

    quarter = width // 4
    pos_rates = jnp.exp(-math.log(10000.0) * jnp.arange(quarter, dtype=F32) / quarter)
    side_angle = jnp.arange(grid_side, dtype=F32)[:, None] * pos_rates[None, :]
    side = jnp.concatenate([jnp.sin(side_angle), jnp.cos(side_angle)], axis=-1)
    rows_side = jnp.broadcast_to(side[:, None, :], (tok_count // grid_side, grid_side, 2 * quarter))
    cols_side = jnp.broadcast_to(side[None, :, :], (tok_count // grid_side, grid_side, 2 * quarter))
    positions = jnp.concatenate([rows_side, cols_side], axis=-1).reshape(tok_count, width)

    bias_width = jnp.stack([biases[0], biases[11], biases[16]])

    def heads_bias(rows):
        shaped = rows.reshape(-1, nt, 2, half)
        return jnp.where(c == 0, shaped[:, :, 0], shaped[:, :, 1]).transpose(1, 0, 2)

    bias_qv = heads_bias(biases[9:11])
    bias_qkv = jnp.stack([bias_qv[:, 0], jnp.zeros_like(bias_qv[:, 0]), bias_qv[:, 1]], axis=1).reshape(-1)
    bias_up = heads_bias(biases[12:16]).reshape(-1)
    qkv_view, proj_view = View(full, 3 * half, 0), View(full, half, 3)

    own_count = img_count * tok_count
    core_width = nt * half
    matrix_flops = 4 * own_count * width * half

    two_sums = [shape(own_count, width, F32), shape(own_count, width, BF)]

    def run(body, outs, blocks, *args):
        return call(body, outs, args, blocks * nt * matrix_flops)

    def small_run(body, outs, *args):
        return call(functools.partial(body, img_count), outs, args, 0)

    def cube(rows):
        return jax.ShapeDtypeStruct((img_count, rows, width), F32)

    flat_f32, flat_low = shape(own_count, width, F32), shape(own_count, width, BF)

    patches = patches.reshape(own_count, PATCH_ROWS)
    resid_in, attn_own = small_run(
        enter_kernel,
        [flat_f32, flat_low],
        patches,
        w_patch,
        positions + bias_width[0],
        modulation,
    )
    attn_other = swap(attn_own, "ctx", 1)
    qkv_low, attended = run(
        functools.partial(qkv_kernel, tok_count, half),
        [shape(2 * own_count, 3 * core_width, BF), shape(2 * own_count, core_width, BF)],
        4,
        attn_own,
        attn_other,
        qkv_view,
        bias_qkv[None],
    )
    own, other = run(features_kernel, two_sums, 1, attended, proj_view)
    attn_out, resid_mid, mlp_own = small_run(
        middle_kernel,
        [flat_f32, flat_f32, flat_low],
        own,
        swap(other, "ctx", 1),
        bias_width[1:2],
        resid_in,
        modulation,
    )
    mlp_other = swap(mlp_own, "ctx", 1)
    hidden = 4 * half
    fixed = lambda i: (0, 0)
    column = lambda i: (0, i)
    wide_rows = (own_count, width)
    up_pre, up_act, own, other = over_hidden(
        mlp_kernel,
        nt,
        [
            (shape(2 * own_count, nt * hidden, F32), (2 * own_count, hidden), column),
            (shape(2 * own_count, nt * hidden, BF), (2 * own_count, hidden), column),
            (flat_f32, wide_rows, fixed),
            (flat_f32, wide_rows, fixed),
        ],
        [
            (mlp_own, wide_rows, fixed),
            (mlp_other, wide_rows, fixed),
            (full, (width, hidden), lambda i: (i, 1)),
            (full, (width, hidden), lambda i: (i, 2)),
            (bias_up[None], (1, hidden), column),
        ],
        8 * nt * matrix_flops,
    )
    grad_resid, grad_mlp, top_rows_grad, grad_head, loss_part = small_run(
        functools.partial(top_kernel, images_all=images_all),
        [flat_f32, flat_low, cube(4), shape(PATCH_ROWS, width, F32), shape(1, 128, F32)],
        own,
        swap(other, "ctx", 1),
        bias_width[2:3],
        resid_mid,
        modulation,
        final_mod,
        w_head_t,
        target.reshape(own_count, PATCH_ROWS),
    )
    loss_part = loss_part[0, 0]

    grad_mlp_other = swap(grad_mlp, "ctx", 1)
    grad_hidden_w, grad_b_up, own, other = over_hidden(
        mlp_back_kernel,
        nt,
        [
            (shape(nt * width, 2 * hidden, BF), (width, 2 * hidden), lambda i: (i, 0)),
            (shape(1, nt * hidden, F32), (1, hidden), column),
            (flat_f32, wide_rows, fixed),
            (flat_f32, wide_rows, fixed),
        ],
        [
            (grad_mlp, wide_rows, fixed),
            (grad_mlp_other, wide_rows, fixed),
            (mlp_own, wide_rows, fixed),
            (mlp_other, wide_rows, fixed),
            (full, (width, hidden), lambda i: (i, 1)),
            (full, (width, hidden), lambda i: (i, 2)),
            (up_pre, (2 * own_count, hidden), column),
            (up_act, (2 * own_count, hidden), column),
        ],
        16 * nt * matrix_flops,
        [pltpu.VMEM((2 * width, 2 * own_count), BF)],
    )
    grad_b_up = grad_b_up[0]
    lanes = Lanes(2, 2, 1)
    count = 4 if is_ring() else 1
    block_rows = width // count
    hidden_pieces = [
        [
            lax.dynamic_slice_in_dim(
                grad_hidden_w, (t ^ k_t) * width + ((f + k_f) & (count - 1)) * block_rows, block_rows, 0
            )
            for k_t in range(4)
        ]
        for k_f in range(count)
    ]
    hidden_sum = reduce_grid(lanes, hidden_pieces)

    def pin(value, at):
        if lanes.ended and at is not None:
            value, _ = lax.optimization_barrier((value, lanes.ended[at]))
        return value

    own = pin(own, PINS[0])
    grad_resid, grad_attn, middle_rows = small_run(
        middle_back_kernel,
        [flat_f32, flat_low, cube(4)],
        own,
        swap(other, "ctx", 1),
        resid_mid,
        modulation,
        grad_resid,
        attn_out,
    )
    grad_attn_other = swap(grad_attn, "ctx", 1)
    grad_qkv, grad_b_qkv = run(
        functools.partial(attention_back_kernel, tok_count, half),
        [shape(2 * own_count, 3 * core_width, BF), shape(1, 3 * core_width, F32)],
        2,
        pin(grad_attn, PINS[1]),
        grad_attn_other,
        proj_view,
        qkv_low,
    )
    grad_b_qkv = grad_b_qkv[0]
    lists = [(2, 3), (1, 0)] if is_ring() else [(0,)]
    pieces = [None] * (4 if is_ring() else 1)
    piece_size = shape(width // len(pieces), 4 * half, BF)
    for at, distances in enumerate(lists):
        made = call(
            functools.partial(piece_kernel, half, distances),
            [piece_size] * (4 * len(distances)),
            (
                (attn_own, attn_other),
                (grad_attn, grad_attn_other),
                pin(grad_qkv, PINS[2 + at]),
                attended,
            ),
            4 * nt * matrix_flops // len(lists),
            [pltpu.VMEM((2 * width, 2 * own_count), BF)],
        )
        for i, k_f in enumerate(distances):
            pieces[k_f] = made[4 * i : 4 * i + 4]
    first_sum = reduce_grid(lanes, pieces)
    grad_qkv, _ = lax.optimization_barrier((grad_qkv, pieces[0][0]))
    grad_qkv = pin(grad_qkv, PINS[4])
    own, other = run(features_kernel, two_sums, 3, grad_qkv, qkv_view)
    enter_rows, grad_patch = small_run(
        enter_back_kernel,
        [cube(3), shape(PATCH_ROWS, width, F32)],
        own,
        swap(other, "ctx", 1),
        resid_in,
        modulation,
        grad_resid,
        patches,
    )
    grad_b_patch = jnp.sum(enter_rows[:, 2], axis=0)
    grad_b_proj = jnp.sum(middle_rows[:, 3], axis=0)
    grad_b_down = jnp.sum(top_rows_grad[:, 3], axis=0)

    grad_mod = jnp.concatenate(
        [enter_rows[:, 0:2], middle_rows[:, 2:3], middle_rows[:, 0:2], top_rows_grad[:, 2:3]], axis=1
    )
    grad_final = top_rows_grad[:, 0:2]
    def heads_place(grad_rows):
        rows = grad_rows.transpose(1, 0, 2)
        empty = jnp.zeros_like(rows)
        return jnp.stack(
            [jnp.where(c == 0, rows, empty), jnp.where(c == 0, empty, rows)], axis=2
        ).reshape(-1, width)

    qkv_rows = grad_b_qkv.reshape(nt, 3, half)
    up_rows = heads_place(grad_b_up.reshape(nt, 4, half))
    loss_row = jnp.broadcast_to(loss_part, (1, width))
    shared = jnp.concatenate(
        [
            heads_place(jnp.stack([qkv_rows[:, 0], qkv_rows[:, 2]], axis=1)),
            grad_b_proj[None],
            up_rows,
            grad_b_down[None],
            loss_row,
        ],
        axis=0,
    )
    split = jnp.concatenate([grad_patch, grad_head, grad_b_patch[None]], axis=0)
    chain = Pace(lanes, *CHAIN)
    final_flat = jnp.concatenate(
        [jnp.zeros((img_count, width), F32), grad_final.reshape(img_count, 2 * width)], axis=1
    )
    to_tp = jnp.concatenate(
        [
            grad_mod.reshape(img_count, 6, nt, local_width)
            .transpose(2, 0, 1, 3)
            .reshape(nt, img_count, mod_width),
            final_flat.reshape(img_count, nt, top_cols).transpose(1, 0, 2),
        ],
        axis=-1,
    )
    if is_ring():
        all_grad, shared, split = gather_and_sum(to_tp, shared, split, chain)
    else:
        group_grad = exchange_tp(to_tp).reshape(group_images, -1)
        all_grad = gather_fc(group_grad).reshape(images_all, -1)
        shared = sum_over(shared, ("tp", "fsdp", "ctx"))
        split = split.reshape(split.shape[0], places, row_count).transpose(1, 0, 2)
        split = scatter_fc(sum_over(split, ("tp",)))
    all_mod, all_final = all_grad[:, :mod_width], all_grad[:, mod_width:]
    cond_rows = cond_low.astype(F32)
    grad_w_mod = exact_dot(cond_rows.T, all_mod)
    mod_flat = mod_low.astype(F32).transpose(1, 0, 2).reshape(row_count, mod_width)
    top_rows = top_low.astype(F32)
    part = exact_dot(all_mod, mod_flat.T) + exact_dot(all_final, top_rows.T)
    sent = chain(jnp.concatenate([part, jnp.sum(all_grad, axis=0).reshape(-1, row_count)], axis=0))
    got = [sent] + [swap(sent, "tp", k) for k in (1, 2, 3)]
    grad_cond_act = (got[0] + got[1])[:images_all] + (got[2] + got[3])[:images_all]
    col_sums = by_xor(jnp.stack([g[images_all:] for g in got]), t).reshape(nt, -1)
    bias_mod = col_sums[:, :mod_width].reshape(nt, 6, local_width).transpose(1, 0, 2).reshape(6, width)
    bias_final = col_sums[:, mod_width:].reshape(-1)[width:].reshape(2, width)
    grad_cond = jax.vjp(jax.nn.silu, cond)[1](grad_cond_act)[0]
    rows_all = gather_fc(jnp.concatenate([grad_cond, split[2 * PATCH_ROWS :]], axis=0), chain)
    rows_all = rows_all.transpose(1, 0, 2).reshape(-1, width)
    cond_all, bias_patch = rows_all[:images_all], rows_all[images_all:]
    grad_b_cond = jnp.sum(cond_all, axis=0)
    cond_padded = jnp.concatenate([cond_all, jnp.zeros((images_all, 2 * width), F32)], axis=1)
    cond_top = lax.dynamic_slice_in_dim(cond_padded, top_cols * t, top_cols, 1)
    top_grad = exact_dot(cond_rows.T, all_final) + exact_dot(t_hidden.astype(F32).T, cond_top)
    grad_hidden = sum_over(exact_dot(cond_top, top_rows.T), ("tp",), chain)
    grad_t_pre = jax.vjp(jax.nn.silu, t_pre)[1](grad_hidden)[0]

    loss_total = shared[8, 0]
    patch_sum, head_sum = split[:PATCH_ROWS], split[PATCH_ROWS : 2 * PATCH_ROWS]
    head_grad_sum = head_sum.T

    def from_cores(total):
        low, high = total[:row_count], total[row_count:]
        return jnp.where(c == 0, low, high), swap(jnp.where(c == 0, high, low), "ctx", 1)

    block_sum, output_sum, shard_squares = call(
        functools.partial(shards_kernel, half),
        [
            shape(block_count * row_count, local_width, F32),
            shape(5 * local_width, row_count, F32),
            shape(1, local_width, F32),
        ],
        from_cores(first_sum) + from_cores(hidden_sum) + (grad_w_mod,),
        0,
    )
    embed_sum = exact_dot(one_hot.astype(F32).T, grad_cond) + exact_dot(
        freq_low.astype(F32).T, grad_t_pre
    )
    patch_padded = jnp.concatenate(
        [jnp.zeros((embed_rows, row_count), F32), patch_sum, jnp.zeros((embed_rows, row_count), F32)],
        axis=0,
    )
    patch_start = embed_rows * t + embed_rows - (FREQ + CLASSES)
    embed_sum = embed_sum + lax.dynamic_slice_in_dim(
        patch_padded, jnp.clip(patch_start, 0, embed_rows + PATCH_ROWS), embed_rows, 0
    )

    head_squares = jnp.where(t == 0, jnp.sum(head_grad_sum * head_grad_sum), 0.0)
    shard_squares = (
        jnp.sum(shard_squares)
        + jnp.sum(embed_sum * embed_sum)
        + jnp.sum(top_grad * top_grad)
        + head_squares
    )
    b1_part = jnp.where(t == 0, jnp.sum(grad_t_pre, axis=0), 0.0)
    b1_row = lax.dynamic_update_slice_in_dim(jnp.zeros((width,), F32), b1_part, place * row_count, 0)
    last = jnp.concatenate([b1_row, jnp.broadcast_to(shard_squares, (128,))])
    last = sum_over(last, ("ctx", "tp", "fsdp"))
    bias_sum = jnp.concatenate(
        [bias_patch, last[None, :width], grad_b_cond[None], bias_mod, shared[:8], bias_final], axis=0
    )
    grad_norm = jnp.sqrt(last[width] + jnp.sum(bias_sum * bias_sum))
    clip_factor = jnp.minimum(1.0, 1.0 / (grad_norm + 1e-06))
    def tall(values):
        return jnp.transpose(values, (1, 0, 2)).reshape(block_count * row_count, local_width)

    upd_block = [
        jnp.transpose(u.reshape(block_count, row_count, local_width), (1, 0, 2))
        for u in adam_blocks(tall(w_block), block_sum, tall(m_block), tall(v_block), clip_factor)
    ]
    upd_output = [
        u.reshape(w_output.shape)
        for u in adam_blocks(
            *[m.reshape(output_sum.shape) if m.ndim == 3 else m for m in (w_output, output_sum, m_output, v_output)],
            clip_factor,
        )
    ]
    upd_top = adam_update(w_top, top_grad, m_top, v_top, clip_factor)
    upd_head = adam_update(w_head, head_grad_sum, m_head, v_head, clip_factor)
    upd_embed = adam_update(w_embed, embed_sum, m_embed, v_embed, clip_factor)
    upd_biases = adam_update(biases, bias_sum, m_biases, v_biases, clip_factor)
    updates = (upd_block, upd_output, upd_top, upd_head, upd_embed, upd_biases)
    return (
        (loss_total, grad_norm)
        + tuple(u[0] for u in updates)
        + tuple(u[1] for u in updates)
        + tuple(u[2] for u in updates)
        + (bias_sum * clip_factor,)
    )


def solution(mesh):
    both = ("fsdp", "ctx")
    weights = (
        P(both, None, "tp"),
        P(None, "tp", both),
        P(both, "tp"),
        P(both, None),
        P("tp", both),
        P(),
    )
    images = (P(both, None, None, None), P(both, None, None, None), P(both), P(both))
    return jax.shard_map(
        on_device,
        mesh=mesh,
        in_specs=images + weights * 3,
        out_specs=(P(), P()) + weights * 3 + (P(),),
        check_vma=False,
    )
```
